512 devices in a mesh: tx: 32 (over z_lo, y, core), ty: 16 (over z_hi, x).
Axes of the slice: x: 4, y: 8, z: 8 (z_hi: 4, z_lo: 2; z = z_hi * 2 + z_lo), core: 2. Of those that a mesh axis runs over, the one named last changes fastest.
Arguments:
- species: float32 [32, 1024, 4096], P(None, 'tx', 'ty'), may hold values from -6 to 6
- cell_factor: float32 [1024, 4096], P('tx', 'ty'), may hold values from 0.5 to 2
- species_rate: float32 [32], replicated, may hold values from 0.01 to 0.08
- factor_x: float32 [1024, 128], P('tx'), may hold values from -0.375 to 0.375
- factor_y: float32 [128, 128], P('ty'), may hold values from -0.75 to 0.75
- factor_species: float32 [32, 16], replicated, may hold values from -1 to 1
Outputs:
- advanced: float32 [32, 1024, 4096], P(None, 'tx', 'ty')
- core_tensor: float32 [128, 16, 4096], P('tx', None, 'ty')
The draws below stay inside these ranges and needn't reach their ends.
All inputs are finite; a program needn't handle non-finite values.
Results may differ from the reference program's by a relative error of at most 0.000075.
Values sent between devices are 32-bit elements; how exact they have to be, the bound alone decides.
No kernel may reach another device: no remote copies, remote signals or barrier semaphores. Data moves between devices by JAX's collectives and lax.ppermute only.
A program may use at most 64 MiB of HBM per device.

```python
import math
import jax
import jax.numpy as jnp
from jax import lax

S = 32
RS = 16
R1 = 128
R2 = 128
NZ = 32
NX = 1024
NY = 128


def with_spikes(values, stream_key, source, target, shards_of, factor):
    owner, partner = [(jnp.arange(values.shape[position]) // (values.shape[position] // shards_of)).reshape([-1 if axis == position else 1 for axis in range(values.ndim)]) for position in (source, target)]
    chosen = jax.random.permutation(stream_key, shards_of)[partner]
    strong = (owner == chosen) | (owner == (partner + shards_of // 2) % shards_of)
    return jnp.where(strong, factor * values, values)


def levels(stream_key, shape, cuts, least, top_value):
    factor_of = 1.0
    for position, shards_of in cuts:
        heights = jax.random.uniform(jax.random.fold_in(jax.random.fold_in(stream_key, 6), position), (shards_of,), jnp.float32, least / len(cuts), top_value / len(cuts))
        factor_of = factor_of * jnp.repeat(jnp.exp(heights), shape[position] // shards_of).reshape((-1,) + (1,) * (len(shape) - 1 - position))
    return factor_of


def gaussian(key, dims, deviation, most, pieces=(), kind=jnp.bfloat16):
    gain = levels(key, dims, pieces, -0.22, 0.18) if pieces else 1.0
    result = jax.random.normal(key, dims, jnp.float32) * deviation * gain
    return jnp.minimum(jnp.maximum(result, -most), most).astype(kind)


def bell_draw_with(rng, dims, spread, most, cuts, heavy, held_as=jnp.bfloat16):
    array = spread * jax.random.normal(rng, dims, jnp.float32)
    if cuts:
        array = array * levels(rng, dims, cuts, -0.22, 0.18)
    return jnp.clip(with_spikes(array, jax.random.fold_in(rng, 3), *heavy), -most, most).astype(held_as)


def setup_inputs(seed: int = 0) -> dict:
    key_of = jax.random.split(jax.random.key(seed), 7)
    return {
        "species": gaussian(key_of[0], (S, NX, NY * NZ), 1.0, 6.0, ((1, 32), (2, 16)), jnp.float32),
        "cell_factor": jnp.clip(jnp.exp(math.log(2.0) - 1.3862944 * jax.random.uniform(key_of[1], (NX, NY * NZ), jnp.float32) ** levels(key_of[1], (NX, NY * NZ), ((0, 32), (1, 16)), -0.2, 0.2)), 0.5, 2.0),
        "species_rate": jnp.clip(jnp.exp(jax.random.uniform(key_of[2], (S,), jnp.float32, math.log(0.01), math.log(0.08))), 0.01, 0.08),
        "factor_x": bell_draw_with(key_of[3], (NX, R1), NX ** -0.5, 0.375, ((0, 32),), (0, 1, 32, 2.75), jnp.float32),
        "factor_y": bell_draw_with(key_of[4], (NY, R2), NY ** -0.5, 0.75, ((0, 16),), (0, 1, 16, 2.0), jnp.float32),
        "factor_species": gaussian(key_of[5], (S, RS), S ** -0.5, 1.0, (), jnp.float32),
    }


exact_mode = lax.Precision.HIGHEST


def laplace(field):
    padded = jnp.pad(field, 1)
    center = padded[1:-1, 1:-1, 1:-1]
    total = padded[2:, 1:-1, 1:-1] + padded[:-2, 1:-1, 1:-1]
    total = total + padded[1:-1, 2:, 1:-1] + padded[1:-1, :-2, 1:-1]
    total = total + padded[1:-1, 1:-1, 2:] + padded[1:-1, 1:-1, :-2]
    return total - 6.0 * center


def reference(species, cell_factor, species_rate, factor_x, factor_y, factor_species):
    grid = species.reshape(S, NX, NY, NZ)
    factor_grid = cell_factor.reshape(NX, NY, NZ)

    def advance_one(pair):
        field, rate_value = pair
        for iteration in range(2):
            field = field + (rate_value * factor_grid) * laplace(field)
        return field

    advanced_grid = lax.map(advance_one, (grid, species_rate))
    advanced = advanced_grid.reshape(S, NX, NY * NZ)
    reduced = jnp.einsum("sq,sxv->qxv", factor_species, advanced, precision=exact_mode)
    first = jnp.einsum("xa,qxv->aqv", factor_x, reduced, precision=exact_mode)
    first = first.reshape(R1, RS, NY, NZ)
    core = jnp.einsum("yb,aqyz->aqbz", factor_y, first, precision=exact_mode)
    return advanced, core.reshape(R1, RS, R2 * NZ)
```

```python
import jax
import jax.numpy as jnp
from jax import lax
from jax.sharding import PartitionSpec as P

exact_mode = lax.Precision.HIGHEST


def padded_2(x, sides, width):
    for axis, dim in sides:
        count, length = (lax.axis_size(axis), x.shape[dim])
        up = [(i, (i + 1) % count) for i in range(count - 1)]
        down = [(j, i) for i, j in up]
        last = lax.slice_in_dim(x, length - width, length, axis=dim)
        first = lax.slice_in_dim(x, 0, width, axis=dim)
        before = lax.ppermute(last, axis, up)
        after = lax.ppermute(first, axis, down)
        x = jnp.concatenate([before, x, after], axis=dim)
    return x


def laplace(padded):
    center = padded[:, 1:-1, 1:-1, :]
    z_padded = jnp.pad(center, ((0, 0), (0, 0), (0, 0), (1, 1)))
    total = padded[:, 2:, 1:-1, :] + padded[:, :-2, 1:-1, :]
    total = total + padded[:, 1:-1, 2:, :] + padded[:, 1:-1, :-2, :]
    total = total + z_padded[..., 2:] + z_padded[..., :-2]
    return total - 6.0 * center


def whole_of(block, axis):
    count = lax.axis_size(axis)
    copies = jnp.broadcast_to(block[None], (count,) + block.shape)
    return lax.all_to_all(copies, axis, 0, 0, tiled=True).reshape((-1,) + block.shape[1:])


def body(species, cell_factor, species_rate, factor_x, factor_y, factor_species):
    nspec, cells_x, merged = species.shape
    cells_y = factor_y.shape[0]
    depth = merged // cells_y
    n_tx, n_ty = lax.axis_size("tx"), lax.axis_size("ty")
    whole_x = whole_of(factor_x, "tx")
    whole_y = whole_of(factor_y, "ty")
    field = species.reshape(nspec, cells_x, cells_y, depth)
    factor_grid = cell_factor.reshape(cells_x, cells_y, depth)
    rate_field = species_rate[:, None, None, None] * factor_grid[None]
    for iteration in range(2):
        padded = padded_2(field, (("tx", 1), ("ty", 2)), 1)
        field = field + rate_field * laplace(padded)
    advanced = field.reshape(nspec, cells_x, merged)
    reduced = jnp.einsum("sq,sxv->qxv", factor_species, advanced, precision=exact_mode)
    ranks_q = reduced.shape[0]
    planes = reduced.reshape(ranks_q, cells_x, cells_y, depth).transpose(3, 1, 0, 2)
    planes = planes.reshape(depth, cells_x, ranks_q * cells_y)
    planes = lax.all_to_all(planes, "tx", 0, 0, tiled=True).reshape(-1, ranks_q * cells_y)
    first = lax.dot_general(planes, whole_x, (((0,), (0,)), ((), ())), precision=exact_mode)
    first = first.reshape(ranks_q, cells_y, -1)
    first = lax.all_to_all(first, "ty", 0, 0, tiled=True).reshape(n_ty * cells_y, -1)
    plane = lax.dot_general(first, whole_y, (((0,), (0,)), ((), ())), precision=exact_mode)
    rank_a, rank_b = plane.shape
    plane = plane.reshape(n_tx, rank_a // n_tx, n_ty, rank_b // n_ty).transpose(0, 2, 1, 3)
    plane = plane.reshape(n_tx * n_ty, 1, -1)
    core = lax.all_to_all(plane, ("tx", "ty"), 0, 0, tiled=True)
    core = core.reshape(depth, ranks_q, rank_a // n_tx, rank_b // n_ty).transpose(2, 1, 3, 0)
    return advanced, core.reshape(rank_a // n_tx, ranks_q, -1)


def solution(mesh):
    in_specs = (P(None, "tx", "ty"), P("tx", "ty"), P(), P("tx", None), P("ty", None), P())
    out_specs = (P(None, "tx", "ty"), P("tx", None, "ty"))
    return jax.shard_map(body, mesh=mesh, in_specs=in_specs, out_specs=out_specs, check_vma=False)
```

```python
import jax
import jax.numpy as jnp
from jax import lax
from jax.experimental import pallas as pl
from jax.experimental.pallas import tpu as pltpu
from jax.sharding import PartitionSpec as P

exact_mode = lax.Precision.HIGHEST
f32, bf16 = jnp.float32, jnp.bfloat16
NS, NX, NV, NH, NZ, NQ = 32, 32, 256, 128, 32, 16


def lanes(rows):
    return lax.broadcasted_iota(jnp.int32, (rows, 128), 1)


def pack_kernel(c0_ref, c1_ref, k_ref, xl_ref, xh_ref, yl_ref, yh_ref, mm_ref, mp_ref, pm_ref, pp_ref):
    low = lanes(NS // 2) < 64

    def row(x):
        return [r[pl.ds(x, NS, stride=NX), :] for r in (c0_ref, c1_ref)]

    for ref, at, x in ((xl_ref, 0, 0), (xl_ref, NS, 1), (xh_ref, 0, NX - 1), (xh_ref, NS, NX - 2)):
        ref[at : at + NS, :128], ref[at : at + NS, 128:] = row(x)
    xl_ref[2 * NS :, :] = jnp.broadcast_to(k_ref[0:1, :], (8, NV))
    xh_ref[2 * NS :, :] = jnp.broadcast_to(k_ref[NX - 1 : NX, :], (8, NV))
    mm_ref[...], mp_ref[...] = row(0)
    pm_ref[...], pp_ref[...] = row(NX - 1)
    half = NS // 2
    for x in range(NX):
        t0, t1 = row(x)
        yl_ref[x * half : (x + 1) * half, :] = jnp.where(low, t0[:half], pltpu.roll(t0[half:], 64, 1))
        yh_ref[x * half : (x + 1) * half, :] = jnp.where(low, pltpu.roll(t1[half:], 64, 1), t1[:half])
    yl_ref[NX * half :, :] = k_ref[:, :128]
    yh_ref[NX * half :, :] = k_ref[:, 128:]


def whole_block(shape):
    return pl.BlockSpec(shape, lambda i: (0, 0))


def halves(v):
    return [pl.BlockSpec((v.shape[0], 128), lambda i, side=side: (0, side)) for side in range(2)]


def pack(c2d, k):
    shapes = [(2 * NS + 8, NV)] * 2 + [(NX * NS // 2 + NX, 128)] * 2 + [(NS, 128)] * 4
    return pl.pallas_call(
        pack_kernel,
        grid=(1,),
        out_shape=[jax.ShapeDtypeStruct(s, f32) for s in shapes],
        in_specs=halves(c2d) + [whole_block(k.shape)],
        out_specs=[whole_block(s) for s in shapes],
        name="pack_faces",
    )(c2d, c2d, k)


def split_2(v):
    hi = v.astype(bf16)
    return hi, (v - hi.astype(f32)).astype(bf16)


def advance_kernel(c0_ref, c1_ref, k_ref, rate_ref, fs_ref, xl_ref, xh_ref, yl_ref, yh_ref, mm_ref, mp_ref, pm_ref, pp_ref, whole_ref,
                   adv_ref, planes_ref, e0, e1, ke, left, right):
    half = NS // 2
    lane_s, lane_h, lane_q = lanes(NS), lanes(half), lanes(NQ)
    z = lane_s % NZ
    not_first, not_last = z > 0, z < NZ - 1
    below, above = lane_s >= 32, lane_s < 96

    low_s, low_h = lane_s < 64, lane_h < 64
    e0[0, :, :NV] = xh_ref[NS : 2 * NS, :]
    e0[1, :, :NV] = xh_ref[0:NS, :]
    e0[1, :, NV:] = jnp.where(low_s, pm_ref[...], pp_ref[...])
    e0[NX + 2, :, :NV] = xl_ref[0:NS, :]
    e0[NX + 2, :, NV:] = jnp.where(low_s, mm_ref[...], mp_ref[...])
    e0[NX + 3, :, :NV] = xl_ref[NS : 2 * NS, :]
    e0[0, :, NV:] = jnp.zeros((NS, NH), f32)
    e0[NX + 3, :, NV:] = jnp.zeros((NS, NH), f32)
    for x in range(NX):
        after, before = yl_ref[x * half : (x + 1) * half, :], yh_ref[x * half : (x + 1) * half, :]
        e0[x + 2, :, :128] = c0_ref[pl.ds(x, NS, stride=NX), :]
        e0[x + 2, :, 128:NV] = c1_ref[pl.ds(x, NS, stride=NX), :]
        e0[x + 2, :half, NV:] = jnp.where(low_h, after, before)
        e0[x + 2, half:, NV:] = pltpu.roll(jnp.where(low_h, before, after), 64, 1)
    ke[8 : 8 + NX, :NV] = k_ref[...]
    ke[8 : 8 + NX, NV:] = jnp.where(lanes(NX) < 64, yl_ref[NX * half :, :], yh_ref[NX * half :, :])
    ke[0:8, :NV] = xh_ref[2 * NS :, :]
    ke[0:8, NV:] = jnp.zeros((8, NH), f32)
    ke[8 + NX :, :NV] = xl_ref[2 * NS :, :]
    ke[8 + NX :, NV:] = jnp.zeros((8, NH), f32)
    rate = jnp.broadcast_to(rate_ref[...], (NS, 128))

    def step(src, row, k_row, tiles):
        t = [src[row, :, i * 128 : (i + 1) * 128] for i in range(3)]
        up = [pltpu.roll(v, 96, 1) for v in t]
        down = [pltpu.roll(v, 32, 1) for v in t]
        out = []
        for i in range(tiles):
            cut = slice(i * 128, (i + 1) * 128)
            total = src[row - 1, :, cut] + src[row + 1, :, cut]
            total = total + jnp.where(above, up[i], up[(i + 1) % 3]) + jnp.where(below, down[i], down[(i + 2) % 3])
            total = total + jnp.where(not_first, pltpu.roll(t[i], 1, 1), 0.0)
            total = total + jnp.where(not_last, pltpu.roll(t[i], 127, 1), 0.0)
            lap = total - 6.0 * t[i]
            out.append(t[i] + (rate * k_row[:, cut]) * lap)
        return out

    def first_step(x, carry):
        for i, v in enumerate(step(e0, x + 1, ke[pl.ds(x + 7, 1), :], 3)):
            e1[x, :, i * 128 : (i + 1) * 128] = v
        return carry

    lax.fori_loop(0, NX + 2, first_step, 0)

    fs_hi, fs_lo = split_2(fs_ref[...])
    weights = jnp.concatenate([fs_hi, fs_hi, fs_lo, fs_lo], axis=1)

    low_q, even_q = lane_q < 64, (lane_q & 32) == 0

    def second_step(group, carry):
        rows = []
        for g in range(4):
            x = group * 4 + g
            done = step(e1, x + 1, ke[pl.ds(x + 8, 1), :], 2)
            left[pl.ds(x, NS, stride=NX), :], right[pl.ds(x, NS, stride=NX), :] = done
            v = jnp.concatenate(done, axis=1)
            hi, lo = split_2(v)
            stacked = jnp.concatenate([hi, lo, hi, lo], axis=0)
            rows.append(jnp.dot(weights, stacked, preferred_element_type=f32))
        swapped = []
        for t in range(2):
            v = [r[:, t * 128 : (t + 1) * 128] for r in rows]
            a = [jnp.where(low_q, v[g], pltpu.roll(v[g + 2], 64, 1)) for g in range(2)]
            b = [jnp.where(low_q, pltpu.roll(v[g], 64, 1), v[g + 2]) for g in range(2)]
            for p, r in (a, b):
                swapped.append(jnp.where(even_q, p, pltpu.roll(r, 32, 1)))
                swapped.append(jnp.where(even_q, pltpu.roll(p, 96, 1), r))
        turned = jnp.concatenate(swapped, axis=0).T
        for g in range(4):
            planes_ref[pl.ds(group * 4 + g, NZ, stride=NX), :] = turned[g * NZ : (g + 1) * NZ, :]
        return carry

    lax.fori_loop(0, NX // 4, second_step, 0)
    adv_ref[:, :128] = left[...]
    adv_ref[:, 128:] = right[...]


def advance(c2d, k, rate, fs, faces, whole):
    small = (k, rate, fs, *faces)
    shapes = [(NS * NX, NV), (NZ * NX, 128)]
    return pl.pallas_call(
        advance_kernel,
        grid=(1,),
        out_shape=[jax.ShapeDtypeStruct(s, f32) for s in shapes],
        in_specs=halves(c2d) + [whole_block(v.shape) for v in small] + [pl.BlockSpec(memory_space=pl.ANY)],
        out_specs=[whole_block(s) for s in shapes],
        scratch_shapes=[
            pltpu.VMEM((NX + 4, NS, NV + NH), f32),
            pltpu.VMEM((NX + 2, NS, NV + NH), f32),
            pltpu.VMEM((NX + 16, NV + NH), f32),
            pltpu.VMEM((NS * NX, 128), f32),
            pltpu.VMEM((NS * NX, 128), f32),
        ],
        compiler_params=pltpu.CompilerParams(vmem_limit_bytes=40 * 1024 * 1024),
        name="advance_twice",
    )(c2d, c2d, *small, whole)


def whole_of(block, axis):
    count = lax.axis_size(axis)
    copies = jnp.broadcast_to(block[None], (count,) + block.shape)
    return lax.all_to_all(copies, axis, 0, 0, tiled=True).reshape((-1,) + block.shape[1:])


def shift_to(v, dx, dy):
    n_tx, n_ty = lax.axis_size("tx"), lax.axis_size("ty")
    if dy == 0:
        return lax.ppermute(v, "tx", [(i, i + dx) for i in range(n_tx) if 0 <= i + dx < n_tx])
    if dx == 0:
        return lax.ppermute(v, "ty", [(j, j + dy) for j in range(n_ty) if 0 <= j + dy < n_ty])
    pairs = [
        (i * n_ty + j, (i + dx) * n_ty + j + dy)
        for i in range(n_tx)
        for j in range(n_ty)
        if 0 <= i + dx < n_tx and 0 <= j + dy < n_ty
    ]
    return lax.ppermute(v, ("tx", "ty"), pairs)


def body(species, cell_factor, species_rate, factor_x, factor_y, factor_species):
    nspec, cells_x, merged = species.shape
    cells_y = factor_y.shape[0]
    depth = merged // cells_y
    n_tx, n_ty = lax.axis_size("tx"), lax.axis_size("ty")
    ranks_q = factor_species.shape[1]
    whole_x = whole_of(factor_x, "tx")
    c2d = species.reshape(nspec * cells_x, merged)
    faces = pack(c2d, cell_factor)
    ways = [(-1, 0), (1, 0), (0, -1), (0, 1), (-1, -1), (-1, 1), (1, -1), (1, 1)]
    faces = [shift_to(v, dx, dy) for v, (dx, dy) in zip(faces, ways)]
    advanced, planes = advance(c2d, cell_factor, species_rate[:, None], factor_species.T, faces, whole_x)
    planes = planes.reshape(depth, cells_x, cells_y * ranks_q)
    planes = lax.all_to_all(planes, "tx", 0, 0, tiled=True).reshape(-1, cells_y * ranks_q)
    first = lax.dot_general(planes, whole_x, (((0,), (0,)), ((), ())), precision=exact_mode)
    first = first.reshape(cells_y, ranks_q, -1).transpose(1, 0, 2)
    sent = jnp.concatenate([first, jnp.broadcast_to(factor_y[None], (n_ty,) + factor_y.shape)], axis=1)
    came = lax.all_to_all(sent, "ty", 0, 0, tiled=True)
    first = came[:, :cells_y].reshape(n_ty * cells_y, -1)
    whole_y = came[:, cells_y:].reshape(n_ty * cells_y, -1)
    plane = lax.dot_general(first, whole_y, (((0,), (0,)), ((), ())), precision=exact_mode)
    rank_a, rank_b = plane.shape
    plane = plane.reshape(n_tx, rank_a // n_tx, n_ty, rank_b // n_ty).transpose(0, 2, 1, 3)
    plane = plane.reshape(n_tx * n_ty, 1, -1)
    core = lax.all_to_all(plane, ("tx", "ty"), 0, 0, tiled=True)
    core = core.reshape(depth, ranks_q, rank_a // n_tx, rank_b // n_ty).transpose(2, 1, 3, 0)
    return advanced.reshape(species.shape), core.reshape(rank_a // n_tx, ranks_q, -1)


def solution(mesh):
    in_specs = (P(None, "tx", "ty"), P("tx", "ty"), P(), P("tx", None), P("ty", None), P())
    out_specs = (P(None, "tx", "ty"), P("tx", None, "ty"))
    return jax.shard_map(body, mesh=mesh, in_specs=in_specs, out_specs=out_specs, check_vma=False)
```

```python
import jax
import jax.numpy as jnp
from jax import lax
from jax.experimental import pallas as pl
from jax.experimental.pallas import tpu as pltpu
from jax.sharding import PartitionSpec as P

exact_mode = lax.Precision.HIGHEST
f32, bf16 = jnp.float32, jnp.bfloat16
NS, NX, NV, NH, NZ, NQ = 32, 32, 256, 128, 32, 16


def lanes(rows):
    return lax.broadcasted_iota(jnp.int32, (rows, 128), 1)


def pack_kernel(c0_ref, c1_ref, k_ref, fx_ref, xl_ref, xh_ref, yl_ref, yh_ref, copies_ref):
    low = lanes(NS // 2) < 64

    def row(x):
        return [r[pl.ds(x, NS, stride=NX), :] for r in (c0_ref, c1_ref)]

    for ref, at, x in ((xl_ref, 0, 0), (xl_ref, NS, 1), (xh_ref, 0, NX - 1), (xh_ref, NS, NX - 2)):
        ref[at : at + NS, :128], ref[at : at + NS, 128:] = row(x)
    xl_ref[2 * NS :, :] = jnp.broadcast_to(k_ref[0:1, :], (8, NV))
    xh_ref[2 * NS :, :] = jnp.broadcast_to(k_ref[NX - 1 : NX, :], (8, NV))
    half = NS // 2
    for x in range(NX):
        t0, t1 = row(x)
        yl_ref[x * half : (x + 1) * half, :] = jnp.where(low, t0[:half], pltpu.roll(t0[half:], 64, 1))
        yh_ref[x * half : (x + 1) * half, :] = jnp.where(low, pltpu.roll(t1[half:], 64, 1), t1[:half])
    yl_ref[NX * half :, :] = k_ref[:, :128]
    yh_ref[NX * half :, :] = k_ref[:, 128:]
    copies_ref[...] = jnp.broadcast_to(fx_ref[...][None], copies_ref.shape)


def whole_block(shape):
    return pl.BlockSpec(shape, lambda i: (0,) * len(shape))


def halves(v):
    return [pl.BlockSpec((v.shape[0], 128), lambda i, side=side: (0, side)) for side in range(2)]


def pack(c2d, k, factor_x, copies):
    shapes = [(2 * NS + 8, NV)] * 2 + [(NX * NS // 2 + NX, 128)] * 2 + [(copies,) + factor_x.shape]
    return pl.pallas_call(
        pack_kernel,
        grid=(1,),
        out_shape=[jax.ShapeDtypeStruct(s, f32) for s in shapes],
        in_specs=halves(c2d) + [whole_block(k.shape), whole_block(factor_x.shape)],
        out_specs=[whole_block(s) for s in shapes],
        name="pack_faces",
    )(c2d, c2d, k, factor_x)


def corner_kernel(xl_ref, xh_ref, lo_ref, hi_ref):
    for at, ref in ((0, xh_ref), (NS, xl_ref)):
        lo_ref[at : at + NS, :] = ref[0:NS, :128]
        hi_ref[at : at + NS, :] = ref[0:NS, 128:]


def corners(xl, xh):
    shape = (2 * NS, 128)
    return pl.pallas_call(
        corner_kernel,
        grid=(1,),
        out_shape=[jax.ShapeDtypeStruct(shape, f32)] * 2,
        in_specs=[whole_block(xl.shape)] * 2,
        out_specs=[whole_block(shape)] * 2,
        name="corner_columns",
    )(xl, xh)


def split_2(v):
    hi = v.astype(bf16)
    return hi, (v - hi.astype(f32)).astype(bf16)


def advance_kernel(c0_ref, c1_ref, k_ref, rate_ref, fs_ref, xl_ref, xh_ref, yl_ref, yh_ref, cl_ref, ch_ref, whole_ref,
                   adv_ref, planes_ref, e0, e1, ke, left, right):
    half = NS // 2
    lane_s, lane_h, lane_q = lanes(NS), lanes(half), lanes(NQ)
    z = lane_s % NZ
    not_first, not_last = z > 0, z < NZ - 1
    below, above = lane_s >= 32, lane_s < 96

    low_s, low_h = lane_s < 64, lane_h < 64
    e0[0, :, :NV] = xh_ref[NS : 2 * NS, :]
    e0[1, :, :NV] = xh_ref[0:NS, :]
    e0[1, :, NV:] = jnp.where(low_s, cl_ref[:NS, :], ch_ref[:NS, :])
    e0[NX + 2, :, :NV] = xl_ref[0:NS, :]
    e0[NX + 2, :, NV:] = jnp.where(low_s, cl_ref[NS:, :], ch_ref[NS:, :])
    e0[NX + 3, :, :NV] = xl_ref[NS : 2 * NS, :]
    e0[0, :, NV:] = jnp.zeros((NS, NH), f32)
    e0[NX + 3, :, NV:] = jnp.zeros((NS, NH), f32)
    for x in range(NX):
        after, before = yl_ref[x * half : (x + 1) * half, :], yh_ref[x * half : (x + 1) * half, :]
        e0[x + 2, :, :128] = c0_ref[pl.ds(x, NS, stride=NX), :]
        e0[x + 2, :, 128:NV] = c1_ref[pl.ds(x, NS, stride=NX), :]
        e0[x + 2, :half, NV:] = jnp.where(low_h, after, before)
        e0[x + 2, half:, NV:] = pltpu.roll(jnp.where(low_h, before, after), 64, 1)
    ke[8 : 8 + NX, :NV] = k_ref[...]
    ke[8 : 8 + NX, NV:] = jnp.where(lanes(NX) < 64, yl_ref[NX * half :, :], yh_ref[NX * half :, :])
    ke[0:8, :NV] = xh_ref[2 * NS :, :]
    ke[0:8, NV:] = jnp.zeros((8, NH), f32)
    ke[8 + NX :, :NV] = xl_ref[2 * NS :, :]
    ke[8 + NX :, NV:] = jnp.zeros((8, NH), f32)
    rate = jnp.broadcast_to(rate_ref[...], (NS, 128))

    def step(src, row, k_row, tiles):
        t = [src[row, :, i * 128 : (i + 1) * 128] for i in range(3)]
        up = [pltpu.roll(v, 96, 1) for v in t]
        down = [pltpu.roll(v, 32, 1) for v in t]
        out = []
        for i in range(tiles):
            cut = slice(i * 128, (i + 1) * 128)
            total = src[row - 1, :, cut] + src[row + 1, :, cut]
            total = total + jnp.where(above, up[i], up[(i + 1) % 3]) + jnp.where(below, down[i], down[(i + 2) % 3])
            total = total + jnp.where(not_first, pltpu.roll(t[i], 1, 1), 0.0)
            total = total + jnp.where(not_last, pltpu.roll(t[i], 127, 1), 0.0)
            lap = total - 6.0 * t[i]
            out.append(t[i] + (rate * k_row[:, cut]) * lap)
        return out

    def first_step(x, carry):
        for i, v in enumerate(step(e0, x + 1, ke[pl.ds(x + 7, 1), :], 3)):
            e1[x, :, i * 128 : (i + 1) * 128] = v
        return carry

    lax.fori_loop(0, NX + 2, first_step, 0)

    fs_hi, fs_lo = split_2(fs_ref[...])
    weights = jnp.concatenate([fs_hi, fs_hi, fs_lo, fs_lo], axis=1)

    low_q, even_q = lane_q < 64, (lane_q & 32) == 0

    def second_step(group, carry):
        rows = []
        for g in range(4):
            x = group * 4 + g
            done = step(e1, x + 1, ke[pl.ds(x + 8, 1), :], 2)
            left[pl.ds(x, NS, stride=NX), :], right[pl.ds(x, NS, stride=NX), :] = done
            v = jnp.concatenate(done, axis=1)
            hi, lo = split_2(v)
            stacked = jnp.concatenate([hi, lo, hi, lo], axis=0)
            rows.append(jnp.dot(weights, stacked, preferred_element_type=f32))
        swapped = []
        for t in range(2):
            v = [r[:, t * 128 : (t + 1) * 128] for r in rows]
            a = [jnp.where(low_q, v[g], pltpu.roll(v[g + 2], 64, 1)) for g in range(2)]
            b = [jnp.where(low_q, pltpu.roll(v[g], 64, 1), v[g + 2]) for g in range(2)]
            for p, r in (a, b):
                swapped.append(jnp.where(even_q, p, pltpu.roll(r, 32, 1)))
                swapped.append(jnp.where(even_q, pltpu.roll(p, 96, 1), r))
        turned = jnp.concatenate(swapped, axis=0).T
        for g in range(4):
            planes_ref[pl.ds(group * 4 + g, NZ, stride=NX), :] = turned[g * NZ : (g + 1) * NZ, :]
        return carry

    lax.fori_loop(0, NX // 4, second_step, 0)
    adv_ref[:, :128] = left[...]
    adv_ref[:, 128:] = right[...]


def advance(c2d, k, rate, fs, faces, whole):
    small = (k, rate, fs, *faces)
    shapes = [(NS * NX, NV), (NZ * NX, 128)]
    return pl.pallas_call(
        advance_kernel,
        grid=(1,),
        out_shape=[jax.ShapeDtypeStruct(s, f32) for s in shapes],
        in_specs=halves(c2d) + [whole_block(v.shape) for v in small] + [pl.BlockSpec(memory_space=pl.ANY)],
        out_specs=[whole_block(s) for s in shapes],
        scratch_shapes=[
            pltpu.VMEM((NX + 4, NS, NV + NH), f32),
            pltpu.VMEM((NX + 2, NS, NV + NH), f32),
            pltpu.VMEM((NX + 16, NV + NH), f32),
            pltpu.VMEM((NS * NX, 128), f32),
            pltpu.VMEM((NS * NX, 128), f32),
        ],
        compiler_params=pltpu.CompilerParams(vmem_limit_bytes=40 * 1024 * 1024),
        name="advance_twice",
    )(c2d, c2d, *small, whole)


def shift_to(v, dx, dy):
    axis, step = ("tx", dx) if dx else ("ty", dy)
    count = lax.axis_size(axis)
    return lax.ppermute(v, axis, [(i, i + step) for i in range(count) if 0 <= i + step < count])


def body(species, cell_factor, species_rate, factor_x, factor_y, factor_species):
    nspec, cells_x, merged = species.shape
    cells_y = factor_y.shape[0]
    depth = merged // cells_y
    n_tx, n_ty = lax.axis_size("tx"), lax.axis_size("ty")
    ranks_q = factor_species.shape[1]
    c2d = species.reshape(nspec * cells_x, merged)
    *faces, copies = pack(c2d, cell_factor, factor_x, n_tx)
    xl, xh, yl, yh = (shift_to(v, dx, dy) for v, (dx, dy) in zip(faces, [(-1, 0), (1, 0), (0, -1), (0, 1)]))
    lo, hi = corners(xl, xh)
    faces = xl, xh, yl, yh, shift_to(lo, 0, -1), shift_to(hi, 0, 1)
    whole_x = lax.all_to_all(copies, "tx", 0, 0, tiled=True).reshape(-1, factor_x.shape[1])
    advanced, planes = advance(c2d, cell_factor, species_rate[:, None], factor_species.T, faces, whole_x)
    planes = planes.reshape(depth, cells_x, cells_y * ranks_q)
    planes = lax.all_to_all(planes, "tx", 0, 0, tiled=True).reshape(-1, cells_y * ranks_q)
    first = lax.dot_general(planes, whole_x, (((0,), (0,)), ((), ())), precision=exact_mode)
    first = first.reshape(cells_y, ranks_q, -1).transpose(1, 0, 2)
    sent = jnp.concatenate([first, jnp.broadcast_to(factor_y[None], (n_ty,) + factor_y.shape)], axis=1)
    came = lax.all_to_all(sent, "ty", 0, 0, tiled=True)
    first = came[:, :cells_y].reshape(n_ty * cells_y, -1)
    whole_y = came[:, cells_y:].reshape(n_ty * cells_y, -1)
    plane = lax.dot_general(first, whole_y, (((0,), (0,)), ((), ())), precision=exact_mode)
    rank_a, rank_b = plane.shape
    plane = plane.reshape(n_tx, rank_a // n_tx, n_ty, rank_b // n_ty).transpose(0, 2, 1, 3)
    plane = plane.reshape(n_tx * n_ty, 1, -1)
    core = lax.all_to_all(plane, ("tx", "ty"), 0, 0, tiled=True)
    core = core.reshape(depth, ranks_q, rank_a // n_tx, rank_b // n_ty).transpose(2, 1, 3, 0)
    return advanced.reshape(species.shape), core.reshape(rank_a // n_tx, ranks_q, -1)


def solution(mesh):
    in_specs = (P(None, "tx", "ty"), P("tx", "ty"), P(), P("tx", None), P("ty", None), P())
    out_specs = (P(None, "tx", "ty"), P("tx", None, "ty"))
    return jax.shard_map(body, mesh=mesh, in_specs=in_specs, out_specs=out_specs, check_vma=False)
```

```python
import jax
import jax.numpy as jnp
from jax import lax
from jax.experimental import pallas as pl
from jax.experimental.pallas import tpu as pltpu
from jax.sharding import PartitionSpec as P

exact_mode = lax.Precision.HIGHEST
f32, bf16 = jnp.float32, jnp.bfloat16
U1, U2, U3 = 2, 8, 8
NS, NX, NV, NH, NZ, NQ = 32, 32, 256, 128, 32, 16


def lanes(rows):
    return lax.broadcasted_iota(jnp.int32, (rows, 128), 1)


def pack_kernel(c0_ref, c1_ref, k_ref, xl_ref, xh_ref, yl_ref, yh_ref):
    low = lanes(NS // 2) < 64

    def row(x):
        return [r[pl.ds(x, NS, stride=NX), :] for r in (c0_ref, c1_ref)]

    for ref, at, x in ((xl_ref, 0, 0), (xl_ref, NS, 1), (xh_ref, 0, NX - 1), (xh_ref, NS, NX - 2)):
        ref[at : at + NS, :128], ref[at : at + NS, 128:] = row(x)
    xl_ref[2 * NS :, :] = jnp.broadcast_to(k_ref[0:1, :], (8, NV))
    xh_ref[2 * NS :, :] = jnp.broadcast_to(k_ref[NX - 1 : NX, :], (8, NV))
    half = NS // 2
    for x in range(NX):
        t0, t1 = row(x)
        yl_ref[x * half : (x + 1) * half, :] = jnp.where(low, t0[:half], pltpu.roll(t0[half:], 64, 1))
        yh_ref[x * half : (x + 1) * half, :] = jnp.where(low, pltpu.roll(t1[half:], 64, 1), t1[:half])
    yl_ref[NX * half :, :] = k_ref[:, :128]
    yh_ref[NX * half :, :] = k_ref[:, 128:]


def whole_block(shape):
    return pl.BlockSpec(shape, lambda i: (0,) * len(shape))


def halves(v):
    return [pl.BlockSpec((v.shape[0], 128), lambda i, side=side: (0, side)) for side in range(2)]


def pack(c2d, k):
    shapes = [(2 * NS + 8, NV)] * 2 + [(NX * NS // 2 + NX, 128)] * 2
    return pl.pallas_call(
        pack_kernel,
        grid=(1,),
        out_shape=[jax.ShapeDtypeStruct(s, f32) for s in shapes],
        in_specs=halves(c2d) + [whole_block(k.shape)],
        out_specs=[whole_block(s) for s in shapes],
        name="pack_faces",
    )(c2d, c2d, k)


def corner_kernel(xl_ref, xh_ref, fx_ref, lo_ref, hi_ref, copies_ref):
    for at, ref in ((0, xh_ref), (NS, xl_ref)):
        lo_ref[at : at + NS, :] = ref[0:NS, :128]
        hi_ref[at : at + NS, :] = ref[0:NS, 128:]
    copies_ref[...] = jnp.broadcast_to(fx_ref[...][None], copies_ref.shape)


def corners(xl, xh, factor_x, copies):
    shapes = [(2 * NS, 128)] * 2 + [(copies,) + factor_x.shape]
    return pl.pallas_call(
        corner_kernel,
        grid=(1,),
        out_shape=[jax.ShapeDtypeStruct(s, f32) for s in shapes],
        in_specs=[whole_block(v.shape) for v in (xl, xh, factor_x)],
        out_specs=[whole_block(s) for s in shapes],
        name="corner_columns",
    )(xl, xh, factor_x)


def split_2(v):
    hi = v.astype(bf16)
    return hi, (v - hi.astype(f32)).astype(bf16)


def advance_kernel(c0_ref, c1_ref, k_ref, rate_ref, xl_ref, xh_ref, yl_ref, yh_ref, cl_ref, ch_ref, adv_ref, e0, e1, ke, left, right):
    half = NS // 2
    lane_s, lane_h = lanes(NS), lanes(half)
    z = lane_s % NZ
    not_first, not_last = z > 0, z < NZ - 1
    below, above = lane_s >= 32, lane_s < 96

    low_s, low_h = lane_s < 64, lane_h < 64
    e0[0, :, :NV] = xh_ref[NS : 2 * NS, :]
    e0[1, :, :NV] = xh_ref[0:NS, :]
    e0[1, :, NV:] = jnp.where(low_s, cl_ref[:NS, :], ch_ref[:NS, :])
    e0[NX + 2, :, :NV] = xl_ref[0:NS, :]
    e0[NX + 2, :, NV:] = jnp.where(low_s, cl_ref[NS:, :], ch_ref[NS:, :])
    e0[NX + 3, :, :NV] = xl_ref[NS : 2 * NS, :]
    e0[0, :, NV:] = jnp.zeros((NS, NH), f32)
    e0[NX + 3, :, NV:] = jnp.zeros((NS, NH), f32)
    for x in range(NX):
        after, before = yl_ref[x * half : (x + 1) * half, :], yh_ref[x * half : (x + 1) * half, :]
        e0[x + 2, :, :128] = c0_ref[pl.ds(x, NS, stride=NX), :]
        e0[x + 2, :, 128:NV] = c1_ref[pl.ds(x, NS, stride=NX), :]
        e0[x + 2, :half, NV:] = jnp.where(low_h, after, before)
        e0[x + 2, half:, NV:] = pltpu.roll(jnp.where(low_h, before, after), 64, 1)
    ke[8 : 8 + NX, :NV] = k_ref[...]
    ke[8 : 8 + NX, NV:] = jnp.where(lanes(NX) < 64, yl_ref[NX * half :, :], yh_ref[NX * half :, :])
    ke[0:8, :NV] = xh_ref[2 * NS :, :]
    ke[0:8, NV:] = jnp.zeros((8, NH), f32)
    ke[8 + NX :, :NV] = xl_ref[2 * NS :, :]
    ke[8 + NX :, NV:] = jnp.zeros((8, NH), f32)
    rate = jnp.broadcast_to(rate_ref[...], (NS, 128))

    def step(src, row, k_row, tiles):
        t = [src[row, :, i * 128 : (i + 1) * 128] for i in range(3)]
        up = [pltpu.roll(v, 96, 1) for v in t]
        down = [pltpu.roll(v, 32, 1) for v in t]
        out = []
        for i in range(tiles):
            cut = slice(i * 128, (i + 1) * 128)
            total = src[row - 1, :, cut] + src[row + 1, :, cut]
            total = total + jnp.where(above, up[i], up[(i + 1) % 3]) + jnp.where(below, down[i], down[(i + 2) % 3])
            total = total + jnp.where(not_first, pltpu.roll(t[i], 1, 1), 0.0)
            total = total + jnp.where(not_last, pltpu.roll(t[i], 127, 1), 0.0)
            lap = total - 6.0 * t[i]
            out.append(t[i] + (rate * k_row[:, cut]) * lap)
        return out

    def first_step(x, carry):
        for i, v in enumerate(step(e0, x + 1, ke[pl.ds(x + 7, 1), :], 3)):
            e1[x, :, i * 128 : (i + 1) * 128] = v
        return carry

    lax.fori_loop(0, NX + 2, first_step, 0, unroll=U1)

    def second_step(x, carry):
        done = step(e1, x + 1, ke[pl.ds(x + 8, 1), :], 2)
        left[pl.ds(x, NS, stride=NX), :], right[pl.ds(x, NS, stride=NX), :] = done
        return carry

    lax.fori_loop(0, NX, second_step, 0, unroll=U2)
    adv_ref[:, :128] = left[...]
    adv_ref[:, 128:] = right[...]


def advance(c2d, k, rate, faces):
    small = (k, rate, *faces)
    return pl.pallas_call(
        advance_kernel,
        grid=(1,),
        out_shape=jax.ShapeDtypeStruct((NS * NX, NV), f32),
        in_specs=halves(c2d) + [whole_block(v.shape) for v in small],
        out_specs=whole_block((NS * NX, NV)),
        scratch_shapes=[
            pltpu.VMEM((NX + 4, NS, NV + NH), f32),
            pltpu.VMEM((NX + 2, NS, NV + NH), f32),
            pltpu.VMEM((NX + 16, NV + NH), f32),
            pltpu.VMEM((NS * NX, 128), f32),
            pltpu.VMEM((NS * NX, 128), f32),
        ],
        compiler_params=pltpu.CompilerParams(vmem_limit_bytes=40 * 1024 * 1024),
        cost_estimate=pl.CostEstimate(flops=40000000000, bytes_accessed=4 * 2**20, transcendentals=0),
        name="advance_twice",
    )(c2d, c2d, *small)


def reduce_kernel(a0_ref, a1_ref, fs_ref, whole_ref, planes_ref):
    lane_q = lanes(NQ)
    low_q, even_q = lane_q < 64, (lane_q & 32) == 0
    fs_hi, fs_lo = split_2(fs_ref[...])
    weights = jnp.concatenate([fs_hi, fs_hi, fs_lo, fs_lo], axis=1)

    def four_rows(group, carry):
        rows = []
        for g in range(4):
            cut = pl.ds(group * 4 + g, NS, stride=NX)
            hi, lo = split_2(jnp.concatenate([a0_ref[cut, :], a1_ref[cut, :]], axis=1))
            stacked = jnp.concatenate([hi, lo, hi, lo], axis=0)
            rows.append(jnp.dot(weights, stacked, preferred_element_type=f32))
        swapped = []
        for t in range(2):
            v = [r[:, t * 128 : (t + 1) * 128] for r in rows]
            a = [jnp.where(low_q, v[g], pltpu.roll(v[g + 2], 64, 1)) for g in range(2)]
            b = [jnp.where(low_q, pltpu.roll(v[g], 64, 1), v[g + 2]) for g in range(2)]
            for p, r in (a, b):
                swapped.append(jnp.where(even_q, p, pltpu.roll(r, 32, 1)))
                swapped.append(jnp.where(even_q, pltpu.roll(p, 96, 1), r))
        turned = jnp.concatenate(swapped, axis=0).T
        for g in range(4):
            planes_ref[pl.ds(group * 4 + g, NZ, stride=NX), :] = turned[g * NZ : (g + 1) * NZ, :]
        return carry

    lax.fori_loop(0, NX // 4, four_rows, 0, unroll=U3)


def reduce_species(advanced, fs, whole):
    return pl.pallas_call(
        reduce_kernel,
        grid=(1,),
        out_shape=jax.ShapeDtypeStruct((NZ * NX, 128), f32),
        in_specs=halves(advanced) + [whole_block(fs.shape), pl.BlockSpec(memory_space=pl.ANY)],
        out_specs=whole_block((NZ * NX, 128)),
        name="reduce_species",
    )(advanced, advanced, fs, whole)


def shift_to(v, dx, dy):
    axis, step = ("tx", dx) if dx else ("ty", dy)
    count = lax.axis_size(axis)
    return lax.ppermute(v, axis, [(i, i + step) for i in range(count) if 0 <= i + step < count])


def body(species, cell_factor, species_rate, factor_x, factor_y, factor_species):
    nspec, cells_x, merged = species.shape
    cells_y = factor_y.shape[0]
    depth = merged // cells_y
    n_tx, n_ty = lax.axis_size("tx"), lax.axis_size("ty")
    ranks_q = factor_species.shape[1]
    c2d = species.reshape(nspec * cells_x, merged)
    faces = pack(c2d, cell_factor)
    xl, xh, yl, yh = (shift_to(v, dx, dy) for v, (dx, dy) in zip(faces, [(-1, 0), (1, 0), (0, -1), (0, 1)]))
    lo, hi, copies = corners(xl, xh, factor_x, n_tx)
    faces = xl, xh, yl, yh, shift_to(lo, 0, -1), shift_to(hi, 0, 1)
    whole_x = lax.all_to_all(copies, "tx", 0, 0, tiled=True).reshape(-1, factor_x.shape[1])
    advanced = advance(c2d, cell_factor, species_rate[:, None], faces)
    planes = reduce_species(advanced, factor_species.T, whole_x)
    planes = planes.reshape(depth, cells_x, cells_y * ranks_q)
    planes = lax.all_to_all(planes, "tx", 0, 0, tiled=True).reshape(-1, cells_y * ranks_q)
    first = lax.dot_general(planes, whole_x, (((0,), (0,)), ((), ())), precision=exact_mode)
    first = first.reshape(cells_y, ranks_q, -1).transpose(1, 0, 2)
    sent = jnp.concatenate([first, jnp.broadcast_to(factor_y[None], (n_ty,) + factor_y.shape)], axis=1)
    came = lax.all_to_all(sent, "ty", 0, 0, tiled=True)
    first = came[:, :cells_y].reshape(n_ty * cells_y, -1)
    whole_y = came[:, cells_y:].reshape(n_ty * cells_y, -1)
    plane = lax.dot_general(first, whole_y, (((0,), (0,)), ((), ())), precision=exact_mode)
    rank_a, rank_b = plane.shape
    plane = plane.reshape(n_tx, rank_a // n_tx, n_ty, rank_b // n_ty).transpose(0, 2, 1, 3)
    plane = plane.reshape(n_tx * n_ty, 1, -1)
    core = lax.all_to_all(plane, ("tx", "ty"), 0, 0, tiled=True)
    core = core.reshape(depth, ranks_q, rank_a // n_tx, rank_b // n_ty).transpose(2, 1, 3, 0)
    return advanced.reshape(species.shape), core.reshape(rank_a // n_tx, ranks_q, -1)


def solution(mesh):
    in_specs = (P(None, "tx", "ty"), P("tx", "ty"), P(), P("tx", None), P("ty", None), P())
    out_specs = (P(None, "tx", "ty"), P("tx", None, "ty"))
    return jax.shard_map(body, mesh=mesh, in_specs=in_specs, out_specs=out_specs, check_vma=False)
```

```python
import jax
import jax.numpy as jnp
from jax import lax
from jax.experimental import pallas as pl
from jax.experimental.pallas import tpu as pltpu
from jax.sharding import PartitionSpec as P

exact_mode = lax.Precision.HIGHEST
f32, bf16 = jnp.float32, jnp.bfloat16
U1, U2, U3 = 2, 8, 8
NS, NX, NV, NH, NZ, NQ = 32, 32, 256, 128, 32, 16


def lanes(rows):
    return lax.broadcasted_iota(jnp.int32, (rows, 128), 1)


def pack_kernel(c0_ref, c1_ref, k_ref, xl_ref, xh_ref, yl_ref, yh_ref):
    low = lanes(NS // 2) < 64

    def row(x):
        return [r[pl.ds(x, NS, stride=NX), :] for r in (c0_ref, c1_ref)]

    for ref, at, x in ((xl_ref, 0, 0), (xl_ref, NS, 1), (xh_ref, 0, NX - 1), (xh_ref, NS, NX - 2)):
        ref[at : at + NS, :128], ref[at : at + NS, 128:] = row(x)
    xl_ref[2 * NS :, :] = jnp.broadcast_to(k_ref[0:1, :], (8, NV))
    xh_ref[2 * NS :, :] = jnp.broadcast_to(k_ref[NX - 1 : NX, :], (8, NV))
    half = NS // 2
    for x in range(NX):
        t0, t1 = row(x)
        yl_ref[x * half : (x + 1) * half, :] = jnp.where(low, t0[:half], pltpu.roll(t0[half:], 64, 1))
        yh_ref[x * half : (x + 1) * half, :] = jnp.where(low, pltpu.roll(t1[half:], 64, 1), t1[:half])
    yl_ref[NX * half :, :] = k_ref[:, :128]
    yh_ref[NX * half :, :] = k_ref[:, 128:]


def whole_block(shape):
    return pl.BlockSpec(shape, lambda i: (0,) * len(shape))


def halves(v):
    return [pl.BlockSpec((v.shape[0], 128), lambda i, side=side: (0, side)) for side in range(2)]


def pack(c2d, k):
    shapes = [(2 * NS + 8, NV)] * 2 + [(NX * NS // 2 + NX, 128)] * 2
    return pl.pallas_call(
        pack_kernel,
        grid=(1,),
        out_shape=[jax.ShapeDtypeStruct(s, f32) for s in shapes],
        in_specs=halves(c2d) + [whole_block(k.shape)],
        out_specs=[whole_block(s) for s in shapes],
        compiler_params=pltpu.CompilerParams(vmem_limit_bytes=8 * 2**20),
        name="pack_faces",
    )(c2d, c2d, k)


def corner_kernel(xl_ref, xh_ref, lo_ref, hi_ref):
    for at, ref in ((0, xh_ref), (NS, xl_ref)):
        lo_ref[at : at + NS, :] = ref[0:NS, :128]
        hi_ref[at : at + NS, :] = ref[0:NS, 128:]


def corners(xl, xh):
    shapes = [(2 * NS, 128)] * 2
    return pl.pallas_call(
        corner_kernel,
        grid=(1,),
        out_shape=[jax.ShapeDtypeStruct(s, f32) for s in shapes],
        in_specs=[whole_block(v.shape) for v in (xl, xh)],
        out_specs=[whole_block(s) for s in shapes],
        compiler_params=pltpu.CompilerParams(vmem_limit_bytes=4 * 2**20),
        name="corner_columns",
    )(xl, xh)


def copies_kernel(v_ref, after_ref, out_ref):
    out_ref[...] = jnp.broadcast_to(v_ref[...][None], out_ref.shape)


def copies_of(v, count, after):
    return pl.pallas_call(
        copies_kernel,
        grid=(1,),
        out_shape=jax.ShapeDtypeStruct((count,) + v.shape, f32),
        in_specs=[whole_block(v.shape), pl.BlockSpec(memory_space=pl.ANY)],
        out_specs=whole_block((count,) + v.shape),
        compiler_params=pltpu.CompilerParams(vmem_limit_bytes=4 * 2**20),
        name="copies_of_factor",
    )(v, after)


def split_2(v):
    hi = v.astype(bf16)
    return hi, (v - hi.astype(f32)).astype(bf16)


def advance_kernel(c0_ref, c1_ref, k_ref, rate_ref, xl_ref, xh_ref, yl_ref, yh_ref, cl_ref, ch_ref, adv_ref, e0, e1, ke, left, right):
    half = NS // 2
    lane_s, lane_h = lanes(NS), lanes(half)
    z = lane_s % NZ
    not_first, not_last = z > 0, z < NZ - 1
    below, above = lane_s >= 32, lane_s < 96

    low_s, low_h = lane_s < 64, lane_h < 64
    e0[0, :, :NV] = xh_ref[NS : 2 * NS, :]
    e0[1, :, :NV] = xh_ref[0:NS, :]
    e0[1, :, NV:] = jnp.where(low_s, cl_ref[:NS, :], ch_ref[:NS, :])
    e0[NX + 2, :, :NV] = xl_ref[0:NS, :]
    e0[NX + 2, :, NV:] = jnp.where(low_s, cl_ref[NS:, :], ch_ref[NS:, :])
    e0[NX + 3, :, :NV] = xl_ref[NS : 2 * NS, :]
    e0[0, :, NV:] = jnp.zeros((NS, NH), f32)
    e0[NX + 3, :, NV:] = jnp.zeros((NS, NH), f32)
    for x in range(NX):
        after, before = yl_ref[x * half : (x + 1) * half, :], yh_ref[x * half : (x + 1) * half, :]
        e0[x + 2, :, :128] = c0_ref[pl.ds(x, NS, stride=NX), :]
        e0[x + 2, :, 128:NV] = c1_ref[pl.ds(x, NS, stride=NX), :]
        e0[x + 2, :half, NV:] = jnp.where(low_h, after, before)
        e0[x + 2, half:, NV:] = pltpu.roll(jnp.where(low_h, before, after), 64, 1)
    ke[8 : 8 + NX, :NV] = k_ref[...]
    ke[8 : 8 + NX, NV:] = jnp.where(lanes(NX) < 64, yl_ref[NX * half :, :], yh_ref[NX * half :, :])
    ke[0:8, :NV] = xh_ref[2 * NS :, :]
    ke[0:8, NV:] = jnp.zeros((8, NH), f32)
    ke[8 + NX :, :NV] = xl_ref[2 * NS :, :]
    ke[8 + NX :, NV:] = jnp.zeros((8, NH), f32)
    rate = jnp.broadcast_to(rate_ref[...], (NS, 128))

    def step(src, row, k_row, tiles):
        t = [src[row, :, i * 128 : (i + 1) * 128] for i in range(3)]
        up = [pltpu.roll(v, 96, 1) for v in t]
        down = [pltpu.roll(v, 32, 1) for v in t]
        out = []
        for i in range(tiles):
            cut = slice(i * 128, (i + 1) * 128)
            total = src[row - 1, :, cut] + src[row + 1, :, cut]
            total = total + jnp.where(above, up[i], up[(i + 1) % 3]) + jnp.where(below, down[i], down[(i + 2) % 3])
            total = total + jnp.where(not_first, pltpu.roll(t[i], 1, 1), 0.0)
            total = total + jnp.where(not_last, pltpu.roll(t[i], 127, 1), 0.0)
            lap = total - 6.0 * t[i]
            out.append(t[i] + (rate * k_row[:, cut]) * lap)
        return out

    def first_step(x, carry):
        for i, v in enumerate(step(e0, x + 1, ke[pl.ds(x + 7, 1), :], 3)):
            e1[x, :, i * 128 : (i + 1) * 128] = v
        return carry

    lax.fori_loop(0, NX + 2, first_step, 0, unroll=U1)

    def second_step(x, carry):
        done = step(e1, x + 1, ke[pl.ds(x + 8, 1), :], 2)
        left[pl.ds(x, NS, stride=NX), :], right[pl.ds(x, NS, stride=NX), :] = done
        return carry

    lax.fori_loop(0, NX, second_step, 0, unroll=U2)
    adv_ref[:, :128] = left[...]
    adv_ref[:, 128:] = right[...]


def advance(c2d, k, rate, faces):
    small = (k, rate, *faces)
    return pl.pallas_call(
        advance_kernel,
        grid=(1,),
        out_shape=jax.ShapeDtypeStruct((NS * NX, NV), f32),
        in_specs=halves(c2d) + [whole_block(v.shape) for v in small],
        out_specs=whole_block((NS * NX, NV)),
        scratch_shapes=[
            pltpu.VMEM((NX + 4, NS, NV + NH), f32),
            pltpu.VMEM((NX + 2, NS, NV + NH), f32),
            pltpu.VMEM((NX + 16, NV + NH), f32),
            pltpu.VMEM((NS * NX, 128), f32),
            pltpu.VMEM((NS * NX, 128), f32),
        ],
        compiler_params=pltpu.CompilerParams(vmem_limit_bytes=16 * 2**20),
        cost_estimate=pl.CostEstimate(flops=10000000000, bytes_accessed=4 * 2**20, transcendentals=0),
        name="advance_twice",
    )(c2d, c2d, *small)


def reduce_kernel(a0_ref, a1_ref, fs_ref, whole_ref, planes_ref):
    lane_q = lanes(NQ)
    low_q, even_q = lane_q < 64, (lane_q & 32) == 0
    fs_hi, fs_lo = split_2(fs_ref[...])
    weights = jnp.concatenate([fs_hi, fs_hi, fs_lo, fs_lo], axis=1)

    def four_rows(group, carry):
        rows = []
        for g in range(4):
            cut = pl.ds(group * 4 + g, NS, stride=NX)
            hi, lo = split_2(jnp.concatenate([a0_ref[cut, :], a1_ref[cut, :]], axis=1))
            stacked = jnp.concatenate([hi, lo, hi, lo], axis=0)
            rows.append(jnp.dot(weights, stacked, preferred_element_type=f32))
        swapped = []
        for t in range(2):
            v = [r[:, t * 128 : (t + 1) * 128] for r in rows]
            a = [jnp.where(low_q, v[g], pltpu.roll(v[g + 2], 64, 1)) for g in range(2)]
            b = [jnp.where(low_q, pltpu.roll(v[g], 64, 1), v[g + 2]) for g in range(2)]
            for p, r in (a, b):
                swapped.append(jnp.where(even_q, p, pltpu.roll(r, 32, 1)))
                swapped.append(jnp.where(even_q, pltpu.roll(p, 96, 1), r))
        turned = jnp.concatenate(swapped, axis=0).T
        for g in range(4):
            planes_ref[pl.ds(group * 4 + g, NZ, stride=NX), :] = turned[g * NZ : (g + 1) * NZ, :]
        return carry

    lax.fori_loop(0, NX // 4, four_rows, 0, unroll=U3)


def reduce_species(advanced, fs, whole):
    return pl.pallas_call(
        reduce_kernel,
        grid=(1,),
        out_shape=jax.ShapeDtypeStruct((NZ * NX, 128), f32),
        in_specs=halves(advanced) + [whole_block(fs.shape), pl.BlockSpec(memory_space=pl.ANY)],
        out_specs=whole_block((NZ * NX, 128)),
        compiler_params=pltpu.CompilerParams(vmem_limit_bytes=8 * 2**20),
        name="reduce_species",
    )(advanced, advanced, fs, whole)


def shift_to(v, dx, dy):
    axis, step = ("tx", dx) if dx else ("ty", dy)
    count = lax.axis_size(axis)
    return lax.ppermute(v, axis, [(i, i + step) for i in range(count) if 0 <= i + step < count])


def body(species, cell_factor, species_rate, factor_x, factor_y, factor_species):
    nspec, cells_x, merged = species.shape
    cells_y = factor_y.shape[0]
    depth = merged // cells_y
    n_tx, n_ty = lax.axis_size("tx"), lax.axis_size("ty")
    ranks_q = factor_species.shape[1]
    c2d = species.reshape(nspec * cells_x, merged)
    faces = pack(c2d, cell_factor)
    xl, xh, yl, yh = (shift_to(v, dx, dy) for v, (dx, dy) in zip(faces, [(-1, 0), (1, 0), (0, -1), (0, 1)]))
    lo, hi = corners(xl, xh)
    copies = copies_of(factor_x, n_tx, xh)
    faces = xl, xh, yl, yh, shift_to(lo, 0, -1), shift_to(hi, 0, 1)
    whole_x = lax.all_to_all(copies, "tx", 0, 0, tiled=True).reshape(-1, factor_x.shape[1])
    advanced = advance(c2d, cell_factor, species_rate[:, None], faces)
    planes = reduce_species(advanced, factor_species.T, whole_x)
    planes = planes.reshape(depth, cells_x, cells_y * ranks_q)
    planes = lax.all_to_all(planes, "tx", 0, 0, tiled=True).reshape(-1, cells_y * ranks_q)
    first = lax.dot_general(planes, whole_x, (((0,), (0,)), ((), ())), precision=exact_mode)
    first = first.reshape(cells_y, ranks_q, -1).transpose(1, 0, 2)
    sent = jnp.concatenate([first, jnp.broadcast_to(factor_y[None], (n_ty,) + factor_y.shape)], axis=1)
    came = lax.all_to_all(sent, "ty", 0, 0, tiled=True)
    first = came[:, :cells_y].reshape(n_ty * cells_y, -1)
    whole_y = came[:, cells_y:].reshape(n_ty * cells_y, -1)
    plane = lax.dot_general(first, whole_y, (((0,), (0,)), ((), ())), precision=exact_mode)
    rank_a, rank_b = plane.shape
    plane = plane.reshape(n_tx, rank_a // n_tx, n_ty, rank_b // n_ty).transpose(0, 2, 1, 3)
    plane = plane.reshape(n_tx * n_ty, 1, -1)
    core = lax.all_to_all(plane, ("tx", "ty"), 0, 0, tiled=True)
    core = core.reshape(depth, ranks_q, rank_a // n_tx, rank_b // n_ty).transpose(2, 1, 3, 0)
    return advanced.reshape(species.shape), core.reshape(rank_a // n_tx, ranks_q, -1)


def solution(mesh):
    in_specs = (P(None, "tx", "ty"), P("tx", "ty"), P(), P("tx", None), P("ty", None), P())
    out_specs = (P(None, "tx", "ty"), P("tx", None, "ty"))
    return jax.shard_map(body, mesh=mesh, in_specs=in_specs, out_specs=out_specs, check_vma=False)
```

```python
import jax
import jax.numpy as jnp
from jax import lax
from jax.experimental import pallas as pl
from jax.experimental.pallas import tpu as pltpu
from jax.sharding import PartitionSpec as P

exact_mode = lax.Precision.HIGHEST
f32, bf16 = jnp.float32, jnp.bfloat16
U1, U2, U3 = 2, 8, 8
NS, NX, NV, NH, NZ, NQ = 32, 32, 256, 128, 32, 16


def lanes(rows):
    return lax.broadcasted_iota(jnp.int32, (rows, 128), 1)


def pack_kernel(c0_ref, c1_ref, k_ref, xl_ref, xh_ref, yl_ref, yh_ref):
    low = lanes(NS // 2) < 64

    def row(x):
        return [r[pl.ds(x, NS, stride=NX), :] for r in (c0_ref, c1_ref)]

    for ref, at, x in ((xl_ref, 0, 0), (xl_ref, NS, 1), (xh_ref, 0, NX - 1), (xh_ref, NS, NX - 2)):
        ref[at : at + NS, :128], ref[at : at + NS, 128:] = row(x)
    xl_ref[2 * NS :, :] = jnp.broadcast_to(k_ref[0:1, :], (8, NV))
    xh_ref[2 * NS :, :] = jnp.broadcast_to(k_ref[NX - 1 : NX, :], (8, NV))
    half = NS // 2
    for x in range(NX):
        t0, t1 = row(x)
        yl_ref[x * half : (x + 1) * half, :] = jnp.where(low, t0[:half], pltpu.roll(t0[half:], 64, 1))
        yh_ref[x * half : (x + 1) * half, :] = jnp.where(low, pltpu.roll(t1[half:], 64, 1), t1[:half])
    yl_ref[NX * half :, :] = k_ref[:, :128]
    yh_ref[NX * half :, :] = k_ref[:, 128:]


def whole_block(shape):
    return pl.BlockSpec(shape, lambda i: (0,) * len(shape))


def halves(v):
    return [pl.BlockSpec((v.shape[0], 128), lambda i, side=side: (0, side)) for side in range(2)]


def pack(c2d, k):
    shapes = [(2 * NS + 8, NV)] * 2 + [(NX * NS // 2 + NX, 128)] * 2
    return pl.pallas_call(
        pack_kernel,
        grid=(1,),
        out_shape=[jax.ShapeDtypeStruct(s, f32) for s in shapes],
        in_specs=halves(c2d) + [whole_block(k.shape)],
        out_specs=[whole_block(s) for s in shapes],
        compiler_params=pltpu.CompilerParams(vmem_limit_bytes=8 * 2**20),
        name="pack_faces",
    )(c2d, c2d, k)


def corner_kernel(xl_ref, xh_ref, lo_ref, hi_ref):
    for at, ref in ((0, xh_ref), (NS, xl_ref)):
        lo_ref[at : at + NS, :] = ref[0:NS, :128]
        hi_ref[at : at + NS, :] = ref[0:NS, 128:]


def corners(xl, xh):
    shapes = [(2 * NS, 128)] * 2
    return pl.pallas_call(
        corner_kernel,
        grid=(1,),
        out_shape=[jax.ShapeDtypeStruct(s, f32) for s in shapes],
        in_specs=[whole_block(v.shape) for v in (xl, xh)],
        out_specs=[whole_block(s) for s in shapes],
        compiler_params=pltpu.CompilerParams(vmem_limit_bytes=4 * 2**20),
        name="corner_columns",
    )(xl, xh)


def copies_kernel(v_ref, after_ref, out_ref):
    out_ref[...] = jnp.broadcast_to(v_ref[...][None], out_ref.shape)


def copies_of(v, count, after):
    return pl.pallas_call(
        copies_kernel,
        grid=(1,),
        out_shape=jax.ShapeDtypeStruct((count,) + v.shape, f32),
        in_specs=[whole_block(v.shape), pl.BlockSpec(memory_space=pl.ANY)],
        out_specs=whole_block((count,) + v.shape),
        compiler_params=pltpu.CompilerParams(vmem_limit_bytes=4 * 2**20),
        name="copies_of_factor",
    )(v, after)


def split_2(v):
    hi = v.astype(bf16)
    return hi, (v - hi.astype(f32)).astype(bf16)


def advance_kernel(c0_ref, c1_ref, k_ref, rate_ref, xl_ref, xh_ref, yl_ref, yh_ref, left, right, e0, e1, ke):
    half = NS // 2
    lane_s, lane_h = lanes(NS), lanes(half)
    z = lane_s % NZ
    not_first, not_last = z > 0, z < NZ - 1
    below, above = lane_s >= 32, lane_s < 96

    low_h = lane_h < 64
    e0[0, :, :NV] = xh_ref[NS : 2 * NS, :]
    e0[1, :, :NV] = xh_ref[0:NS, :]
    e0[NX + 2, :, :NV] = xl_ref[0:NS, :]
    e0[NX + 3, :, :NV] = xl_ref[NS : 2 * NS, :]
    for row in (0, 1, NX + 2, NX + 3):
        e0[row, :, NV:] = jnp.zeros((NS, NH), f32)
    for x in range(NX):
        after, before = yl_ref[x * half : (x + 1) * half, :], yh_ref[x * half : (x + 1) * half, :]
        e0[x + 2, :, :128] = c0_ref[pl.ds(x, NS, stride=NX), :]
        e0[x + 2, :, 128:NV] = c1_ref[pl.ds(x, NS, stride=NX), :]
        e0[x + 2, :half, NV:] = jnp.where(low_h, after, before)
        e0[x + 2, half:, NV:] = pltpu.roll(jnp.where(low_h, before, after), 64, 1)
    ke[8 : 8 + NX, :NV] = k_ref[...]
    ke[8 : 8 + NX, NV:] = jnp.where(lanes(NX) < 64, yl_ref[NX * half :, :], yh_ref[NX * half :, :])
    ke[0:8, :NV] = xh_ref[2 * NS :, :]
    ke[0:8, NV:] = jnp.zeros((8, NH), f32)
    ke[8 + NX :, :NV] = xl_ref[2 * NS :, :]
    ke[8 + NX :, NV:] = jnp.zeros((8, NH), f32)
    rate = jnp.broadcast_to(rate_ref[...], (NS, 128))

    def step(src, row, k_row, tiles):
        t = [src[row, :, i * 128 : (i + 1) * 128] for i in range(3)]
        up = [pltpu.roll(v, 96, 1) for v in t]
        down = [pltpu.roll(v, 32, 1) for v in t]
        out = []
        for i in range(tiles):
            cut = slice(i * 128, (i + 1) * 128)
            total = src[row - 1, :, cut] + src[row + 1, :, cut]
            total = total + jnp.where(above, up[i], up[(i + 1) % 3]) + jnp.where(below, down[i], down[(i + 2) % 3])
            total = total + jnp.where(not_first, pltpu.roll(t[i], 1, 1), 0.0)
            total = total + jnp.where(not_last, pltpu.roll(t[i], 127, 1), 0.0)
            lap = total - 6.0 * t[i]
            out.append(t[i] + (rate * k_row[:, cut]) * lap)
        return out

    def first_step(x, carry):
        for i, v in enumerate(step(e0, x + 1, ke[pl.ds(x + 7, 1), :], 3)):
            e1[x, :, i * 128 : (i + 1) * 128] = v
        return carry

    lax.fori_loop(0, NX + 2, first_step, 0, unroll=U1)

    def second_step(x, carry):
        done = step(e1, x + 1, ke[pl.ds(x + 8, 1), :], 2)
        left[pl.ds(x, NS, stride=NX), :], right[pl.ds(x, NS, stride=NX), :] = done
        return carry

    lax.fori_loop(0, NX, second_step, 0, unroll=U2)


def advance(c2d, k, rate, faces):
    small = (k, rate, *faces)
    return pl.pallas_call(
        advance_kernel,
        grid=(1,),
        out_shape=[jax.ShapeDtypeStruct((NS * NX, 128), f32)] * 2,
        in_specs=halves(c2d) + [whole_block(v.shape) for v in small],
        out_specs=[whole_block((NS * NX, 128))] * 2,
        scratch_shapes=[
            pltpu.VMEM((NX + 4, NS, NV + NH), f32),
            pltpu.VMEM((NX + 2, NS, NV + NH), f32),
            pltpu.VMEM((NX + 16, NV + NH), f32),
        ],
        compiler_params=pltpu.CompilerParams(vmem_limit_bytes=16 * 2**20),
        cost_estimate=pl.CostEstimate(flops=10000000000, bytes_accessed=4 * 2**20, transcendentals=0),
        name="advance_twice",
    )(c2d, c2d, *small)


def reduce_kernel(a0_ref, a1_ref, k_ref, rate_ref, kxl_ref, kxh_ref, kyl_ref, kyh_ref, cl_ref, ch_ref, fs_ref, whole_ref,
                  adv_ref, planes_ref, left, right):
    left[...], right[...] = a0_ref[...], a1_ref[...]
    rate = jnp.broadcast_to(rate_ref[...], (NS, 128))
    first_y, last_y = lanes(NS) < NZ, lanes(NS) >= 128 - NZ
    for x, at, kx_ref in ((0, 0, kxh_ref), (NX - 1, NS, kxl_ref)):
        cut = pl.ds(x, NS, stride=NX)
        for ref, own, corner_ref, ky_ref, turn, mask in (
            (left, slice(0, 128), ch_ref, kyh_ref, 32, first_y),
            (right, slice(128, 256), cl_ref, kyl_ref, 96, last_y),
        ):
            paths = kx_ref[0:1, own] + pltpu.roll(jnp.broadcast_to(ky_ref[x : x + 1, :], (8, 128)), turn, 1)[0:1, :]
            term = (rate * k_ref[x : x + 1, own]) * (rate * paths) * pltpu.roll(corner_ref[at : at + NS, :], turn, 1)
            ref[cut, :] = ref[cut, :] + jnp.where(mask, term, 0.0)
    adv_ref[:, :128] = left[...]
    adv_ref[:, 128:] = right[...]

    lane_q = lanes(NQ)
    low_q, even_q = lane_q < 64, (lane_q & 32) == 0
    fs_hi, fs_lo = split_2(fs_ref[...])
    weights = jnp.concatenate([fs_hi, fs_hi, fs_lo, fs_lo], axis=1)

    def four_rows(group, carry):
        rows = []
        for g in range(4):
            cut = pl.ds(group * 4 + g, NS, stride=NX)
            hi, lo = split_2(jnp.concatenate([left[cut, :], right[cut, :]], axis=1))
            stacked = jnp.concatenate([hi, lo, hi, lo], axis=0)
            rows.append(jnp.dot(weights, stacked, preferred_element_type=f32))
        swapped = []
        for t in range(2):
            v = [r[:, t * 128 : (t + 1) * 128] for r in rows]
            a = [jnp.where(low_q, v[g], pltpu.roll(v[g + 2], 64, 1)) for g in range(2)]
            b = [jnp.where(low_q, pltpu.roll(v[g], 64, 1), v[g + 2]) for g in range(2)]
            for p, r in (a, b):
                swapped.append(jnp.where(even_q, p, pltpu.roll(r, 32, 1)))
                swapped.append(jnp.where(even_q, pltpu.roll(p, 96, 1), r))
        turned = jnp.concatenate(swapped, axis=0).T
        for g in range(4):
            planes_ref[pl.ds(group * 4 + g, NZ, stride=NX), :] = turned[g * NZ : (g + 1) * NZ, :]
        return carry

    lax.fori_loop(0, NX // 4, four_rows, 0, unroll=U3)


def reduce_species(sides, k, rate, faces, corner, fs, whole):
    xl, xh, yl, yh = faces
    tail_x, tail_y = pl.BlockSpec((8, NV), lambda i: (2 * NS // 8, 0)), pl.BlockSpec((NX, 128), lambda i: (NS // 2, 0))
    shapes = [(NS * NX, NV), (NZ * NX, 128)]
    return pl.pallas_call(
        reduce_kernel,
        grid=(1,),
        out_shape=[jax.ShapeDtypeStruct(s, f32) for s in shapes],
        in_specs=[whole_block(v.shape) for v in (*sides, k, rate)]
        + [tail_x, tail_x, tail_y, tail_y]
        + [whole_block(v.shape) for v in (*corner, fs)]
        + [pl.BlockSpec(memory_space=pl.ANY)],
        out_specs=[whole_block(s) for s in shapes],
        scratch_shapes=[pltpu.VMEM((NS * NX, 128), f32)] * 2,
        compiler_params=pltpu.CompilerParams(vmem_limit_bytes=12 * 2**20),
        name="reduce_species",
    )(*sides, k, rate, xl, xh, yl, yh, *corner, fs, whole)


def shift_to(v, dx, dy):
    axis, step = ("tx", dx) if dx else ("ty", dy)
    count = lax.axis_size(axis)
    return lax.ppermute(v, axis, [(i, i + step) for i in range(count) if 0 <= i + step < count])


def body(species, cell_factor, species_rate, factor_x, factor_y, factor_species):
    nspec, cells_x, merged = species.shape
    cells_y = factor_y.shape[0]
    depth = merged // cells_y
    n_tx, n_ty = lax.axis_size("tx"), lax.axis_size("ty")
    ranks_q = factor_species.shape[1]
    c2d = species.reshape(nspec * cells_x, merged)
    faces = pack(c2d, cell_factor)
    xl, xh, yl, yh = (shift_to(v, dx, dy) for v, (dx, dy) in zip(faces, [(-1, 0), (1, 0), (0, -1), (0, 1)]))
    lo, hi = corners(xl, xh)
    copies = copies_of(factor_x, n_tx, xh)
    corner = shift_to(lo, 0, -1), shift_to(hi, 0, 1)
    whole_x = lax.all_to_all(copies, "tx", 0, 0, tiled=True).reshape(-1, factor_x.shape[1])
    faces, rate = (xl, xh, yl, yh), species_rate[:, None]
    sides = advance(c2d, cell_factor, rate, faces)
    advanced, planes = reduce_species(sides, cell_factor, rate, faces, corner, factor_species.T, whole_x)
    planes = planes.reshape(depth, cells_x, cells_y * ranks_q)
    planes = lax.all_to_all(planes, "tx", 0, 0, tiled=True).reshape(-1, cells_y * ranks_q)
    first = lax.dot_general(planes, whole_x, (((0,), (0,)), ((), ())), precision=exact_mode)
    first = first.reshape(cells_y, ranks_q, -1).transpose(1, 0, 2)
    sent = jnp.concatenate([first, jnp.broadcast_to(factor_y[None], (n_ty,) + factor_y.shape)], axis=1)
    came = lax.all_to_all(sent, "ty", 0, 0, tiled=True)
    first = came[:, :cells_y].reshape(n_ty * cells_y, -1)
    whole_y = came[:, cells_y:].reshape(n_ty * cells_y, -1)
    plane = lax.dot_general(first, whole_y, (((0,), (0,)), ((), ())), precision=exact_mode)
    rank_a, rank_b = plane.shape
    plane = plane.reshape(n_tx, rank_a // n_tx, n_ty, rank_b // n_ty).transpose(0, 2, 1, 3)
    plane = plane.reshape(n_tx * n_ty, 1, -1)
    core = lax.all_to_all(plane, ("tx", "ty"), 0, 0, tiled=True)
    core = core.reshape(depth, ranks_q, rank_a // n_tx, rank_b // n_ty).transpose(2, 1, 3, 0)
    return advanced.reshape(species.shape), core.reshape(rank_a // n_tx, ranks_q, -1)


def solution(mesh):
    in_specs = (P(None, "tx", "ty"), P("tx", "ty"), P(), P("tx", None), P("ty", None), P())
    out_specs = (P(None, "tx", "ty"), P("tx", None, "ty"))
    return jax.shard_map(body, mesh=mesh, in_specs=in_specs, out_specs=out_specs, check_vma=False)
```

```python
import jax
import jax.numpy as jnp
from jax import lax
from jax.experimental import pallas as pl
from jax.experimental.pallas import tpu as pltpu
from jax.sharding import PartitionSpec as P

exact_mode = lax.Precision.HIGHEST
f32, bf16 = jnp.float32, jnp.bfloat16
U1, U2, U3 = 2, 8, 8
NS, NX, NV, NH, NZ, NQ = 32, 32, 256, 128, 32, 16


def lanes(rows):
    return lax.broadcasted_iota(jnp.int32, (rows, 128), 1)


def pack_kernel(c0_ref, c1_ref, k_ref, xl_ref, xh_ref, yl_ref, yh_ref):
    low = lanes(NS // 2) < 64

    def row(x):
        return [r[pl.ds(x, NS, stride=NX), :] for r in (c0_ref, c1_ref)]

    for ref, at, x in ((xl_ref, 0, 0), (xl_ref, NS, 1), (xh_ref, 0, NX - 1), (xh_ref, NS, NX - 2)):
        ref[at : at + NS, :128], ref[at : at + NS, 128:] = row(x)
    xl_ref[2 * NS :, :] = jnp.broadcast_to(k_ref[0:1, :], (8, NV))
    xh_ref[2 * NS :, :] = jnp.broadcast_to(k_ref[NX - 1 : NX, :], (8, NV))
    half = NS // 2
    for x in range(NX):
        t0, t1 = row(x)
        yl_ref[x * half : (x + 1) * half, :] = jnp.where(low, t0[:half], pltpu.roll(t0[half:], 64, 1))
        yh_ref[x * half : (x + 1) * half, :] = jnp.where(low, pltpu.roll(t1[half:], 64, 1), t1[:half])
    yl_ref[NX * half :, :] = k_ref[:, :128]
    yh_ref[NX * half :, :] = k_ref[:, 128:]


def whole_block(shape):
    return pl.BlockSpec(shape, lambda i: (0,) * len(shape))


def halves(v):
    return [pl.BlockSpec((v.shape[0], 128), lambda i, side=side: (0, side)) for side in range(2)]


def pack(c2d, k):
    shapes = [(2 * NS + 8, NV)] * 2 + [(NX * NS // 2 + NX, 128)] * 2
    return pl.pallas_call(
        pack_kernel,
        grid=(1,),
        out_shape=[jax.ShapeDtypeStruct(s, f32) for s in shapes],
        in_specs=halves(c2d) + [whole_block(k.shape)],
        out_specs=[whole_block(s) for s in shapes],
        compiler_params=pltpu.CompilerParams(vmem_limit_bytes=8 * 2**20),
        name="pack_faces",
    )(c2d, c2d, k)


def corner_kernel(xl_ref, xh_ref, lo_ref, hi_ref):
    for at, ref in ((0, xh_ref), (NS, xl_ref)):
        lo_ref[at : at + NS, :] = ref[0:NS, :128]
        hi_ref[at : at + NS, :] = ref[0:NS, 128:]


def corners(xl, xh):
    shapes = [(2 * NS, 128)] * 2
    return pl.pallas_call(
        corner_kernel,
        grid=(1,),
        out_shape=[jax.ShapeDtypeStruct(s, f32) for s in shapes],
        in_specs=[whole_block(v.shape) for v in (xl, xh)],
        out_specs=[whole_block(s) for s in shapes],
        compiler_params=pltpu.CompilerParams(vmem_limit_bytes=4 * 2**20),
        name="corner_columns",
    )(xl, xh)


def copies_kernel(v_ref, after0_ref, after1_ref, out_ref):
    out_ref[...] = jnp.broadcast_to(v_ref[...][None], out_ref.shape)


def copies_of(v, count, after):
    return pl.pallas_call(
        copies_kernel,
        grid=(1,),
        out_shape=jax.ShapeDtypeStruct((count,) + v.shape, f32),
        in_specs=[whole_block(v.shape)] + [pl.BlockSpec(memory_space=pl.ANY)] * 2,
        out_specs=whole_block((count,) + v.shape),
        compiler_params=pltpu.CompilerParams(vmem_limit_bytes=4 * 2**20),
        name="copies_of_factor",
    )(v, *after)


def split_2(v):
    hi = v.astype(bf16)
    return hi, (v - hi.astype(f32)).astype(bf16)


def advance_kernel(c0_ref, c1_ref, k_ref, rate_ref, xl_ref, xh_ref, yl_ref, yh_ref, left, right, e0, e1, ke):
    half = NS // 2
    lane_s, lane_h = lanes(NS), lanes(half)
    z = lane_s % NZ
    not_first, not_last = z > 0, z < NZ - 1
    below, above = lane_s >= 32, lane_s < 96

    low_h = lane_h < 64
    e0[0, :, :NV] = xh_ref[NS : 2 * NS, :]
    e0[1, :, :NV] = xh_ref[0:NS, :]
    e0[NX + 2, :, :NV] = xl_ref[0:NS, :]
    e0[NX + 3, :, :NV] = xl_ref[NS : 2 * NS, :]
    for row in (0, 1, NX + 2, NX + 3):
        e0[row, :, NV:] = jnp.zeros((NS, NH), f32)
    for x in range(NX):
        after, before = yl_ref[x * half : (x + 1) * half, :], yh_ref[x * half : (x + 1) * half, :]
        e0[x + 2, :, :128] = c0_ref[pl.ds(x, NS, stride=NX), :]
        e0[x + 2, :, 128:NV] = c1_ref[pl.ds(x, NS, stride=NX), :]
        e0[x + 2, :half, NV:] = jnp.where(low_h, after, before)
        e0[x + 2, half:, NV:] = pltpu.roll(jnp.where(low_h, before, after), 64, 1)
    ke[8 : 8 + NX, :NV] = k_ref[...]
    ke[8 : 8 + NX, NV:] = jnp.where(lanes(NX) < 64, yl_ref[NX * half :, :], yh_ref[NX * half :, :])
    ke[0:8, :NV] = xh_ref[2 * NS :, :]
    ke[0:8, NV:] = jnp.zeros((8, NH), f32)
    ke[8 + NX :, :NV] = xl_ref[2 * NS :, :]
    ke[8 + NX :, NV:] = jnp.zeros((8, NH), f32)
    rate = jnp.broadcast_to(rate_ref[...], (NS, 128))

    def step(src, row, k_row, tiles):
        t = [src[row, :, i * 128 : (i + 1) * 128] for i in range(3)]
        up = [pltpu.roll(v, 96, 1) for v in t]
        down = [pltpu.roll(v, 32, 1) for v in t]
        out = []
        for i in range(tiles):
            cut = slice(i * 128, (i + 1) * 128)
            total = src[row - 1, :, cut] + src[row + 1, :, cut]
            total = total + jnp.where(above, up[i], up[(i + 1) % 3]) + jnp.where(below, down[i], down[(i + 2) % 3])
            total = total + jnp.where(not_first, pltpu.roll(t[i], 1, 1), 0.0)
            total = total + jnp.where(not_last, pltpu.roll(t[i], 127, 1), 0.0)
            lap = total - 6.0 * t[i]
            out.append(t[i] + (rate * k_row[:, cut]) * lap)
        return out

    def first_step(x, carry):
        for i, v in enumerate(step(e0, x + 1, ke[pl.ds(x + 7, 1), :], 3)):
            e1[x, :, i * 128 : (i + 1) * 128] = v
        return carry

    lax.fori_loop(0, NX + 2, first_step, 0, unroll=U1)

    def second_step(x, carry):
        done = step(e1, x + 1, ke[pl.ds(x + 8, 1), :], 2)
        left[pl.ds(x, NS, stride=NX), :], right[pl.ds(x, NS, stride=NX), :] = done
        return carry

    lax.fori_loop(0, NX, second_step, 0, unroll=U2)


def advance(c2d, k, rate, faces):
    small = (k, rate, *faces)
    return pl.pallas_call(
        advance_kernel,
        grid=(1,),
        out_shape=[jax.ShapeDtypeStruct((NS * NX, 128), f32)] * 2,
        in_specs=halves(c2d) + [whole_block(v.shape) for v in small],
        out_specs=[whole_block((NS * NX, 128))] * 2,
        scratch_shapes=[
            pltpu.VMEM((NX + 4, NS, NV + NH), f32),
            pltpu.VMEM((NX + 2, NS, NV + NH), f32),
            pltpu.VMEM((NX + 16, NV + NH), f32),
        ],
        compiler_params=pltpu.CompilerParams(vmem_limit_bytes=16 * 2**20),
        cost_estimate=pl.CostEstimate(flops=10000000000, bytes_accessed=4 * 2**20, transcendentals=0),
        name="advance_twice",
    )(c2d, c2d, *small)


def reduce_kernel(a0_ref, a1_ref, k_ref, rate_ref, kxl_ref, kxh_ref, kyl_ref, kyh_ref, cl_ref, ch_ref, fs_ref, whole_ref,
                  adv_ref, planes_ref, left, right):
    left[...], right[...] = a0_ref[...], a1_ref[...]
    rate = jnp.broadcast_to(rate_ref[...], (NS, 128))
    first_y, last_y = lanes(NS) < NZ, lanes(NS) >= 128 - NZ
    for x, at, kx_ref in ((0, 0, kxh_ref), (NX - 1, NS, kxl_ref)):
        cut = pl.ds(x, NS, stride=NX)
        for ref, own, corner_ref, ky_ref, turn, mask in (
            (left, slice(0, 128), ch_ref, kyh_ref, 32, first_y),
            (right, slice(128, 256), cl_ref, kyl_ref, 96, last_y),
        ):
            paths = kx_ref[0:1, own] + pltpu.roll(jnp.broadcast_to(ky_ref[x : x + 1, :], (8, 128)), turn, 1)[0:1, :]
            term = (rate * k_ref[x : x + 1, own]) * (rate * paths) * pltpu.roll(corner_ref[at : at + NS, :], turn, 1)
            ref[cut, :] = ref[cut, :] + jnp.where(mask, term, 0.0)
    adv_ref[:, :128] = left[...]
    adv_ref[:, 128:] = right[...]

    lane_q = lanes(NQ)
    low_q, even_q = lane_q < 64, (lane_q & 32) == 0
    fs_hi, fs_lo = split_2(fs_ref[...])
    weights = jnp.concatenate([fs_hi, fs_hi, fs_lo, fs_lo], axis=1)

    def four_rows(group, carry):
        rows = []
        for g in range(4):
            cut = pl.ds(group * 4 + g, NS, stride=NX)
            hi, lo = split_2(jnp.concatenate([left[cut, :], right[cut, :]], axis=1))
            stacked = jnp.concatenate([hi, lo, hi, lo], axis=0)
            rows.append(jnp.dot(weights, stacked, preferred_element_type=f32))
        swapped = []
        for t in range(2):
            v = [r[:, t * 128 : (t + 1) * 128] for r in rows]
            a = [jnp.where(low_q, v[g], pltpu.roll(v[g + 2], 64, 1)) for g in range(2)]
            b = [jnp.where(low_q, pltpu.roll(v[g], 64, 1), v[g + 2]) for g in range(2)]
            for p, r in (a, b):
                swapped.append(jnp.where(even_q, p, pltpu.roll(r, 32, 1)))
                swapped.append(jnp.where(even_q, pltpu.roll(p, 96, 1), r))
        turned = jnp.concatenate(swapped, axis=0).T
        for g in range(4):
            planes_ref[pl.ds(group * 4 + g, NZ, stride=NX), :] = turned[g * NZ : (g + 1) * NZ, :]
        return carry

    lax.fori_loop(0, NX // 4, four_rows, 0, unroll=U3)


def reduce_species(sides, k, rate, faces, corner, fs, whole):
    xl, xh, yl, yh = faces
    tail_x, tail_y = pl.BlockSpec((8, NV), lambda i: (2 * NS // 8, 0)), pl.BlockSpec((NX, 128), lambda i: (NS // 2, 0))
    shapes = [(NS * NX, NV), (NZ * NX, 128)]
    return pl.pallas_call(
        reduce_kernel,
        grid=(1,),
        out_shape=[jax.ShapeDtypeStruct(s, f32) for s in shapes],
        in_specs=[whole_block(v.shape) for v in (*sides, k, rate)]
        + [tail_x, tail_x, tail_y, tail_y]
        + [whole_block(v.shape) for v in (*corner, fs)]
        + [pl.BlockSpec(memory_space=pl.ANY)],
        out_specs=[whole_block(s) for s in shapes],
        scratch_shapes=[pltpu.VMEM((NS * NX, 128), f32)] * 2,
        compiler_params=pltpu.CompilerParams(vmem_limit_bytes=12 * 2**20),
        name="reduce_species",
    )(*sides, k, rate, xl, xh, yl, yh, *corner, fs, whole)


def shift_to(v, dx, dy):
    axis, step = ("tx", dx) if dx else ("ty", dy)
    count = lax.axis_size(axis)
    return lax.ppermute(v, axis, [(i, i + step) for i in range(count) if 0 <= i + step < count])


def body(species, cell_factor, species_rate, factor_x, factor_y, factor_species):
    nspec, cells_x, merged = species.shape
    cells_y = factor_y.shape[0]
    depth = merged // cells_y
    n_tx, n_ty = lax.axis_size("tx"), lax.axis_size("ty")
    ranks_q = factor_species.shape[1]
    c2d = species.reshape(nspec * cells_x, merged)
    faces = pack(c2d, cell_factor)
    xl, xh, yl, yh = (shift_to(v, dx, dy) for v, (dx, dy) in zip(faces, [(-1, 0), (1, 0), (0, -1), (0, 1)]))
    lo, hi = corners(xl, xh)
    copies = copies_of(factor_x, n_tx, (xl, xh))
    corner = shift_to(lo, 0, -1), shift_to(hi, 0, 1)
    whole_x = lax.all_to_all(copies, "tx", 0, 0, tiled=True).reshape(-1, factor_x.shape[1])
    faces, rate = (xl, xh, yl, yh), species_rate[:, None]
    sides = advance(c2d, cell_factor, rate, faces)
    advanced, planes = reduce_species(sides, cell_factor, rate, faces, corner, factor_species.T, whole_x)
    planes = planes.reshape(depth, cells_x, cells_y * ranks_q)
    planes = lax.all_to_all(planes, "tx", 0, 0, tiled=True).reshape(-1, cells_y * ranks_q)
    first = lax.dot_general(planes, whole_x, (((0,), (0,)), ((), ())), precision=exact_mode)
    first = first.reshape(cells_y, ranks_q, -1).transpose(1, 0, 2)
    sent = jnp.concatenate([first, jnp.broadcast_to(factor_y[None], (n_ty,) + factor_y.shape)], axis=1)
    came = lax.all_to_all(sent, "ty", 0, 0, tiled=True)
    first = came[:, :cells_y].reshape(n_ty * cells_y, -1)
    whole_y = came[:, cells_y:].reshape(n_ty * cells_y, -1)
    plane = lax.dot_general(first, whole_y, (((0,), (0,)), ((), ())), precision=exact_mode)
    rank_a, rank_b = plane.shape
    plane = plane.reshape(n_tx, rank_a // n_tx, n_ty, rank_b // n_ty).transpose(0, 2, 1, 3)
    plane = plane.reshape(n_tx * n_ty, 1, -1)
    core = lax.all_to_all(plane, ("tx", "ty"), 0, 0, tiled=True)
    core = core.reshape(depth, ranks_q, rank_a // n_tx, rank_b // n_ty).transpose(2, 1, 3, 0)
    return advanced.reshape(species.shape), core.reshape(rank_a // n_tx, ranks_q, -1)


def solution(mesh):
    in_specs = (P(None, "tx", "ty"), P("tx", "ty"), P(), P("tx", None), P("ty", None), P())
    out_specs = (P(None, "tx", "ty"), P("tx", None, "ty"))
    return jax.shard_map(body, mesh=mesh, in_specs=in_specs, out_specs=out_specs, check_vma=False)
```

```python
import jax
import jax.numpy as jnp
from jax import lax
from jax.experimental import pallas as pl
from jax.experimental.pallas import tpu as pltpu
from jax.sharding import PartitionSpec as P

exact_mode = lax.Precision.HIGHEST
f32, bf16 = jnp.float32, jnp.bfloat16
NS, NX, NV, NH, NZ, NQ = 32, 32, 256, 128, 32, 16


def lanes(rows):
    return lax.broadcasted_iota(jnp.int32, (rows, 128), 1)


def pack_kernel(c0_ref, c1_ref, k_ref, xl_ref, xh_ref, yl_ref, yh_ref):
    low = lanes(NS // 2) < 64

    def row(x):
        return [r[pl.ds(x, NS, stride=NX), :] for r in (c0_ref, c1_ref)]

    for ref, at, x in ((xl_ref, 0, 0), (xl_ref, NS, 1), (xh_ref, 0, NX - 1), (xh_ref, NS, NX - 2)):
        ref[at : at + NS, :128], ref[at : at + NS, 128:] = row(x)
    xl_ref[2 * NS :, :] = jnp.broadcast_to(k_ref[0:1, :], (8, NV))
    xh_ref[2 * NS :, :] = jnp.broadcast_to(k_ref[NX - 1 : NX, :], (8, NV))
    half = NS // 2
    for x in range(NX):
        t0, t1 = row(x)
        yl_ref[x * half : (x + 1) * half, :] = jnp.where(low, t0[:half], pltpu.roll(t0[half:], 64, 1))
        yh_ref[x * half : (x + 1) * half, :] = jnp.where(low, pltpu.roll(t1[half:], 64, 1), t1[:half])
    yl_ref[NX * half :, :] = k_ref[:, :128]
    yh_ref[NX * half :, :] = k_ref[:, 128:]


def whole_block(shape):
    return pl.BlockSpec(shape, lambda i: (0,) * len(shape))


def halves(v):
    return [pl.BlockSpec((v.shape[0], 128), lambda i, side=side: (0, side)) for side in range(2)]


def pack(c2d, k):
    shapes = [(2 * NS + 8, NV)] * 2 + [(NX * NS // 2 + NX, 128)] * 2
    return pl.pallas_call(
        pack_kernel,
        grid=(1,),
        out_shape=[jax.ShapeDtypeStruct(s, f32) for s in shapes],
        in_specs=halves(c2d) + [whole_block(k.shape)],
        out_specs=[whole_block(s) for s in shapes],
        compiler_params=pltpu.CompilerParams(vmem_limit_bytes=8 * 2**20),
        name="pack_faces",
    )(c2d, c2d, k)


def corner_kernel(xl_ref, xh_ref, fx_ref, lo_ref, hi_ref, copies_ref):
    for at, ref in ((0, xh_ref), (NS, xl_ref)):
        lo_ref[at : at + NS, :] = ref[0:NS, :128]
        hi_ref[at : at + NS, :] = ref[0:NS, 128:]
    copies_ref[...] = jnp.broadcast_to(fx_ref[...][None], copies_ref.shape)


def corners(xl, xh, factor_x, count):
    shapes = [(2 * NS, 128)] * 2 + [(count,) + factor_x.shape]
    return pl.pallas_call(
        corner_kernel,
        grid=(1,),
        out_shape=[jax.ShapeDtypeStruct(s, f32) for s in shapes],
        in_specs=[whole_block(v.shape) for v in (xl, xh, factor_x)],
        out_specs=[whole_block(s) for s in shapes],
        compiler_params=pltpu.CompilerParams(vmem_limit_bytes=4 * 2**20),
        name="corner_columns",
    )(xl, xh, factor_x)


def split_2(v):
    hi = v.astype(bf16)
    return hi, (v - hi.astype(f32)).astype(bf16)


def advance_kernel(c0_ref, c1_ref, k_ref, rate_ref, xl_ref, xh_ref, yl_ref, yh_ref, left, right, e0, e1, ke):
    half = NS // 2
    lane_s, lane_h = lanes(NS), lanes(half)
    z = lane_s % NZ
    not_first, not_last = z > 0, z < NZ - 1
    below, above = lane_s >= 32, lane_s < 96

    low_h = lane_h < 64
    e0[0, :, :NV] = xh_ref[NS : 2 * NS, :]
    e0[1, :, :NV] = xh_ref[0:NS, :]
    e0[NX + 2, :, :NV] = xl_ref[0:NS, :]
    e0[NX + 3, :, :NV] = xl_ref[NS : 2 * NS, :]
    for row in (0, 1, NX + 2, NX + 3):
        e0[row, :, NV:] = jnp.zeros((NS, NH), f32)
    for x in range(NX):
        after, before = yl_ref[x * half : (x + 1) * half, :], yh_ref[x * half : (x + 1) * half, :]
        e0[x + 2, :, :128] = c0_ref[pl.ds(x, NS, stride=NX), :]
        e0[x + 2, :, 128:NV] = c1_ref[pl.ds(x, NS, stride=NX), :]
        e0[x + 2, :half, NV:] = jnp.where(low_h, after, before)
        e0[x + 2, half:, NV:] = pltpu.roll(jnp.where(low_h, before, after), 64, 1)
    ke[8 : 8 + NX, :NV] = k_ref[...]
    ke[8 : 8 + NX, NV:] = jnp.where(lanes(NX) < 64, yl_ref[NX * half :, :], yh_ref[NX * half :, :])
    ke[0:8, :NV] = xh_ref[2 * NS :, :]
    ke[0:8, NV:] = jnp.zeros((8, NH), f32)
    ke[8 + NX :, :NV] = xl_ref[2 * NS :, :]
    ke[8 + NX :, NV:] = jnp.zeros((8, NH), f32)
    rate = jnp.broadcast_to(rate_ref[...], (NS, 128))

    def step(src, row, k_row, tiles):
        t = [src[row, :, i * 128 : (i + 1) * 128] for i in range(3)]
        up = [pltpu.roll(v, 96, 1) for v in t]
        down = [pltpu.roll(v, 32, 1) for v in t]
        out = []
        for i in range(tiles):
            cut = slice(i * 128, (i + 1) * 128)
            total = src[row - 1, :, cut] + src[row + 1, :, cut]
            total = total + jnp.where(above, up[i], up[(i + 1) % 3]) + jnp.where(below, down[i], down[(i + 2) % 3])
            total = total + jnp.where(not_first, pltpu.roll(t[i], 1, 1), 0.0)
            total = total + jnp.where(not_last, pltpu.roll(t[i], 127, 1), 0.0)
            lap = total - 6.0 * t[i]
            out.append(t[i] + (rate * k_row[:, cut]) * lap)
        return out

    def first_step(x, carry):
        for i, v in enumerate(step(e0, x + 1, ke[pl.ds(x + 7, 1), :], 3)):
            e1[x, :, i * 128 : (i + 1) * 128] = v
        return carry

    lax.fori_loop(0, NX + 2, first_step, 0, unroll=True)

    def second_step(x, carry):
        done = step(e1, x + 1, ke[pl.ds(x + 8, 1), :], 2)
        left[pl.ds(x, NS, stride=NX), :], right[pl.ds(x, NS, stride=NX), :] = done
        return carry

    lax.fori_loop(0, NX, second_step, 0, unroll=True)


def advance(c2d, k, rate, faces):
    small = (k, rate, *faces)
    return pl.pallas_call(
        advance_kernel,
        grid=(1,),
        out_shape=[jax.ShapeDtypeStruct((NS * NX, 128), f32)] * 2,
        in_specs=halves(c2d) + [whole_block(v.shape) for v in small],
        out_specs=[whole_block((NS * NX, 128))] * 2,
        scratch_shapes=[
            pltpu.VMEM((NX + 4, NS, NV + NH), f32),
            pltpu.VMEM((NX + 2, NS, NV + NH), f32),
            pltpu.VMEM((NX + 16, NV + NH), f32),
        ],
        compiler_params=pltpu.CompilerParams(vmem_limit_bytes=16 * 2**20),
        cost_estimate=pl.CostEstimate(flops=10000000000, bytes_accessed=4 * 2**20, transcendentals=0),
        name="advance_twice",
    )(c2d, c2d, *small)


def reduce_kernel(a0_ref, a1_ref, k_ref, rate_ref, kxl_ref, kxh_ref, kyl_ref, kyh_ref, cl_ref, ch_ref, fs_ref, whole_ref,
                  adv_ref, planes_ref, left, right):
    left[...], right[...] = a0_ref[...], a1_ref[...]
    rate = jnp.broadcast_to(rate_ref[...], (NS, 128))
    first_y, last_y = lanes(NS) < NZ, lanes(NS) >= 128 - NZ
    for x, at, kx_ref in ((0, 0, kxh_ref), (NX - 1, NS, kxl_ref)):
        cut = pl.ds(x, NS, stride=NX)
        for ref, own, corner_ref, ky_ref, turn, mask in (
            (left, slice(0, 128), ch_ref, kyh_ref, 32, first_y),
            (right, slice(128, 256), cl_ref, kyl_ref, 96, last_y),
        ):
            paths = kx_ref[0:1, own] + pltpu.roll(jnp.broadcast_to(ky_ref[x : x + 1, :], (8, 128)), turn, 1)[0:1, :]
            term = (rate * k_ref[x : x + 1, own]) * (rate * paths) * pltpu.roll(corner_ref[at : at + NS, :], turn, 1)
            ref[cut, :] = ref[cut, :] + jnp.where(mask, term, 0.0)
    adv_ref[:, :128] = left[...]
    adv_ref[:, 128:] = right[...]

    lane_q = lanes(NQ)
    low_q, even_q = lane_q < 64, (lane_q & 32) == 0
    fs_hi, fs_lo = split_2(fs_ref[...])
    weights = jnp.concatenate([fs_hi, fs_hi, fs_lo, fs_lo], axis=1)

    def four_rows(group, carry):
        rows = []
        for g in range(4):
            cut = pl.ds(group * 4 + g, NS, stride=NX)
            hi, lo = split_2(jnp.concatenate([left[cut, :], right[cut, :]], axis=1))
            stacked = jnp.concatenate([hi, lo, hi, lo], axis=0)
            rows.append(jnp.dot(weights, stacked, preferred_element_type=f32))
        swapped = []
        for t in range(2):
            v = [r[:, t * 128 : (t + 1) * 128] for r in rows]
            a = [jnp.where(low_q, v[g], pltpu.roll(v[g + 2], 64, 1)) for g in range(2)]
            b = [jnp.where(low_q, pltpu.roll(v[g], 64, 1), v[g + 2]) for g in range(2)]
            for p, r in (a, b):
                swapped.append(jnp.where(even_q, p, pltpu.roll(r, 32, 1)))
                swapped.append(jnp.where(even_q, pltpu.roll(p, 96, 1), r))
        turned = jnp.concatenate(swapped, axis=0).T
        for g in range(4):
            planes_ref[pl.ds(group * 4 + g, NZ, stride=NX), :] = turned[g * NZ : (g + 1) * NZ, :]
        return carry

    lax.fori_loop(0, NX // 4, four_rows, 0, unroll=True)


def reduce_species(sides, k, rate, faces, corner, fs, whole):
    xl, xh, yl, yh = faces
    tail_x, tail_y = pl.BlockSpec((8, NV), lambda i: (2 * NS // 8, 0)), pl.BlockSpec((NX, 128), lambda i: (NS // 2, 0))
    shapes = [(NS * NX, NV), (NZ * NX, 128)]
    return pl.pallas_call(
        reduce_kernel,
        grid=(1,),
        out_shape=[jax.ShapeDtypeStruct(s, f32) for s in shapes],
        in_specs=[whole_block(v.shape) for v in (*sides, k, rate)]
        + [tail_x, tail_x, tail_y, tail_y]
        + [whole_block(v.shape) for v in (*corner, fs)]
        + [pl.BlockSpec(memory_space=pl.ANY)],
        out_specs=[whole_block(s) for s in shapes],
        scratch_shapes=[pltpu.VMEM((NS * NX, 128), f32)] * 2,
        compiler_params=pltpu.CompilerParams(vmem_limit_bytes=12 * 2**20),
        name="reduce_species",
    )(*sides, k, rate, xl, xh, yl, yh, *corner, fs, whole)


def shift_to(v, dx, dy):
    axis, step = ("tx", dx) if dx else ("ty", dy)
    count = lax.axis_size(axis)
    return lax.ppermute(v, axis, [(i, i + step) for i in range(count) if 0 <= i + step < count])


def body(species, cell_factor, species_rate, factor_x, factor_y, factor_species):
    nspec, cells_x, merged = species.shape
    cells_y = factor_y.shape[0]
    depth = merged // cells_y
    n_tx, n_ty = lax.axis_size("tx"), lax.axis_size("ty")
    ranks_q = factor_species.shape[1]
    c2d = species.reshape(nspec * cells_x, merged)
    faces = pack(c2d, cell_factor)
    xl, xh, yl, yh = (shift_to(v, dx, dy) for v, (dx, dy) in zip(faces, [(-1, 0), (1, 0), (0, -1), (0, 1)]))
    lo, hi, copies = corners(xl, xh, factor_x, n_tx)
    corner = shift_to(lo, 0, -1), shift_to(hi, 0, 1)
    whole_x = lax.all_to_all(copies, "tx", 0, 0, tiled=True).reshape(-1, factor_x.shape[1])
    faces, rate = (xl, xh, yl, yh), species_rate[:, None]
    sides = advance(c2d, cell_factor, rate, faces)
    advanced, planes = reduce_species(sides, cell_factor, rate, faces, corner, factor_species.T, whole_x)
    planes = planes.reshape(depth, cells_x, cells_y * ranks_q)
    planes = lax.all_to_all(planes, "tx", 0, 0, tiled=True).reshape(-1, cells_y * ranks_q)
    first = lax.dot_general(planes, whole_x, (((0,), (0,)), ((), ())), precision=exact_mode)
    first = first.reshape(cells_y, ranks_q, -1).transpose(1, 0, 2)
    sent = jnp.concatenate([first, jnp.broadcast_to(factor_y[None], (n_ty,) + factor_y.shape)], axis=1)
    came = lax.all_to_all(sent, "ty", 0, 0, tiled=True)
    first = came[:, :cells_y].reshape(n_ty * cells_y, -1)
    whole_y = came[:, cells_y:].reshape(n_ty * cells_y, -1)
    plane = lax.dot_general(first, whole_y, (((0,), (0,)), ((), ())), precision=exact_mode)
    rank_a, rank_b = plane.shape
    plane = plane.reshape(n_tx, rank_a // n_tx, n_ty, rank_b // n_ty).transpose(0, 2, 1, 3)
    plane = plane.reshape(n_tx * n_ty, 1, -1)
    core = lax.all_to_all(plane, ("tx", "ty"), 0, 0, tiled=True)
    core = core.reshape(depth, ranks_q, rank_a // n_tx, rank_b // n_ty).transpose(2, 1, 3, 0)
    return advanced.reshape(species.shape), core.reshape(rank_a // n_tx, ranks_q, -1)


def solution(mesh):
    in_specs = (P(None, "tx", "ty"), P("tx", "ty"), P(), P("tx", None), P("ty", None), P())
    out_specs = (P(None, "tx", "ty"), P("tx", None, "ty"))
    return jax.shard_map(body, mesh=mesh, in_specs=in_specs, out_specs=out_specs, check_vma=False)
```

```python
import jax
import jax.numpy as jnp
from jax import lax
from jax.experimental import pallas as pl
from jax.experimental.pallas import tpu as pltpu
from jax.sharding import PartitionSpec as P

exact_mode = lax.Precision.HIGHEST
f32, bf16 = jnp.float32, jnp.bfloat16
NS, NX, NV, NH, NZ, NQ = 32, 32, 256, 128, 32, 16


def lanes(rows):
    return lax.broadcasted_iota(jnp.int32, (rows, 128), 1)


def pack_kernel(c0_ref, c1_ref, k_ref, xl_ref, xh_ref, yl_ref, yh_ref):
    low = lanes(NS // 2) < 64

    def row(x):
        return [r[pl.ds(x, NS, stride=NX), :] for r in (c0_ref, c1_ref)]

    for ref, at, x in ((xl_ref, 0, 0), (xl_ref, NS, 1), (xh_ref, 0, NX - 1), (xh_ref, NS, NX - 2)):
        ref[at : at + NS, :128], ref[at : at + NS, 128:] = row(x)
    xl_ref[2 * NS :, :] = jnp.broadcast_to(k_ref[0:1, :], (8, NV))
    xh_ref[2 * NS :, :] = jnp.broadcast_to(k_ref[NX - 1 : NX, :], (8, NV))
    half = NS // 2
    for x in range(NX):
        t0, t1 = row(x)
        yl_ref[x * half : (x + 1) * half, :] = jnp.where(low, t0[:half], pltpu.roll(t0[half:], 64, 1))
        yh_ref[x * half : (x + 1) * half, :] = jnp.where(low, pltpu.roll(t1[half:], 64, 1), t1[:half])
    yl_ref[NX * half :, :] = k_ref[:, :128]
    yh_ref[NX * half :, :] = k_ref[:, 128:]


def whole_block(shape):
    return pl.BlockSpec(shape, lambda i: (0,) * len(shape))


def halves(v):
    return [pl.BlockSpec((v.shape[0], 128), lambda i, side=side: (0, side)) for side in range(2)]


def pack(c2d, k):
    shapes = [(2 * NS + 8, NV)] * 2 + [(NX * NS // 2 + NX, 128)] * 2
    return pl.pallas_call(
        pack_kernel,
        grid=(1,),
        out_shape=[jax.ShapeDtypeStruct(s, f32) for s in shapes],
        in_specs=halves(c2d) + [whole_block(k.shape)],
        out_specs=[whole_block(s) for s in shapes],
        compiler_params=pltpu.CompilerParams(vmem_limit_bytes=8 * 2**20),
        name="pack_faces",
    )(c2d, c2d, k)


def corner_kernel(xl_ref, xh_ref, lo_ref, hi_ref):
    for at, ref in ((0, xh_ref), (NS, xl_ref)):
        lo_ref[at : at + NS, :] = ref[0:NS, :128]
        hi_ref[at : at + NS, :] = ref[0:NS, 128:]


def corners(xl, xh):
    shapes = [(2 * NS, 128)] * 2
    return pl.pallas_call(
        corner_kernel,
        grid=(1,),
        out_shape=[jax.ShapeDtypeStruct(s, f32) for s in shapes],
        in_specs=[whole_block(v.shape) for v in (xl, xh)],
        out_specs=[whole_block(s) for s in shapes],
        compiler_params=pltpu.CompilerParams(vmem_limit_bytes=4 * 2**20),
        name="corner_columns",
    )(xl, xh)


def split_2(v):
    hi = v.astype(bf16)
    return hi, (v - hi.astype(f32)).astype(bf16)


def advance_kernel(c0_ref, c1_ref, k_ref, rate_ref, xl_ref, xh_ref, yl_ref, yh_ref, left, right, e0, e1, ke):
    half = NS // 2
    lane_s, lane_h = lanes(NS), lanes(half)
    z = lane_s % NZ
    not_first, not_last = z > 0, z < NZ - 1
    below, above = lane_s >= 32, lane_s < 96

    low_h = lane_h < 64
    e0[0, :, :NV] = xh_ref[NS : 2 * NS, :]
    e0[1, :, :NV] = xh_ref[0:NS, :]
    e0[NX + 2, :, :NV] = xl_ref[0:NS, :]
    e0[NX + 3, :, :NV] = xl_ref[NS : 2 * NS, :]
    for row in (0, 1, NX + 2, NX + 3):
        e0[row, :, NV:] = jnp.zeros((NS, NH), f32)
    for x in range(NX):
        after, before = yl_ref[x * half : (x + 1) * half, :], yh_ref[x * half : (x + 1) * half, :]
        e0[x + 2, :, :128] = c0_ref[pl.ds(x, NS, stride=NX), :]
        e0[x + 2, :, 128:NV] = c1_ref[pl.ds(x, NS, stride=NX), :]
        e0[x + 2, :half, NV:] = jnp.where(low_h, after, before)
        e0[x + 2, half:, NV:] = pltpu.roll(jnp.where(low_h, before, after), 64, 1)
    ke[8 : 8 + NX, :NV] = k_ref[...]
    ke[8 : 8 + NX, NV:] = jnp.where(lanes(NX) < 64, yl_ref[NX * half :, :], yh_ref[NX * half :, :])
    ke[0:8, :NV] = xh_ref[2 * NS :, :]
    ke[0:8, NV:] = jnp.zeros((8, NH), f32)
    ke[8 + NX :, :NV] = xl_ref[2 * NS :, :]
    ke[8 + NX :, NV:] = jnp.zeros((8, NH), f32)
    rate = jnp.broadcast_to(rate_ref[...], (NS, 128))

    def step(src, row, k_row, tiles):
        t = [src[row, :, i * 128 : (i + 1) * 128] for i in range(3)]
        up = [pltpu.roll(v, 96, 1) for v in t]
        down = [pltpu.roll(v, 32, 1) for v in t]
        out = []
        for i in range(tiles):
            cut = slice(i * 128, (i + 1) * 128)
            total = src[row - 1, :, cut] + src[row + 1, :, cut]
            total = total + jnp.where(above, up[i], up[(i + 1) % 3]) + jnp.where(below, down[i], down[(i + 2) % 3])
            total = total + jnp.where(not_first, pltpu.roll(t[i], 1, 1), 0.0)
            total = total + jnp.where(not_last, pltpu.roll(t[i], 127, 1), 0.0)
            lap = total - 6.0 * t[i]
            out.append(t[i] + (rate * k_row[:, cut]) * lap)
        return out

    def first_step(x, carry):
        for i, v in enumerate(step(e0, x + 1, ke[pl.ds(x + 7, 1), :], 3)):
            e1[x, :, i * 128 : (i + 1) * 128] = v
        return carry

    lax.fori_loop(0, NX + 2, first_step, 0, unroll=True)

    def second_step(x, carry):
        done = step(e1, x + 1, ke[pl.ds(x + 8, 1), :], 2)
        left[pl.ds(x, NS, stride=NX), :], right[pl.ds(x, NS, stride=NX), :] = done
        return carry

    lax.fori_loop(0, NX, second_step, 0, unroll=True)


def advance(c2d, k, rate, faces):
    small = (k, rate, *faces)
    return pl.pallas_call(
        advance_kernel,
        grid=(1,),
        out_shape=[jax.ShapeDtypeStruct((NS * NX, 128), f32)] * 2,
        in_specs=halves(c2d) + [whole_block(v.shape) for v in small],
        out_specs=[whole_block((NS * NX, 128))] * 2,
        scratch_shapes=[
            pltpu.VMEM((NX + 4, NS, NV + NH), f32),
            pltpu.VMEM((NX + 2, NS, NV + NH), f32),
            pltpu.VMEM((NX + 16, NV + NH), f32),
        ],
        compiler_params=pltpu.CompilerParams(vmem_limit_bytes=16 * 2**20),
        cost_estimate=pl.CostEstimate(flops=10000000000, bytes_accessed=4 * 2**20, transcendentals=0),
        name="advance_twice",
    )(c2d, c2d, *small)


def reduce_kernel(a0_ref, a1_ref, k_ref, rate_ref, kxl_ref, kxh_ref, kyl_ref, kyh_ref, cl_ref, ch_ref, fs_ref, fx_ref,
                  adv_ref, planes_ref, left, right):
    left[...], right[...] = a0_ref[...], a1_ref[...]
    rate = jnp.broadcast_to(rate_ref[...], (NS, 128))
    first_y, last_y = lanes(NS) < NZ, lanes(NS) >= 128 - NZ
    for x, at, kx_ref in ((0, 0, kxh_ref), (NX - 1, NS, kxl_ref)):
        cut = pl.ds(x, NS, stride=NX)
        for ref, own, corner_ref, ky_ref, turn, mask in (
            (left, slice(0, 128), ch_ref, kyh_ref, 32, first_y),
            (right, slice(128, 256), cl_ref, kyl_ref, 96, last_y),
        ):
            paths = kx_ref[0:1, own] + pltpu.roll(jnp.broadcast_to(ky_ref[x : x + 1, :], (8, 128)), turn, 1)[0:1, :]
            term = (rate * k_ref[x : x + 1, own]) * (rate * paths) * pltpu.roll(corner_ref[at : at + NS, :], turn, 1)
            ref[cut, :] = ref[cut, :] + jnp.where(mask, term, 0.0)
    adv_ref[:, :128] = left[...]
    adv_ref[:, 128:] = right[...]
    for z in range(NZ):
        planes_ref[(2 * z + 1) * NX : (2 * z + 2) * NX, :] = fx_ref[...]

    lane_q = lanes(NQ)
    low_q, even_q = lane_q < 64, (lane_q & 32) == 0
    fs_hi, fs_lo = split_2(fs_ref[...])
    weights = jnp.concatenate([fs_hi, fs_hi, fs_lo, fs_lo], axis=1)

    def four_rows(group, carry):
        rows = []
        for g in range(4):
            cut = pl.ds(group * 4 + g, NS, stride=NX)
            hi, lo = split_2(jnp.concatenate([left[cut, :], right[cut, :]], axis=1))
            stacked = jnp.concatenate([hi, lo, hi, lo], axis=0)
            rows.append(jnp.dot(weights, stacked, preferred_element_type=f32))
        swapped = []
        for t in range(2):
            v = [r[:, t * 128 : (t + 1) * 128] for r in rows]
            a = [jnp.where(low_q, v[g], pltpu.roll(v[g + 2], 64, 1)) for g in range(2)]
            b = [jnp.where(low_q, pltpu.roll(v[g], 64, 1), v[g + 2]) for g in range(2)]
            for p, r in (a, b):
                swapped.append(jnp.where(even_q, p, pltpu.roll(r, 32, 1)))
                swapped.append(jnp.where(even_q, pltpu.roll(p, 96, 1), r))
        turned = jnp.concatenate(swapped, axis=0).T
        for g in range(4):
            planes_ref[pl.ds(group * 4 + g, NZ, stride=2 * NX), :] = turned[g * NZ : (g + 1) * NZ, :]
        return carry

    lax.fori_loop(0, NX // 4, four_rows, 0, unroll=True)


def reduce_species(sides, k, rate, faces, corner, fs, factor_x):
    xl, xh, yl, yh = faces
    tail_x, tail_y = pl.BlockSpec((8, NV), lambda i: (2 * NS // 8, 0)), pl.BlockSpec((NX, 128), lambda i: (NS // 2, 0))
    shapes = [(NS * NX, NV), (NZ * 2 * NX, 128)]
    return pl.pallas_call(
        reduce_kernel,
        grid=(1,),
        out_shape=[jax.ShapeDtypeStruct(s, f32) for s in shapes],
        in_specs=[whole_block(v.shape) for v in (*sides, k, rate)]
        + [tail_x, tail_x, tail_y, tail_y]
        + [whole_block(v.shape) for v in (*corner, fs, factor_x)],
        out_specs=[whole_block(s) for s in shapes],
        scratch_shapes=[pltpu.VMEM((NS * NX, 128), f32)] * 2,
        compiler_params=pltpu.CompilerParams(vmem_limit_bytes=12 * 2**20),
        name="reduce_species",
    )(*sides, k, rate, xl, xh, yl, yh, *corner, fs, factor_x)


def shift_to(v, dx, dy):
    axis, step = ("tx", dx) if dx else ("ty", dy)
    count = lax.axis_size(axis)
    return lax.ppermute(v, axis, [(i, i + step) for i in range(count) if 0 <= i + step < count])


def body(species, cell_factor, species_rate, factor_x, factor_y, factor_species):
    nspec, cells_x, merged = species.shape
    cells_y = factor_y.shape[0]
    depth = merged // cells_y
    n_tx, n_ty = lax.axis_size("tx"), lax.axis_size("ty")
    ranks_q = factor_species.shape[1]
    c2d = species.reshape(nspec * cells_x, merged)
    faces = pack(c2d, cell_factor)
    xl, xh, yl, yh = (shift_to(v, dx, dy) for v, (dx, dy) in zip(faces, [(-1, 0), (1, 0), (0, -1), (0, 1)]))
    lo, hi = corners(xl, xh)
    corner = shift_to(lo, 0, -1), shift_to(hi, 0, 1)
    faces, rate = (xl, xh, yl, yh), species_rate[:, None]
    sides = advance(c2d, cell_factor, rate, faces)
    advanced, planes = reduce_species(sides, cell_factor, rate, faces, corner, factor_species.T, factor_x)
    planes = planes.reshape(depth, 2 * cells_x, cells_y * ranks_q)
    planes = lax.all_to_all(planes, "tx", 0, 0, tiled=True)
    first = lax.dot_general(
        planes[:, :cells_x], planes[:, cells_x:], (((0, 1), (0, 1)), ((), ())), precision=exact_mode
    )
    first = first.reshape(cells_y, ranks_q, -1).transpose(1, 0, 2)
    sent = jnp.concatenate([first, jnp.broadcast_to(factor_y[None], (n_ty,) + factor_y.shape)], axis=1)
    came = lax.all_to_all(sent, "ty", 0, 0, tiled=True)
    first = came[:, :cells_y].reshape(n_ty * cells_y, -1)
    whole_y = came[:, cells_y:].reshape(n_ty * cells_y, -1)
    plane = lax.dot_general(first, whole_y, (((0,), (0,)), ((), ())), precision=exact_mode)
    rank_a, rank_b = plane.shape
    plane = plane.reshape(n_tx, rank_a // n_tx, n_ty, rank_b // n_ty).transpose(0, 2, 1, 3)
    plane = plane.reshape(n_tx * n_ty, 1, -1)
    core = lax.all_to_all(plane, ("tx", "ty"), 0, 0, tiled=True)
    core = core.reshape(depth, ranks_q, rank_a // n_tx, rank_b // n_ty).transpose(2, 1, 3, 0)
    return advanced.reshape(species.shape), core.reshape(rank_a // n_tx, ranks_q, -1)


def solution(mesh):
    in_specs = (P(None, "tx", "ty"), P("tx", "ty"), P(), P("tx", None), P("ty", None), P())
    out_specs = (P(None, "tx", "ty"), P("tx", None, "ty"))
    return jax.shard_map(body, mesh=mesh, in_specs=in_specs, out_specs=out_specs, check_vma=False)
```

```python
import jax
import jax.numpy as jnp
from jax import lax
from jax.experimental import pallas as pl
from jax.experimental.pallas import tpu as pltpu
from jax.sharding import PartitionSpec as P

exact_mode = lax.Precision.HIGHEST
f32, bf16 = jnp.float32, jnp.bfloat16
SENT = 48
NS, NX, NV, NH, NZ, NQ = 32, 32, 256, 128, 32, 16


def lanes(rows):
    return lax.broadcasted_iota(jnp.int32, (rows, 128), 1)


def pack_kernel(c0_ref, c1_ref, k_ref, xl_ref, xh_ref, yl_ref, yh_ref):
    low = lanes(NS // 2) < 64

    def row(x):
        return [r[pl.ds(x, NS, stride=NX), :] for r in (c0_ref, c1_ref)]

    for ref, at, x in ((xl_ref, 0, 0), (xl_ref, NS, 1), (xh_ref, 0, NX - 1), (xh_ref, NS, NX - 2)):
        ref[at : at + NS, :128], ref[at : at + NS, 128:] = row(x)
    xl_ref[2 * NS :, :] = jnp.broadcast_to(k_ref[0:1, :], (8, NV))
    xh_ref[2 * NS :, :] = jnp.broadcast_to(k_ref[NX - 1 : NX, :], (8, NV))
    half = NS // 2
    for x in range(NX):
        t0, t1 = row(x)
        yl_ref[x * half : (x + 1) * half, :] = jnp.where(low, t0[:half], pltpu.roll(t0[half:], 64, 1))
        yh_ref[x * half : (x + 1) * half, :] = jnp.where(low, pltpu.roll(t1[half:], 64, 1), t1[:half])
    yl_ref[NX * half :, :] = k_ref[:, :128]
    yh_ref[NX * half :, :] = k_ref[:, 128:]


def whole_block(shape):
    return pl.BlockSpec(shape, lambda i: (0,) * len(shape))


def halves(v):
    return [pl.BlockSpec((v.shape[0], 128), lambda i, side=side: (0, side)) for side in range(2)]


def pack(c2d, k):
    shapes = [(2 * NS + 8, NV)] * 2 + [(NX * NS // 2 + NX, 128)] * 2
    return pl.pallas_call(
        pack_kernel,
        grid=(1,),
        out_shape=[jax.ShapeDtypeStruct(s, f32) for s in shapes],
        in_specs=halves(c2d) + [whole_block(k.shape)],
        out_specs=[whole_block(s) for s in shapes],
        compiler_params=pltpu.CompilerParams(vmem_limit_bytes=8 * 2**20),
        name="pack_faces",
    )(c2d, c2d, k)


def corner_kernel(xl_ref, xh_ref, lo_ref, hi_ref):
    for at, ref in ((0, xh_ref), (NS, xl_ref)):
        lo_ref[at : at + NS, :] = ref[0:NS, :128]
        hi_ref[at : at + NS, :] = ref[0:NS, 128:]


def corners(xl, xh):
    shapes = [(2 * NS, 128)] * 2
    return pl.pallas_call(
        corner_kernel,
        grid=(1,),
        out_shape=[jax.ShapeDtypeStruct(s, f32) for s in shapes],
        in_specs=[whole_block(v.shape) for v in (xl, xh)],
        out_specs=[whole_block(s) for s in shapes],
        compiler_params=pltpu.CompilerParams(vmem_limit_bytes=4 * 2**20),
        name="corner_columns",
    )(xl, xh)


def split_2(v):
    hi = v.astype(bf16)
    return hi, (v - hi.astype(f32)).astype(bf16)


def advance_kernel(c0_ref, c1_ref, k_ref, rate_ref, xl_ref, xh_ref, yl_ref, yh_ref, left, right, e0, e1, ke):
    half = NS // 2
    lane_s, lane_h = lanes(NS), lanes(half)
    z = lane_s % NZ
    not_first, not_last = z > 0, z < NZ - 1
    below, above = lane_s >= 32, lane_s < 96

    low_h = lane_h < 64
    e0[0, :, :NV] = xh_ref[NS : 2 * NS, :]
    e0[1, :, :NV] = xh_ref[0:NS, :]
    e0[NX + 2, :, :NV] = xl_ref[0:NS, :]
    e0[NX + 3, :, :NV] = xl_ref[NS : 2 * NS, :]
    for row in (0, 1, NX + 2, NX + 3):
        e0[row, :, NV:] = jnp.zeros((NS, NH), f32)
    for x in range(NX):
        after, before = yl_ref[x * half : (x + 1) * half, :], yh_ref[x * half : (x + 1) * half, :]
        e0[x + 2, :, :128] = c0_ref[pl.ds(x, NS, stride=NX), :]
        e0[x + 2, :, 128:NV] = c1_ref[pl.ds(x, NS, stride=NX), :]
        e0[x + 2, :half, NV:] = jnp.where(low_h, after, before)
        e0[x + 2, half:, NV:] = pltpu.roll(jnp.where(low_h, before, after), 64, 1)
    ke[8 : 8 + NX, :NV] = k_ref[...]
    ke[8 : 8 + NX, NV:] = jnp.where(lanes(NX) < 64, yl_ref[NX * half :, :], yh_ref[NX * half :, :])
    ke[0:8, :NV] = xh_ref[2 * NS :, :]
    ke[0:8, NV:] = jnp.zeros((8, NH), f32)
    ke[8 + NX :, :NV] = xl_ref[2 * NS :, :]
    ke[8 + NX :, NV:] = jnp.zeros((8, NH), f32)
    rate = jnp.broadcast_to(rate_ref[...], (NS, 128))

    def step(src, row, k_row, tiles):
        t = [src[row, :, i * 128 : (i + 1) * 128] for i in range(3)]
        up = [pltpu.roll(v, 96, 1) for v in t]
        down = [pltpu.roll(v, 32, 1) for v in t]
        out = []
        for i in range(tiles):
            cut = slice(i * 128, (i + 1) * 128)
            total = src[row - 1, :, cut] + src[row + 1, :, cut]
            total = total + jnp.where(above, up[i], up[(i + 1) % 3]) + jnp.where(below, down[i], down[(i + 2) % 3])
            total = total + jnp.where(not_first, pltpu.roll(t[i], 1, 1), 0.0)
            total = total + jnp.where(not_last, pltpu.roll(t[i], 127, 1), 0.0)
            lap = total - 6.0 * t[i]
            out.append(t[i] + (rate * k_row[:, cut]) * lap)
        return out

    def first_step(x, carry):
        for i, v in enumerate(step(e0, x + 1, ke[pl.ds(x + 7, 1), :], 3)):
            e1[x, :, i * 128 : (i + 1) * 128] = v
        return carry

    lax.fori_loop(0, NX + 2, first_step, 0, unroll=True)

    def second_step(x, carry):
        done = step(e1, x + 1, ke[pl.ds(x + 8, 1), :], 2)
        left[pl.ds(x, NS, stride=NX), :], right[pl.ds(x, NS, stride=NX), :] = done
        return carry

    lax.fori_loop(0, NX, second_step, 0, unroll=True)


def advance(c2d, k, rate, faces):
    small = (k, rate, *faces)
    return pl.pallas_call(
        advance_kernel,
        grid=(1,),
        out_shape=[jax.ShapeDtypeStruct((NS * NX, 128), f32)] * 2,
        in_specs=halves(c2d) + [whole_block(v.shape) for v in small],
        out_specs=[whole_block((NS * NX, 128))] * 2,
        scratch_shapes=[
            pltpu.VMEM((NX + 4, NS, NV + NH), f32),
            pltpu.VMEM((NX + 2, NS, NV + NH), f32),
            pltpu.VMEM((NX + 16, NV + NH), f32),
        ],
        compiler_params=pltpu.CompilerParams(vmem_limit_bytes=16 * 2**20),
        cost_estimate=pl.CostEstimate(flops=10000000000, bytes_accessed=4 * 2**20, transcendentals=0),
        name="advance_twice",
    )(c2d, c2d, *small)


def reduce_kernel(a0_ref, a1_ref, k_ref, rate_ref, kxl_ref, kxh_ref, kyl_ref, kyh_ref, cl_ref, ch_ref, fs_ref, fx_ref,
                  adv_ref, planes_ref, left, right):
    left[...], right[...] = a0_ref[...], a1_ref[...]
    rate = jnp.broadcast_to(rate_ref[...], (NS, 128))
    first_y, last_y = lanes(NS) < NZ, lanes(NS) >= 128 - NZ
    for x, at, kx_ref in ((0, 0, kxh_ref), (NX - 1, NS, kxl_ref)):
        cut = pl.ds(x, NS, stride=NX)
        for ref, own, corner_ref, ky_ref, turn, mask in (
            (left, slice(0, 128), ch_ref, kyh_ref, 32, first_y),
            (right, slice(128, 256), cl_ref, kyl_ref, 96, last_y),
        ):
            paths = kx_ref[0:1, own] + pltpu.roll(jnp.broadcast_to(ky_ref[x : x + 1, :], (8, 128)), turn, 1)[0:1, :]
            term = (rate * k_ref[x : x + 1, own]) * (rate * paths) * pltpu.roll(corner_ref[at : at + NS, :], turn, 1)
            ref[cut, :] = ref[cut, :] + jnp.where(mask, term, 0.0)
    adv_ref[:, :128] = left[...]
    adv_ref[:, 128:] = right[...]
    for to in range(NZ):
        side = to % 2
        planes_ref[to * SENT + NX : (to + 1) * SENT, :] = fx_ref[side * (NX // 2) : (side + 1) * (NX // 2), :]

    lane_q = lanes(NQ)
    low_q, even_q = lane_q < 64, (lane_q & 32) == 0
    fs_hi, fs_lo = split_2(fs_ref[...])
    weights = jnp.concatenate([fs_hi, fs_hi, fs_lo, fs_lo], axis=1)

    for group in range(NX // 4):
        rows = []
        for g in range(4):
            cut = pl.ds(group * 4 + g, NS, stride=NX)
            hi, lo = split_2(jnp.concatenate([left[cut, :], right[cut, :]], axis=1))
            stacked = jnp.concatenate([hi, lo, hi, lo], axis=0)
            rows.append(jnp.dot(weights, stacked, preferred_element_type=f32))
        swapped = []
        for t in range(2):
            v = [r[:, t * 128 : (t + 1) * 128] for r in rows]
            a = [jnp.where(low_q, v[g], pltpu.roll(v[g + 2], 64, 1)) for g in range(2)]
            b = [jnp.where(low_q, pltpu.roll(v[g], 64, 1), v[g + 2]) for g in range(2)]
            for p, r in (a, b):
                swapped.append(jnp.where(even_q, p, pltpu.roll(r, 32, 1)))
                swapped.append(jnp.where(even_q, pltpu.roll(p, 96, 1), r))
        turned = jnp.concatenate(swapped, axis=0).T
        for g in range(4):
            side, x = divmod(group * 4 + g, NX // 2)
            for e in range(2):
                to = pl.ds(side * SENT + e * (NX // 2) + x, NZ // 2, stride=2 * SENT)
                planes_ref[to, :] = turned[g * NZ + e * (NZ // 2) : g * NZ + (e + 1) * (NZ // 2), :]


def reduce_species(sides, k, rate, faces, corner, fs, factor_x):
    xl, xh, yl, yh = faces
    tail_x, tail_y = pl.BlockSpec((8, NV), lambda i: (2 * NS // 8, 0)), pl.BlockSpec((NX, 128), lambda i: (NS // 2, 0))
    shapes = [(NS * NX, NV), (NZ * SENT, 128)]
    return pl.pallas_call(
        reduce_kernel,
        grid=(1,),
        out_shape=[jax.ShapeDtypeStruct(s, f32) for s in shapes],
        in_specs=[whole_block(v.shape) for v in (*sides, k, rate)]
        + [tail_x, tail_x, tail_y, tail_y]
        + [whole_block(v.shape) for v in (*corner, fs, factor_x)],
        out_specs=[whole_block(s) for s in shapes],
        scratch_shapes=[pltpu.VMEM((NS * NX, 128), f32)] * 2,
        compiler_params=pltpu.CompilerParams(vmem_limit_bytes=12 * 2**20),
        name="reduce_species",
    )(*sides, k, rate, xl, xh, yl, yh, *corner, fs, factor_x)


def shift_to(v, dx, dy):
    axis, step = ("tx", dx) if dx else ("ty", dy)
    count = lax.axis_size(axis)
    return lax.ppermute(v, axis, [(i, i + step) for i in range(count) if 0 <= i + step < count])


def body(species, cell_factor, species_rate, factor_x, factor_y, factor_species):
    nspec, cells_x, merged = species.shape
    cells_y = factor_y.shape[0]
    depth = merged // cells_y
    n_tx, n_ty = lax.axis_size("tx"), lax.axis_size("ty")
    ranks_q = factor_species.shape[1]
    c2d = species.reshape(nspec * cells_x, merged)
    faces = pack(c2d, cell_factor)
    xl, xh, yl, yh = (shift_to(v, dx, dy) for v, (dx, dy) in zip(faces, [(-1, 0), (1, 0), (0, -1), (0, 1)]))
    lo, hi = corners(xl, xh)
    corner = shift_to(lo, 0, -1), shift_to(hi, 0, 1)
    faces, rate = (xl, xh, yl, yh), species_rate[:, None]
    sides = advance(c2d, cell_factor, rate, faces)
    advanced, planes = reduce_species(sides, cell_factor, rate, faces, corner, factor_species.T, factor_x)
    planes = planes.reshape(n_tx, SENT, cells_y * ranks_q)
    planes = lax.all_to_all(planes, "tx", 0, 0, tiled=True)
    side, half = lax.axis_index("tx") % 2, cells_x // 2

    def over_x(which):
        plane = lax.dynamic_slice_in_dim(planes, which * half, half, axis=1)
        return lax.dot_general(plane, planes[:, cells_x:], (((0, 1), (0, 1)), ((), ())), precision=exact_mode)

    came = lax.ppermute(over_x(1 - side), "tx", [(i, i ^ 1) for i in range(n_tx)])
    first = over_x(side) + came
    first = first.reshape(cells_y, ranks_q, -1).transpose(1, 0, 2)
    sent = jnp.concatenate([first, jnp.broadcast_to(factor_y[None], (n_ty,) + factor_y.shape)], axis=1)
    came = lax.all_to_all(sent, "ty", 0, 0, tiled=True)
    first = came[:, :cells_y].reshape(n_ty * cells_y, -1)
    whole_y = came[:, cells_y:].reshape(n_ty * cells_y, -1)
    plane = lax.dot_general(first, whole_y, (((0,), (0,)), ((), ())), precision=exact_mode)
    rank_a, rank_b = plane.shape
    plane = plane.reshape(n_tx, rank_a // n_tx, n_ty, rank_b // n_ty).transpose(0, 2, 1, 3)
    plane = plane.reshape(n_tx * n_ty, 1, -1)
    core = lax.all_to_all(plane, ("tx", "ty"), 0, 0, tiled=True)
    core = core.reshape(depth // 2, 2, ranks_q, rank_a // n_tx, rank_b // n_ty).transpose(3, 2, 4, 1, 0)
    return advanced.reshape(species.shape), core.reshape(rank_a // n_tx, ranks_q, -1)


def solution(mesh):
    in_specs = (P(None, "tx", "ty"), P("tx", "ty"), P(), P("tx", None), P("ty", None), P())
    out_specs = (P(None, "tx", "ty"), P("tx", None, "ty"))
    return jax.shard_map(body, mesh=mesh, in_specs=in_specs, out_specs=out_specs, check_vma=False)
```

```python
import jax
import jax.numpy as jnp
from jax import lax
from jax.experimental import pallas as pl
from jax.experimental.pallas import tpu as pltpu
from jax.sharding import PartitionSpec as P

exact_mode = lax.Precision.HIGHEST
f32, bf16 = jnp.float32, jnp.bfloat16
NS, NX, NV, NH, NZ, NQ = 32, 32, 256, 128, 32, 16


def lanes(rows):
    return lax.broadcasted_iota(jnp.int32, (rows, 128), 1)


def pack_kernel(c0_ref, c1_ref, k_ref, xl_ref, xh_ref, yl_ref, yh_ref):
    low = lanes(NS // 2) < 64

    def row(x):
        return [r[pl.ds(x, NS, stride=NX), :] for r in (c0_ref, c1_ref)]

    for ref, at, x in ((xl_ref, 0, 0), (xl_ref, NS, 1), (xh_ref, 0, NX - 1), (xh_ref, NS, NX - 2)):
        ref[at : at + NS, :128], ref[at : at + NS, 128:] = row(x)
    xl_ref[2 * NS :, :] = jnp.broadcast_to(k_ref[0:1, :], (8, NV))
    xh_ref[2 * NS :, :] = jnp.broadcast_to(k_ref[NX - 1 : NX, :], (8, NV))
    half = NS // 2
    for x in range(NX):
        t0, t1 = row(x)
        yl_ref[x * half : (x + 1) * half, :] = jnp.where(low, t0[:half], pltpu.roll(t0[half:], 64, 1))
        yh_ref[x * half : (x + 1) * half, :] = jnp.where(low, pltpu.roll(t1[half:], 64, 1), t1[:half])
    yl_ref[NX * half :, :] = k_ref[:, :128]
    yh_ref[NX * half :, :] = k_ref[:, 128:]


def whole_block(shape):
    return pl.BlockSpec(shape, lambda i: (0,) * len(shape))


def halves(v):
    return [pl.BlockSpec((v.shape[0], 128), lambda i, side=side: (0, side)) for side in range(2)]


def pack(c2d, k):
    shapes = [(2 * NS + 8, NV)] * 2 + [(NX * NS // 2 + NX, 128)] * 2
    return pl.pallas_call(
        pack_kernel,
        grid=(1,),
        out_shape=[jax.ShapeDtypeStruct(s, f32) for s in shapes],
        in_specs=halves(c2d) + [whole_block(k.shape)],
        out_specs=[whole_block(s) for s in shapes],
        compiler_params=pltpu.CompilerParams(vmem_limit_bytes=8 * 2**20),
        name="pack_faces",
    )(c2d, c2d, k)


def turned(v, shift):
    return pltpu.roll(v, shift % 128, 1) if shift % 128 else v


def corner_kernel(xl_ref, xh_ref, lo_ref, hi_ref):
    group = lanes(NS // 2) // NZ
    for out_ref, side, at in ((lo_ref, 0, 0), (hi_ref, 128, 128 - NZ)):
        packed = None
        for g in range(4):
            ref, row = (xh_ref, xl_ref)[g // 2], (g % 2) * (NS // 2)
            part = turned(ref[row : row + NS // 2, side : side + 128], g * NZ - at)
            packed = part if packed is None else jnp.where(group == g, part, packed)
        out_ref[...] = packed


def corners(xl, xh):
    shapes = [(NS // 2, 128)] * 2
    return pl.pallas_call(
        corner_kernel,
        grid=(1,),
        out_shape=[jax.ShapeDtypeStruct(s, f32) for s in shapes],
        in_specs=[whole_block(v.shape) for v in (xl, xh)],
        out_specs=[whole_block(s) for s in shapes],
        compiler_params=pltpu.CompilerParams(vmem_limit_bytes=4 * 2**20),
        name="corner_columns",
    )(xl, xh)


def split_2(v):
    hi = v.astype(bf16)
    return hi, (v - hi.astype(f32)).astype(bf16)


def advance_kernel(c0_ref, c1_ref, k_ref, rate_ref, xl_ref, xh_ref, yl_ref, yh_ref, left, right, e0, e1, ke):
    half = NS // 2
    lane_s, lane_h = lanes(NS), lanes(half)
    z = lane_s % NZ
    not_first, not_last = z > 0, z < NZ - 1
    below, above = lane_s >= 32, lane_s < 96

    low_h = lane_h < 64
    e0[0, :, :NV] = xh_ref[NS : 2 * NS, :]
    e0[1, :, :NV] = xh_ref[0:NS, :]
    e0[NX + 2, :, :NV] = xl_ref[0:NS, :]
    e0[NX + 3, :, :NV] = xl_ref[NS : 2 * NS, :]
    for row in (0, 1, NX + 2, NX + 3):
        e0[row, :, NV:] = jnp.zeros((NS, NH), f32)
    for x in range(NX):
        after, before = yl_ref[x * half : (x + 1) * half, :], yh_ref[x * half : (x + 1) * half, :]
        e0[x + 2, :, :128] = c0_ref[pl.ds(x, NS, stride=NX), :]
        e0[x + 2, :, 128:NV] = c1_ref[pl.ds(x, NS, stride=NX), :]
        e0[x + 2, :half, NV:] = jnp.where(low_h, after, before)
        e0[x + 2, half:, NV:] = pltpu.roll(jnp.where(low_h, before, after), 64, 1)
    ke[8 : 8 + NX, :NV] = k_ref[...]
    ke[8 : 8 + NX, NV:] = jnp.where(lanes(NX) < 64, yl_ref[NX * half :, :], yh_ref[NX * half :, :])
    ke[0:8, :NV] = xh_ref[2 * NS :, :]
    ke[0:8, NV:] = jnp.zeros((8, NH), f32)
    ke[8 + NX :, :NV] = xl_ref[2 * NS :, :]
    ke[8 + NX :, NV:] = jnp.zeros((8, NH), f32)
    rate = jnp.broadcast_to(rate_ref[...], (NS, 128))

    def step(src, row, k_row, tiles):
        t = [src[row, :, i * 128 : (i + 1) * 128] for i in range(3)]
        up = [pltpu.roll(v, 96, 1) for v in t]
        down = [pltpu.roll(v, 32, 1) for v in t]
        out = []
        for i in range(tiles):
            cut = slice(i * 128, (i + 1) * 128)
            total = src[row - 1, :, cut] + src[row + 1, :, cut]
            total = total + jnp.where(above, up[i], up[(i + 1) % 3]) + jnp.where(below, down[i], down[(i + 2) % 3])
            total = total + jnp.where(not_first, pltpu.roll(t[i], 1, 1), 0.0)
            total = total + jnp.where(not_last, pltpu.roll(t[i], 127, 1), 0.0)
            lap = total - 6.0 * t[i]
            out.append(t[i] + (rate * k_row[:, cut]) * lap)
        return out

    def first_step(x, carry):
        for i, v in enumerate(step(e0, x + 1, ke[pl.ds(x + 7, 1), :], 3)):
            e1[x, :, i * 128 : (i + 1) * 128] = v
        return carry

    lax.fori_loop(0, NX + 2, first_step, 0, unroll=True)

    def second_step(x, carry):
        done = step(e1, x + 1, ke[pl.ds(x + 8, 1), :], 2)
        left[pl.ds(x, NS, stride=NX), :], right[pl.ds(x, NS, stride=NX), :] = done
        return carry

    lax.fori_loop(0, NX, second_step, 0, unroll=True)


def advance(c2d, k, rate, faces):
    small = (k, rate, *faces)
    return pl.pallas_call(
        advance_kernel,
        grid=(1,),
        out_shape=[jax.ShapeDtypeStruct((NS * NX, 128), f32)] * 2,
        in_specs=halves(c2d) + [whole_block(v.shape) for v in small],
        out_specs=[whole_block((NS * NX, 128))] * 2,
        scratch_shapes=[
            pltpu.VMEM((NX + 4, NS, NV + NH), f32),
            pltpu.VMEM((NX + 2, NS, NV + NH), f32),
            pltpu.VMEM((NX + 16, NV + NH), f32),
        ],
        compiler_params=pltpu.CompilerParams(vmem_limit_bytes=16 * 2**20),
        cost_estimate=pl.CostEstimate(flops=10000000000, bytes_accessed=4 * 2**20, transcendentals=0),
        name="advance_twice",
    )(c2d, c2d, *small)


def reduce_kernel(a0_ref, a1_ref, k_ref, rate_ref, kxl_ref, kxh_ref, kyl_ref, kyh_ref, cl_ref, ch_ref, fs_ref, fx_ref,
                  adv_ref, planes_ref, left, right):
    left[...], right[...] = a0_ref[...], a1_ref[...]
    rate = jnp.broadcast_to(rate_ref[...], (NS, 128))
    first_y, last_y = lanes(NS) < NZ, lanes(NS) >= 128 - NZ
    for x, at, kx_ref in ((0, 0, kxh_ref), (NX - 1, 2, kxl_ref)):
        cut = pl.ds(x, NS, stride=NX)
        for ref, own, corner_ref, ky_ref, turn, mask in (
            (left, slice(0, 128), ch_ref, kyh_ref, 32, first_y),
            (right, slice(128, 256), cl_ref, kyl_ref, 96, last_y),
        ):
            paths = kx_ref[0:1, own] + pltpu.roll(jnp.broadcast_to(ky_ref[x : x + 1, :], (8, 128)), turn, 1)[0:1, :]
            to = 0 if turn == NZ else 128 - NZ
            corner = jnp.concatenate([turned(corner_ref[...], to - (at + g) * NZ) for g in range(2)], axis=0)
            term = (rate * k_ref[x : x + 1, own]) * (rate * paths) * corner
            ref[cut, :] = ref[cut, :] + jnp.where(mask, term, 0.0)
    adv_ref[:, :128] = left[...]
    adv_ref[:, 128:] = right[...]
    for z in range(NZ):
        planes_ref[(2 * z + 1) * NX : (2 * z + 2) * NX, :] = fx_ref[...]

    lane_q = lanes(NQ)
    low_q, even_q = lane_q < 64, (lane_q & 32) == 0
    fs_hi, fs_lo = split_2(fs_ref[...])
    weights = jnp.concatenate([fs_hi, fs_hi, fs_lo, fs_lo], axis=1)

    def four_rows(group, carry):
        rows = []
        for g in range(4):
            cut = pl.ds(group * 4 + g, NS, stride=NX)
            hi, lo = split_2(jnp.concatenate([left[cut, :], right[cut, :]], axis=1))
            stacked = jnp.concatenate([hi, lo, hi, lo], axis=0)
            rows.append(jnp.dot(weights, stacked, preferred_element_type=f32))
        swapped = []
        for t in range(2):
            v = [r[:, t * 128 : (t + 1) * 128] for r in rows]
            a = [jnp.where(low_q, v[g], pltpu.roll(v[g + 2], 64, 1)) for g in range(2)]
            b = [jnp.where(low_q, pltpu.roll(v[g], 64, 1), v[g + 2]) for g in range(2)]
            for p, r in (a, b):
                swapped.append(jnp.where(even_q, p, pltpu.roll(r, 32, 1)))
                swapped.append(jnp.where(even_q, pltpu.roll(p, 96, 1), r))
        flipped = jnp.concatenate(swapped, axis=0).T
        for g in range(4):
            planes_ref[pl.ds(group * 4 + g, NZ, stride=2 * NX), :] = flipped[g * NZ : (g + 1) * NZ, :]
        return carry

    lax.fori_loop(0, NX // 4, four_rows, 0, unroll=True)


def reduce_species(sides, k, rate, faces, corner, fs, factor_x):
    xl, xh, yl, yh = faces
    tail_x, tail_y = pl.BlockSpec((8, NV), lambda i: (2 * NS // 8, 0)), pl.BlockSpec((NX, 128), lambda i: (NS // 2, 0))
    shapes = [(NS * NX, NV), (NZ * 2 * NX, 128)]
    return pl.pallas_call(
        reduce_kernel,
        grid=(1,),
        out_shape=[jax.ShapeDtypeStruct(s, f32) for s in shapes],
        in_specs=[whole_block(v.shape) for v in (*sides, k, rate)]
        + [tail_x, tail_x, tail_y, tail_y]
        + [whole_block(v.shape) for v in (*corner, fs, factor_x)],
        out_specs=[whole_block(s) for s in shapes],
        scratch_shapes=[pltpu.VMEM((NS * NX, 128), f32)] * 2,
        compiler_params=pltpu.CompilerParams(vmem_limit_bytes=12 * 2**20),
        name="reduce_species",
    )(*sides, k, rate, xl, xh, yl, yh, *corner, fs, factor_x)


def shift_to(v, dx, dy):
    axis, step = ("tx", dx) if dx else ("ty", dy)
    count = lax.axis_size(axis)
    return lax.ppermute(v, axis, [(i, i + step) for i in range(count) if 0 <= i + step < count])


def body(species, cell_factor, species_rate, factor_x, factor_y, factor_species):
    nspec, cells_x, merged = species.shape
    cells_y = factor_y.shape[0]
    depth = merged // cells_y
    n_tx, n_ty = lax.axis_size("tx"), lax.axis_size("ty")
    ranks_q = factor_species.shape[1]
    c2d = species.reshape(nspec * cells_x, merged)
    faces = pack(c2d, cell_factor)
    xl, xh, yl, yh = (shift_to(v, dx, dy) for v, (dx, dy) in zip(faces, [(-1, 0), (1, 0), (0, -1), (0, 1)]))
    lo, hi = corners(xl, xh)
    corner = shift_to(lo, 0, -1), shift_to(hi, 0, 1)
    faces, rate = (xl, xh, yl, yh), species_rate[:, None]
    sides = advance(c2d, cell_factor, rate, faces)
    advanced, planes = reduce_species(sides, cell_factor, rate, faces, corner, factor_species.T, factor_x)
    planes = planes.reshape(depth, 2 * cells_x, cells_y * ranks_q)
    planes = lax.all_to_all(planes, "tx", 0, 0, tiled=True)
    first = lax.dot_general(
        planes[:, :cells_x], planes[:, cells_x:], (((0, 1), (0, 1)), ((), ())), precision=exact_mode
    )
    first = first.reshape(cells_y, ranks_q, -1).transpose(1, 0, 2)
    sent = jnp.concatenate([first, jnp.broadcast_to(factor_y[None], (n_ty,) + factor_y.shape)], axis=1)
    came = lax.all_to_all(sent, "ty", 0, 0, tiled=True)
    first = came[:, :cells_y].reshape(n_ty * cells_y, -1)
    whole_y = came[:, cells_y:].reshape(n_ty * cells_y, -1)
    plane = lax.dot_general(first, whole_y, (((0,), (0,)), ((), ())), precision=exact_mode)
    rank_a, rank_b = plane.shape
    plane = plane.reshape(n_tx, rank_a // n_tx, n_ty, rank_b // n_ty).transpose(0, 2, 1, 3)
    plane = plane.reshape(n_tx * n_ty, 1, -1)
    core = lax.all_to_all(plane, ("tx", "ty"), 0, 0, tiled=True)
    core = core.reshape(depth, ranks_q, rank_a // n_tx, rank_b // n_ty).transpose(2, 1, 3, 0)
    return advanced.reshape(species.shape), core.reshape(rank_a // n_tx, ranks_q, -1)


def solution(mesh):
    in_specs = (P(None, "tx", "ty"), P("tx", "ty"), P(), P("tx", None), P("ty", None), P())
    out_specs = (P(None, "tx", "ty"), P("tx", None, "ty"))
    return jax.shard_map(body, mesh=mesh, in_specs=in_specs, out_specs=out_specs, check_vma=False)
```

```python
import jax
import jax.numpy as jnp
from jax import lax
from jax.experimental import pallas as pl
from jax.experimental.pallas import tpu as pltpu
from jax.sharding import PartitionSpec as P

exact_mode = lax.Precision.HIGHEST
f32, bf16 = jnp.float32, jnp.bfloat16
NS, NX, NV, NH, NZ, NQ = 32, 32, 256, 128, 32, 16


def lanes(rows):
    return lax.broadcasted_iota(jnp.int32, (rows, 128), 1)


def pack_kernel(c0_ref, c1_ref, k_ref, xl_ref, xh_ref, yl_ref, yh_ref):
    low = lanes(NS // 2) < 64

    def row(x):
        return [r[pl.ds(x, NS, stride=NX), :] for r in (c0_ref, c1_ref)]

    for ref, at, x in ((xl_ref, 0, 0), (xl_ref, NS, 1), (xh_ref, 0, NX - 1), (xh_ref, NS, NX - 2)):
        ref[at : at + NS, :128], ref[at : at + NS, 128:] = row(x)
    xl_ref[2 * NS :, :] = jnp.broadcast_to(k_ref[0:1, :], (8, NV))
    xh_ref[2 * NS :, :] = jnp.broadcast_to(k_ref[NX - 1 : NX, :], (8, NV))
    half = NS // 2
    for x in range(NX):
        t0, t1 = row(x)
        yl_ref[x * half : (x + 1) * half, :] = jnp.where(low, t0[:half], pltpu.roll(t0[half:], 64, 1))
        yh_ref[x * half : (x + 1) * half, :] = jnp.where(low, pltpu.roll(t1[half:], 64, 1), t1[:half])
    yl_ref[NX * half :, :] = k_ref[:, :128]
    yh_ref[NX * half :, :] = k_ref[:, 128:]


def whole_block(shape):
    return pl.BlockSpec(shape, lambda i: (0,) * len(shape))


def halves(v):
    return [pl.BlockSpec((v.shape[0], 128), lambda i, side=side: (0, side)) for side in range(2)]


def pack(c2d, k):
    shapes = [(2 * NS + 8, NV)] * 2 + [(NX * NS // 2 + NX, 128)] * 2
    return pl.pallas_call(
        pack_kernel,
        grid=(1,),
        out_shape=[jax.ShapeDtypeStruct(s, f32) for s in shapes],
        in_specs=halves(c2d) + [whole_block(k.shape)],
        out_specs=[whole_block(s) for s in shapes],
        compiler_params=pltpu.CompilerParams(vmem_limit_bytes=8 * 2**20),
        name="pack_faces",
    )(c2d, c2d, k)


def corner_kernel(xl_ref, xh_ref, fx_ref, lo_ref, hi_ref, copies_ref):
    for at, ref in ((0, xh_ref), (NS, xl_ref)):
        lo_ref[at : at + NS, :] = ref[0:NS, :128]
        hi_ref[at : at + NS, :] = ref[0:NS, 128:]
    copies_ref[...] = jnp.broadcast_to(fx_ref[...][None], copies_ref.shape)


def corners(xl, xh, factor_x, count):
    shapes = [(2 * NS, 128)] * 2 + [(count,) + factor_x.shape]
    return pl.pallas_call(
        corner_kernel,
        grid=(1,),
        out_shape=[jax.ShapeDtypeStruct(s, f32) for s in shapes],
        in_specs=[whole_block(v.shape) for v in (xl, xh, factor_x)],
        out_specs=[whole_block(s) for s in shapes],
        compiler_params=pltpu.CompilerParams(vmem_limit_bytes=4 * 2**20),
        name="corner_columns",
    )(xl, xh, factor_x)


def split_2(v):
    hi = v.astype(bf16)
    return hi, (v - hi.astype(f32)).astype(bf16)


def advance_kernel(c0_ref, c1_ref, k_ref, rate_ref, xl_ref, xh_ref, yl_ref, yh_ref, left, right, e0, e1, ke):
    half = NS // 2
    lane_s, lane_h = lanes(NS), lanes(half)
    z = lane_s % NZ
    not_first, not_last = z > 0, z < NZ - 1
    below, above = lane_s >= 32, lane_s < 96

    low_h = lane_h < 64
    e0[0, :, :NV] = xh_ref[NS : 2 * NS, :]
    e0[1, :, :NV] = xh_ref[0:NS, :]
    e0[NX + 2, :, :NV] = xl_ref[0:NS, :]
    e0[NX + 3, :, :NV] = xl_ref[NS : 2 * NS, :]
    for row in (0, 1, NX + 2, NX + 3):
        e0[row, :, NV:] = jnp.zeros((NS, NH), f32)
    for x in range(NX):
        after, before = yl_ref[x * half : (x + 1) * half, :], yh_ref[x * half : (x + 1) * half, :]
        e0[x + 2, :, :128] = c0_ref[pl.ds(x, NS, stride=NX), :]
        e0[x + 2, :, 128:NV] = c1_ref[pl.ds(x, NS, stride=NX), :]
        e0[x + 2, :half, NV:] = jnp.where(low_h, after, before)
        e0[x + 2, half:, NV:] = pltpu.roll(jnp.where(low_h, before, after), 64, 1)
    ke[8 : 8 + NX, :NV] = k_ref[...]
    ke[8 : 8 + NX, NV:] = jnp.where(lanes(NX) < 64, yl_ref[NX * half :, :], yh_ref[NX * half :, :])
    ke[0:8, :NV] = xh_ref[2 * NS :, :]
    ke[0:8, NV:] = jnp.zeros((8, NH), f32)
    ke[8 + NX :, :NV] = xl_ref[2 * NS :, :]
    ke[8 + NX :, NV:] = jnp.zeros((8, NH), f32)
    rate = jnp.broadcast_to(rate_ref[...], (NS, 128))

    def step(src, row, k_row, tiles):
        t = [src[row, :, i * 128 : (i + 1) * 128] for i in range(3)]
        up = [pltpu.roll(v, 96, 1) for v in t]
        down = [pltpu.roll(v, 32, 1) for v in t]
        out = []
        for i in range(tiles):
            cut = slice(i * 128, (i + 1) * 128)
            total = src[row - 1, :, cut] + src[row + 1, :, cut]
            total = total + jnp.where(above, up[i], up[(i + 1) % 3]) + jnp.where(below, down[i], down[(i + 2) % 3])
            total = total + jnp.where(not_first, pltpu.roll(t[i], 1, 1), 0.0)
            total = total + jnp.where(not_last, pltpu.roll(t[i], 127, 1), 0.0)
            lap = total - 6.0 * t[i]
            out.append(t[i] + (rate * k_row[:, cut]) * lap)
        return out

    def first_step(x, carry):
        for i, v in enumerate(step(e0, x + 1, ke[pl.ds(x + 7, 1), :], 3)):
            e1[x, :, i * 128 : (i + 1) * 128] = v
        return carry

    lax.fori_loop(0, NX + 2, first_step, 0, unroll=True)

    def second_step(x, carry):
        done = step(e1, x + 1, ke[pl.ds(x + 8, 1), :], 2)
        left[pl.ds(x, NS, stride=NX), :], right[pl.ds(x, NS, stride=NX), :] = done
        return carry

    lax.fori_loop(0, NX, second_step, 0, unroll=True)


def advance(c2d, k, rate, faces):
    small = (k, rate, *faces)
    return pl.pallas_call(
        advance_kernel,
        grid=(1,),
        out_shape=[jax.ShapeDtypeStruct((NS * NX, 128), f32)] * 2,
        in_specs=halves(c2d) + [whole_block(v.shape) for v in small],
        out_specs=[whole_block((NS * NX, 128))] * 2,
        scratch_shapes=[
            pltpu.VMEM((NX + 4, NS, NV + NH), f32),
            pltpu.VMEM((NX + 2, NS, NV + NH), f32),
            pltpu.VMEM((NX + 16, NV + NH), f32),
        ],
        compiler_params=pltpu.CompilerParams(vmem_limit_bytes=16 * 2**20),
        cost_estimate=pl.CostEstimate(flops=4000000000, bytes_accessed=4 * 2**20, transcendentals=0),
        name="advance_twice",
    )(c2d, c2d, *small)


def reduce_kernel(a0_ref, a1_ref, k_ref, rate_ref, kxl_ref, kxh_ref, kyl_ref, kyh_ref, cl_ref, ch_ref, fs_ref, whole_ref,
                  adv_ref, planes_ref, left, right):
    left[...], right[...] = a0_ref[...], a1_ref[...]
    rate = jnp.broadcast_to(rate_ref[...], (NS, 128))
    first_y, last_y = lanes(NS) < NZ, lanes(NS) >= 128 - NZ
    for x, at, kx_ref in ((0, 0, kxh_ref), (NX - 1, NS, kxl_ref)):
        cut = pl.ds(x, NS, stride=NX)
        for ref, own, corner_ref, ky_ref, turn, mask in (
            (left, slice(0, 128), ch_ref, kyh_ref, 32, first_y),
            (right, slice(128, 256), cl_ref, kyl_ref, 96, last_y),
        ):
            paths = kx_ref[0:1, own] + pltpu.roll(jnp.broadcast_to(ky_ref[x : x + 1, :], (8, 128)), turn, 1)[0:1, :]
            term = (rate * k_ref[x : x + 1, own]) * (rate * paths) * pltpu.roll(corner_ref[at : at + NS, :], turn, 1)
            ref[cut, :] = ref[cut, :] + jnp.where(mask, term, 0.0)
    adv_ref[:, :128] = left[...]
    adv_ref[:, 128:] = right[...]

    lane_q = lanes(NQ)
    low_q, even_q = lane_q < 64, (lane_q & 32) == 0
    fs_hi, fs_lo = split_2(fs_ref[...])
    weights = jnp.concatenate([fs_hi, fs_hi, fs_lo, fs_lo], axis=1)

    def four_rows(group, carry):
        rows = []
        for g in range(4):
            cut = pl.ds(group * 4 + g, NS, stride=NX)
            hi, lo = split_2(jnp.concatenate([left[cut, :], right[cut, :]], axis=1))
            stacked = jnp.concatenate([hi, lo, hi, lo], axis=0)
            rows.append(jnp.dot(weights, stacked, preferred_element_type=f32))
        swapped = []
        for t in range(2):
            v = [r[:, t * 128 : (t + 1) * 128] for r in rows]
            a = [jnp.where(low_q, v[g], pltpu.roll(v[g + 2], 64, 1)) for g in range(2)]
            b = [jnp.where(low_q, pltpu.roll(v[g], 64, 1), v[g + 2]) for g in range(2)]
            for p, r in (a, b):
                swapped.append(jnp.where(even_q, p, pltpu.roll(r, 32, 1)))
                swapped.append(jnp.where(even_q, pltpu.roll(p, 96, 1), r))
        turned = jnp.concatenate(swapped, axis=0).T
        for g in range(4):
            planes_ref[pl.ds(group * 4 + g, NZ, stride=NX), :] = turned[g * NZ : (g + 1) * NZ, :]
        return carry

    lax.fori_loop(0, NX // 4, four_rows, 0, unroll=True)


def reduce_species(sides, k, rate, faces, corner, fs, whole):
    xl, xh, yl, yh = faces
    tail_x, tail_y = pl.BlockSpec((8, NV), lambda i: (2 * NS // 8, 0)), pl.BlockSpec((NX, 128), lambda i: (NS // 2, 0))
    shapes = [(NS * NX, NV), (NZ * NX, 128)]
    return pl.pallas_call(
        reduce_kernel,
        grid=(1,),
        out_shape=[jax.ShapeDtypeStruct(s, f32) for s in shapes],
        in_specs=[whole_block(v.shape) for v in (*sides, k, rate)]
        + [tail_x, tail_x, tail_y, tail_y]
        + [whole_block(v.shape) for v in (*corner, fs)]
        + [pl.BlockSpec(memory_space=pl.ANY)],
        out_specs=[whole_block(s) for s in shapes],
        scratch_shapes=[pltpu.VMEM((NS * NX, 128), f32)] * 2,
        compiler_params=pltpu.CompilerParams(vmem_limit_bytes=12 * 2**20),
        name="reduce_species",
    )(*sides, k, rate, xl, xh, yl, yh, *corner, fs, whole)


def shift_to(v, dx, dy):
    axis, step = ("tx", dx) if dx else ("ty", dy)
    count = lax.axis_size(axis)
    return lax.ppermute(v, axis, [(i, i + step) for i in range(count) if 0 <= i + step < count])


def body(species, cell_factor, species_rate, factor_x, factor_y, factor_species):
    nspec, cells_x, merged = species.shape
    cells_y = factor_y.shape[0]
    depth = merged // cells_y
    n_tx, n_ty = lax.axis_size("tx"), lax.axis_size("ty")
    ranks_q = factor_species.shape[1]
    c2d = species.reshape(nspec * cells_x, merged)
    faces = pack(c2d, cell_factor)
    xl, xh, yl, yh = (shift_to(v, dx, dy) for v, (dx, dy) in zip(faces, [(-1, 0), (1, 0), (0, -1), (0, 1)]))
    lo, hi, copies = corners(xl, xh, factor_x, n_tx // 2)
    corner = shift_to(lo, 0, -1), shift_to(hi, 0, 1)
    copies = copies.reshape(n_tx, cells_x // 2, factor_x.shape[1])
    mine = lax.all_to_all(copies, "tx", 0, 0, tiled=True)
    other = lax.ppermute(mine, "tx", [(i, i ^ 1) for i in range(n_tx)])
    faces, rate = (xl, xh, yl, yh), species_rate[:, None]
    sides = advance(c2d, cell_factor, rate, faces)
    advanced, planes = reduce_species(sides, cell_factor, rate, faces, corner, factor_species.T, mine)
    planes = planes.reshape(depth, cells_x, cells_y * ranks_q)
    planes = lax.all_to_all(planes, "tx", 0, 0, tiled=True)
    even = lax.axis_index("tx") % 2 == 0
    whole_x = jnp.concatenate([jnp.where(even, mine, other), jnp.where(even, other, mine)], axis=1)
    first = lax.dot_general(planes, whole_x, (((0, 1), (0, 1)), ((), ())), precision=exact_mode)
    first = first.reshape(cells_y, ranks_q, -1).transpose(1, 0, 2)
    sent = jnp.concatenate([first, jnp.broadcast_to(factor_y[None], (n_ty,) + factor_y.shape)], axis=1)
    came = lax.all_to_all(sent, "ty", 0, 0, tiled=True)
    first = came[:, :cells_y].reshape(n_ty * cells_y, -1)
    whole_y = came[:, cells_y:].reshape(n_ty * cells_y, -1)
    plane = lax.dot_general(first, whole_y, (((0,), (0,)), ((), ())), precision=exact_mode)
    rank_a, rank_b = plane.shape
    plane = plane.reshape(n_tx, rank_a // n_tx, n_ty, rank_b // n_ty).transpose(0, 2, 1, 3)
    plane = plane.reshape(n_tx * n_ty, 1, -1)
    core = lax.all_to_all(plane, ("tx", "ty"), 0, 0, tiled=True)
    core = core.reshape(depth, ranks_q, rank_a // n_tx, rank_b // n_ty).transpose(2, 1, 3, 0)
    return advanced.reshape(species.shape), core.reshape(rank_a // n_tx, ranks_q, -1)


def solution(mesh):
    in_specs = (P(None, "tx", "ty"), P("tx", "ty"), P(), P("tx", None), P("ty", None), P())
    out_specs = (P(None, "tx", "ty"), P("tx", None, "ty"))
    return jax.shard_map(body, mesh=mesh, in_specs=in_specs, out_specs=out_specs, check_vma=False)
```

```python
import jax
import jax.numpy as jnp
from jax import lax
from jax.experimental import pallas as pl
from jax.experimental.pallas import tpu as pltpu
from jax.sharding import PartitionSpec as P

exact_mode = lax.Precision.HIGHEST
f32, bf16 = jnp.float32, jnp.bfloat16
SENT = 48
NS, NX, NV, NH, NZ, NQ = 32, 32, 256, 128, 32, 16


def lanes(rows):
    return lax.broadcasted_iota(jnp.int32, (rows, 128), 1)


def pack_kernel(c0_ref, c1_ref, k_ref, xl_ref, xh_ref, yl_ref, yh_ref):
    low = lanes(NS // 2) < 64

    def row(x):
        return [r[pl.ds(x, NS, stride=NX), :] for r in (c0_ref, c1_ref)]

    for ref, at, x in ((xl_ref, 0, 0), (xl_ref, NS, 1), (xh_ref, 0, NX - 1), (xh_ref, NS, NX - 2)):
        ref[at : at + NS, :128], ref[at : at + NS, 128:] = row(x)
    xl_ref[2 * NS :, :] = jnp.broadcast_to(k_ref[0:1, :], (8, NV))
    xh_ref[2 * NS :, :] = jnp.broadcast_to(k_ref[NX - 1 : NX, :], (8, NV))
    half = NS // 2
    for x in range(NX):
        t0, t1 = row(x)
        yl_ref[x * half : (x + 1) * half, :] = jnp.where(low, t0[:half], pltpu.roll(t0[half:], 64, 1))
        yh_ref[x * half : (x + 1) * half, :] = jnp.where(low, pltpu.roll(t1[half:], 64, 1), t1[:half])
    yl_ref[NX * half :, :] = k_ref[:, :128]
    yh_ref[NX * half :, :] = k_ref[:, 128:]


def whole_block(shape):
    return pl.BlockSpec(shape, lambda i: (0,) * len(shape))


def halves(v):
    return [pl.BlockSpec((v.shape[0], 128), lambda i, side=side: (0, side)) for side in range(2)]


def pack(c2d, k):
    shapes = [(2 * NS + 8, NV)] * 2 + [(NX * NS // 2 + NX, 128)] * 2
    return pl.pallas_call(
        pack_kernel,
        grid=(1,),
        out_shape=[jax.ShapeDtypeStruct(s, f32) for s in shapes],
        in_specs=halves(c2d) + [whole_block(k.shape)],
        out_specs=[whole_block(s) for s in shapes],
        compiler_params=pltpu.CompilerParams(vmem_limit_bytes=8 * 2**20),
        name="pack_faces",
    )(c2d, c2d, k)


def corner_kernel(xl_ref, xh_ref, lo_ref, hi_ref):
    for at, ref in ((0, xh_ref), (NS, xl_ref)):
        lo_ref[at : at + NS, :] = ref[0:NS, :128]
        hi_ref[at : at + NS, :] = ref[0:NS, 128:]


def corners(xl, xh):
    shapes = [(2 * NS, 128)] * 2
    return pl.pallas_call(
        corner_kernel,
        grid=(1,),
        out_shape=[jax.ShapeDtypeStruct(s, f32) for s in shapes],
        in_specs=[whole_block(v.shape) for v in (xl, xh)],
        out_specs=[whole_block(s) for s in shapes],
        compiler_params=pltpu.CompilerParams(vmem_limit_bytes=4 * 2**20),
        name="corner_columns",
    )(xl, xh)


def split_2(v):
    hi = v.astype(bf16)
    return hi, (v - hi.astype(f32)).astype(bf16)


def advance_kernel(c0_ref, c1_ref, k_ref, rate_ref, xl_ref, xh_ref, yl_ref, yh_ref, left, right, e0, e1, ke):
    half = NS // 2
    lane_s, lane_h = lanes(NS), lanes(half)
    z = lane_s % NZ
    not_first, not_last = z > 0, z < NZ - 1
    below, above = lane_s >= 32, lane_s < 96

    low_h = lane_h < 64
    e0[0, :, :NV] = xh_ref[NS : 2 * NS, :]
    e0[1, :, :NV] = xh_ref[0:NS, :]
    e0[NX + 2, :, :NV] = xl_ref[0:NS, :]
    e0[NX + 3, :, :NV] = xl_ref[NS : 2 * NS, :]
    for row in (0, 1, NX + 2, NX + 3):
        e0[row, :, NV:] = jnp.zeros((NS, NH), f32)
    for x in range(NX):
        after, before = yl_ref[x * half : (x + 1) * half, :], yh_ref[x * half : (x + 1) * half, :]
        e0[x + 2, :, :128] = c0_ref[pl.ds(x, NS, stride=NX), :]
        e0[x + 2, :, 128:NV] = c1_ref[pl.ds(x, NS, stride=NX), :]
        e0[x + 2, :half, NV:] = jnp.where(low_h, after, before)
        e0[x + 2, half:, NV:] = pltpu.roll(jnp.where(low_h, before, after), 64, 1)
    ke[8 : 8 + NX, :NV] = k_ref[...]
    ke[8 : 8 + NX, NV:] = jnp.where(lanes(NX) < 64, yl_ref[NX * half :, :], yh_ref[NX * half :, :])
    ke[0:8, :NV] = xh_ref[2 * NS :, :]
    ke[0:8, NV:] = jnp.zeros((8, NH), f32)
    ke[8 + NX :, :NV] = xl_ref[2 * NS :, :]
    ke[8 + NX :, NV:] = jnp.zeros((8, NH), f32)
    rate = jnp.broadcast_to(rate_ref[...], (NS, 128))

    def step(src, row, k_row, tiles):
        t = [src[row, :, i * 128 : (i + 1) * 128] for i in range(3)]
        up = [pltpu.roll(v, 96, 1) for v in t]
        down = [pltpu.roll(v, 32, 1) for v in t]
        out = []
        for i in range(tiles):
            cut = slice(i * 128, (i + 1) * 128)
            total = src[row - 1, :, cut] + src[row + 1, :, cut]
            total = total + jnp.where(above, up[i], up[(i + 1) % 3]) + jnp.where(below, down[i], down[(i + 2) % 3])
            total = total + jnp.where(not_first, pltpu.roll(t[i], 1, 1), 0.0)
            total = total + jnp.where(not_last, pltpu.roll(t[i], 127, 1), 0.0)
            lap = total - 6.0 * t[i]
            out.append(t[i] + (rate * k_row[:, cut]) * lap)
        return out

    def first_step(x, carry):
        for i, v in enumerate(step(e0, x + 1, ke[pl.ds(x + 7, 1), :], 3)):
            e1[x, :, i * 128 : (i + 1) * 128] = v
        return carry

    lax.fori_loop(0, NX + 2, first_step, 0, unroll=True)

    def second_step(x, carry):
        done = step(e1, x + 1, ke[pl.ds(x + 8, 1), :], 2)
        left[pl.ds(x, NS, stride=NX), :], right[pl.ds(x, NS, stride=NX), :] = done
        return carry

    lax.fori_loop(0, NX, second_step, 0, unroll=True)


def advance(c2d, k, rate, faces):
    small = (k, rate, *faces)
    return pl.pallas_call(
        advance_kernel,
        grid=(1,),
        out_shape=[jax.ShapeDtypeStruct((NS * NX, 128), f32)] * 2,
        in_specs=halves(c2d) + [whole_block(v.shape) for v in small],
        out_specs=[whole_block((NS * NX, 128))] * 2,
        scratch_shapes=[
            pltpu.VMEM((NX + 4, NS, NV + NH), f32),
            pltpu.VMEM((NX + 2, NS, NV + NH), f32),
            pltpu.VMEM((NX + 16, NV + NH), f32),
        ],
        compiler_params=pltpu.CompilerParams(vmem_limit_bytes=16 * 2**20),
        cost_estimate=pl.CostEstimate(flops=10000000000, bytes_accessed=4 * 2**20, transcendentals=0),
        name="advance_twice",
    )(c2d, c2d, *small)


def reduce_kernel(a0_ref, a1_ref, k_ref, rate_ref, kxl_ref, kxh_ref, kyl_ref, kyh_ref, cl_ref, ch_ref, fs_ref, fx_ref, fy_ref,
                  adv_ref, planes_ref, fy_out_ref, left, right, flip):
    left[...], right[...] = a0_ref[...], a1_ref[...]
    fy_out_ref[...] = fy_ref[...]
    rate = jnp.broadcast_to(rate_ref[...], (NS, 128))
    first_y, last_y = lanes(NS) < NZ, lanes(NS) >= 128 - NZ
    for x, at, kx_ref in ((0, 0, kxh_ref), (NX - 1, NS, kxl_ref)):
        cut = pl.ds(x, NS, stride=NX)
        for ref, own, corner_ref, ky_ref, turn, mask in (
            (left, slice(0, 128), ch_ref, kyh_ref, 32, first_y),
            (right, slice(128, 256), cl_ref, kyl_ref, 96, last_y),
        ):
            paths = kx_ref[0:1, own] + pltpu.roll(jnp.broadcast_to(ky_ref[x : x + 1, :], (8, 128)), turn, 1)[0:1, :]
            term = (rate * k_ref[x : x + 1, own]) * (rate * paths) * pltpu.roll(corner_ref[at : at + NS, :], turn, 1)
            ref[cut, :] = ref[cut, :] + jnp.where(mask, term, 0.0)
    adv_ref[:, :128] = left[...]
    adv_ref[:, 128:] = right[...]
    for to in range(NZ):
        side = to % 2
        planes_ref[to * SENT + NX : (to + 1) * SENT, :] = fx_ref[side * (NX // 2) : (side + 1) * (NX // 2), :]

    lane_q = lanes(NQ)
    low_q, even_q = lane_q < 64, (lane_q & 32) == 0
    fs_hi, fs_lo = split_2(fs_ref[...])
    weights = jnp.concatenate([fs_hi, fs_hi, fs_lo, fs_lo], axis=1)

    for group in range(NX // 4):
        rows = []
        for g in range(4):
            cut = pl.ds(group * 4 + g, NS, stride=NX)
            hi, lo = split_2(jnp.concatenate([left[cut, :], right[cut, :]], axis=1))
            stacked = jnp.concatenate([hi, lo, hi, lo], axis=0)
            rows.append(jnp.dot(weights, stacked, preferred_element_type=f32))
        swapped = []
        for t in range(2):
            v = [r[:, t * 128 : (t + 1) * 128] for r in rows]
            a = [jnp.where(low_q, v[g], pltpu.roll(v[g + 2], 64, 1)) for g in range(2)]
            b = [jnp.where(low_q, pltpu.roll(v[g], 64, 1), v[g + 2]) for g in range(2)]
            for p, r in (a, b):
                swapped.append(jnp.where(even_q, p, pltpu.roll(r, 32, 1)))
                swapped.append(jnp.where(even_q, pltpu.roll(p, 96, 1), r))
        flip[group * 128 : (group + 1) * 128, :] = jnp.concatenate(swapped, axis=0).T
        for g in range(4):
            side, x = divmod(group * 4 + g, NX // 2)
            for e in range(2):
                to = pl.ds(side * SENT + e * (NX // 2) + x, NZ // 2, stride=2 * SENT)
                planes_ref[to, :] = flip[pl.ds(group * 128 + g * NZ + e, NZ // 2, stride=2), :]


def reduce_species(sides, k, rate, faces, corner, fs, factor_x, factor_y):
    xl, xh, yl, yh = faces
    tail_x, tail_y = pl.BlockSpec((8, NV), lambda i: (2 * NS // 8, 0)), pl.BlockSpec((NX, 128), lambda i: (NS // 2, 0))
    shapes = [(NS * NX, NV), (NZ * SENT, 128), factor_y.shape]
    return pl.pallas_call(
        reduce_kernel,
        grid=(1,),
        out_shape=[jax.ShapeDtypeStruct(s, f32) for s in shapes],
        in_specs=[whole_block(v.shape) for v in (*sides, k, rate)]
        + [tail_x, tail_x, tail_y, tail_y]
        + [whole_block(v.shape) for v in (*corner, fs, factor_x, factor_y)],
        out_specs=[whole_block(s) for s in shapes],
        scratch_shapes=[pltpu.VMEM((NS * NX, 128), f32)] * 3,
        compiler_params=pltpu.CompilerParams(vmem_limit_bytes=12 * 2**20),
        name="reduce_species",
    )(*sides, k, rate, xl, xh, yl, yh, *corner, fs, factor_x, factor_y)


def shift_to(v, dx, dy):
    axis, step = ("tx", dx) if dx else ("ty", dy)
    count = lax.axis_size(axis)
    return lax.ppermute(v, axis, [(i, i + step) for i in range(count) if 0 <= i + step < count])


def body(species, cell_factor, species_rate, factor_x, factor_y, factor_species):
    nspec, cells_x, merged = species.shape
    cells_y = factor_y.shape[0]
    depth = merged // cells_y
    n_tx, n_ty = lax.axis_size("tx"), lax.axis_size("ty")
    ranks_q = factor_species.shape[1]
    c2d = species.reshape(nspec * cells_x, merged)
    faces = pack(c2d, cell_factor)
    xl, xh, yl, yh = (shift_to(v, dx, dy) for v, (dx, dy) in zip(faces, [(-1, 0), (1, 0), (0, -1), (0, 1)]))
    lo, hi = corners(xl, xh)
    corner = shift_to(lo, 0, -1), shift_to(hi, 0, 1)
    faces, rate = (xl, xh, yl, yh), species_rate[:, None]
    sides = advance(c2d, cell_factor, rate, faces)
    advanced, planes, factor_y = reduce_species(sides, cell_factor, rate, faces, corner, factor_species.T, factor_x, factor_y)
    planes = planes.reshape(n_tx, SENT, cells_y * ranks_q)
    planes = lax.all_to_all(planes, "tx", 0, 0, tiled=True)
    side, half = lax.axis_index("tx") % 2, cells_x // 2

    def over_x(which):
        plane = lax.dynamic_slice_in_dim(planes, which * half, half, axis=1)
        return lax.dot_general(plane, planes[:, cells_x:], (((0, 1), (0, 1)), ((), ())), precision=exact_mode)

    came = lax.ppermute(over_x(1 - side), "tx", [(i, i ^ 1) for i in range(n_tx)])
    first = over_x(side) + came
    first = first.reshape(cells_y, ranks_q, -1).transpose(1, 0, 2)
    sent = jnp.concatenate([first, jnp.broadcast_to(factor_y[None], (n_ty,) + factor_y.shape)], axis=1)
    came = lax.all_to_all(sent, "ty", 0, 0, tiled=True)
    first = came[:, :cells_y].reshape(n_ty * cells_y, -1)
    whole_y = came[:, cells_y:].reshape(n_ty * cells_y, -1)
    plane = lax.dot_general(first, whole_y, (((0,), (0,)), ((), ())), precision=exact_mode)
    rank_a, rank_b = plane.shape
    plane = plane.reshape(n_tx, rank_a // n_tx, n_ty, rank_b // n_ty).transpose(0, 2, 1, 3)
    plane = plane.reshape(n_tx * n_ty, 1, -1)
    core = lax.all_to_all(plane, ("tx", "ty"), 0, 0, tiled=True)
    core = core.reshape(depth, ranks_q, rank_a // n_tx, rank_b // n_ty).transpose(2, 1, 3, 0)
    return advanced.reshape(species.shape), core.reshape(rank_a // n_tx, ranks_q, -1)


def solution(mesh):
    in_specs = (P(None, "tx", "ty"), P("tx", "ty"), P(), P("tx", None), P("ty", None), P())
    out_specs = (P(None, "tx", "ty"), P("tx", None, "ty"))
    return jax.shard_map(body, mesh=mesh, in_specs=in_specs, out_specs=out_specs, check_vma=False)
```

```python
import jax
import jax.numpy as jnp
from jax import lax
from jax.experimental import pallas as pl
from jax.experimental.pallas import tpu as pltpu
from jax.sharding import PartitionSpec as P

exact_mode = lax.Precision.HIGH
f32, bf16 = jnp.float32, jnp.bfloat16
NS, NX, NV, NH, NZ, NQ = 32, 32, 256, 128, 32, 16


def lanes(rows):
    return lax.broadcasted_iota(jnp.int32, (rows, 128), 1)


def pack_kernel(k_ref, c0_ref, c1_ref, xl_ref, xh_ref, yl_ref, yh_ref):
    low = lanes(NS // 2) < 64

    def row(x):
        return [r[pl.ds(x, NS, stride=NX), :] for r in (c0_ref, c1_ref)]

    for ref, at, x in ((xl_ref, 0, 0), (xl_ref, NS, 1), (xh_ref, 0, NX - 1), (xh_ref, NS, NX - 2)):
        ref[at : at + NS, :128], ref[at : at + NS, 128:] = row(x)
    xl_ref[2 * NS :, :] = jnp.broadcast_to(k_ref[0:1, :], (8, NV))
    xh_ref[2 * NS :, :] = jnp.broadcast_to(k_ref[NX - 1 : NX, :], (8, NV))
    half = NS // 2
    for x in range(NX):
        t0, t1 = row(x)
        yl_ref[x * half : (x + 1) * half, :] = jnp.where(low, t0[:half], pltpu.roll(t0[half:], 64, 1))
        yh_ref[x * half : (x + 1) * half, :] = jnp.where(low, pltpu.roll(t1[half:], 64, 1), t1[:half])
    yl_ref[NX * half :, :] = k_ref[:, :128]
    yh_ref[NX * half :, :] = k_ref[:, 128:]


def whole_block(shape):
    return pl.BlockSpec(shape, lambda i: (0,) * len(shape))


def halves(v):
    return [pl.BlockSpec((v.shape[0], 128), lambda i, side=side: (0, side)) for side in range(2)]


def pack(c2d, k):
    shapes = [(2 * NS + 8, NV)] * 2 + [(NX * NS // 2 + NX, 128)] * 2
    return pl.pallas_call(
        pack_kernel,
        grid=(1,),
        out_shape=[jax.ShapeDtypeStruct(s, f32) for s in shapes],
        in_specs=[whole_block(k.shape)] + halves(c2d),
        out_specs=[whole_block(s) for s in shapes],
        compiler_params=pltpu.CompilerParams(vmem_limit_bytes=8 * 2**20),
        name="pack_faces",
    )(k, c2d, c2d)


def corner_kernel(xl_ref, xh_ref, lo_ref, hi_ref):
    for at, ref in ((0, xh_ref), (NS, xl_ref)):
        lo_ref[at : at + NS, :] = ref[0:NS, :128]
        hi_ref[at : at + NS, :] = ref[0:NS, 128:]


def corners(xl, xh):
    shapes = [(2 * NS, 128)] * 2
    return pl.pallas_call(
        corner_kernel,
        grid=(1,),
        out_shape=[jax.ShapeDtypeStruct(s, f32) for s in shapes],
        in_specs=[whole_block(v.shape) for v in (xl, xh)],
        out_specs=[whole_block(s) for s in shapes],
        compiler_params=pltpu.CompilerParams(vmem_limit_bytes=4 * 2**20),
        name="corner_columns",
    )(xl, xh)


def split_2(v):
    hi = v.astype(bf16)
    return hi, (v - hi.astype(f32)).astype(bf16)


def advance_kernel(c0_ref, c1_ref, k_ref, rate_ref, xl_ref, xh_ref, yl_ref, yh_ref, left, right, e0, e1, ke):
    half = NS // 2
    lane_s, lane_h = lanes(NS), lanes(half)
    z = lane_s % NZ
    not_first, not_last = z > 0, z < NZ - 1
    below, above = lane_s >= 32, lane_s < 96

    low_h = lane_h < 64
    e0[0, :, :NV] = xh_ref[NS : 2 * NS, :]
    e0[1, :, :NV] = xh_ref[0:NS, :]
    e0[NX + 2, :, :NV] = xl_ref[0:NS, :]
    e0[NX + 3, :, :NV] = xl_ref[NS : 2 * NS, :]
    for row in (0, 1, NX + 2, NX + 3):
        e0[row, :, NV:] = jnp.zeros((NS, NH), f32)
    for x in range(NX):
        after, before = yl_ref[x * half : (x + 1) * half, :], yh_ref[x * half : (x + 1) * half, :]
        e0[x + 2, :, :128] = c0_ref[pl.ds(x, NS, stride=NX), :]
        e0[x + 2, :, 128:NV] = c1_ref[pl.ds(x, NS, stride=NX), :]
        e0[x + 2, :half, NV:] = jnp.where(low_h, after, before)
        e0[x + 2, half:, NV:] = pltpu.roll(jnp.where(low_h, before, after), 64, 1)
    ke[8 : 8 + NX, :NV] = k_ref[...]
    ke[8 : 8 + NX, NV:] = jnp.where(lanes(NX) < 64, yl_ref[NX * half :, :], yh_ref[NX * half :, :])
    ke[0:8, :NV] = xh_ref[2 * NS :, :]
    ke[0:8, NV:] = jnp.zeros((8, NH), f32)
    ke[8 + NX :, :NV] = xl_ref[2 * NS :, :]
    ke[8 + NX :, NV:] = jnp.zeros((8, NH), f32)
    rate = jnp.broadcast_to(rate_ref[...], (NS, 128))

    def step(src, row, k_row, tiles):
        t = [src[row, :, i * 128 : (i + 1) * 128] for i in range(3)]
        up = [pltpu.roll(v, 96, 1) for v in t]
        down = [pltpu.roll(v, 32, 1) for v in t]
        out = []
        for i in range(tiles):
            cut = slice(i * 128, (i + 1) * 128)
            total = src[row - 1, :, cut] + src[row + 1, :, cut]
            total = total + jnp.where(above, up[i], up[(i + 1) % 3]) + jnp.where(below, down[i], down[(i + 2) % 3])
            total = total + jnp.where(not_first, pltpu.roll(t[i], 1, 1), 0.0)
            total = total + jnp.where(not_last, pltpu.roll(t[i], 127, 1), 0.0)
            lap = total - 6.0 * t[i]
            out.append(t[i] + (rate * k_row[:, cut]) * lap)
        return out

    def first_step(x, carry):
        for i, v in enumerate(step(e0, x + 1, ke[pl.ds(x + 7, 1), :], 3)):
            e1[x, :, i * 128 : (i + 1) * 128] = v
        return carry

    lax.fori_loop(0, NX + 2, first_step, 0, unroll=True)

    def second_step(x, carry):
        done = step(e1, x + 1, ke[pl.ds(x + 8, 1), :], 2)
        left[pl.ds(x, NS, stride=NX), :], right[pl.ds(x, NS, stride=NX), :] = done
        return carry

    lax.fori_loop(0, NX, second_step, 0, unroll=True)


def advance(c2d, k, rate, faces):
    small = (k, rate, *faces)
    return pl.pallas_call(
        advance_kernel,
        grid=(1,),
        out_shape=[jax.ShapeDtypeStruct((NS * NX, 128), f32)] * 2,
        in_specs=halves(c2d) + [whole_block(v.shape) for v in small],
        out_specs=[whole_block((NS * NX, 128))] * 2,
        scratch_shapes=[
            pltpu.VMEM((NX + 4, NS, NV + NH), f32),
            pltpu.VMEM((NX + 2, NS, NV + NH), f32),
            pltpu.VMEM((NX + 16, NV + NH), f32),
        ],
        compiler_params=pltpu.CompilerParams(vmem_limit_bytes=16 * 2**20),
        cost_estimate=pl.CostEstimate(flops=10000000000, bytes_accessed=4 * 2**20, transcendentals=0),
        name="advance_twice",
    )(c2d, c2d, *small)


def reduce_kernel(a0_ref, a1_ref, k_ref, rate_ref, kxl_ref, kxh_ref, kyl_ref, kyh_ref, cl_ref, ch_ref, fs_ref, fx_ref,
                  adv_ref, planes_ref, left, right):
    left[...], right[...] = a0_ref[...], a1_ref[...]
    rate = jnp.broadcast_to(rate_ref[...], (NS, 128))
    first_y, last_y = lanes(NS) < NZ, lanes(NS) >= 128 - NZ
    for x, at, kx_ref in ((0, 0, kxh_ref), (NX - 1, NS, kxl_ref)):
        cut = pl.ds(x, NS, stride=NX)
        for ref, own, corner_ref, ky_ref, turn, mask in (
            (left, slice(0, 128), ch_ref, kyh_ref, 32, first_y),
            (right, slice(128, 256), cl_ref, kyl_ref, 96, last_y),
        ):
            paths = kx_ref[0:1, own] + pltpu.roll(jnp.broadcast_to(ky_ref[x : x + 1, :], (8, 128)), turn, 1)[0:1, :]
            term = (rate * k_ref[x : x + 1, own]) * (rate * paths) * pltpu.roll(corner_ref[at : at + NS, :], turn, 1)
            ref[cut, :] = ref[cut, :] + jnp.where(mask, term, 0.0)
    adv_ref[:, :128] = left[...]
    adv_ref[:, 128:] = right[...]
    for z in range(NZ):
        planes_ref[(2 * z + 1) * NX : (2 * z + 2) * NX, :] = fx_ref[...]

    lane_q = lanes(NQ)
    low_q, even_q = lane_q < 64, (lane_q & 32) == 0
    fs_hi, fs_lo = split_2(fs_ref[...])
    weights = jnp.concatenate([fs_hi, fs_hi, fs_lo, fs_lo], axis=1)

    def four_rows(group, carry):
        rows = []
        for g in range(4):
            cut = pl.ds(group * 4 + g, NS, stride=NX)
            hi, lo = split_2(jnp.concatenate([left[cut, :], right[cut, :]], axis=1))
            stacked = jnp.concatenate([hi, lo, hi, lo], axis=0)
            rows.append(jnp.dot(weights, stacked, preferred_element_type=f32))
        swapped = []
        for t in range(2):
            v = [r[:, t * 128 : (t + 1) * 128] for r in rows]
            a = [jnp.where(low_q, v[g], pltpu.roll(v[g + 2], 64, 1)) for g in range(2)]
            b = [jnp.where(low_q, pltpu.roll(v[g], 64, 1), v[g + 2]) for g in range(2)]
            for p, r in (a, b):
                swapped.append(jnp.where(even_q, p, pltpu.roll(r, 32, 1)))
                swapped.append(jnp.where(even_q, pltpu.roll(p, 96, 1), r))
        turned = jnp.concatenate(swapped, axis=0).T
        for g in range(4):
            planes_ref[pl.ds(group * 4 + g, NZ, stride=2 * NX), :] = turned[g * NZ : (g + 1) * NZ, :]
        return carry

    lax.fori_loop(0, NX // 4, four_rows, 0, unroll=True)


def reduce_species(sides, k, rate, faces, corner, fs, factor_x):
    xl, xh, yl, yh = faces
    tail_x, tail_y = pl.BlockSpec((8, NV), lambda i: (2 * NS // 8, 0)), pl.BlockSpec((NX, 128), lambda i: (NS // 2, 0))
    shapes = [(NS * NX, NV), (NZ * 2 * NX, 128)]
    return pl.pallas_call(
        reduce_kernel,
        grid=(1,),
        out_shape=[jax.ShapeDtypeStruct(s, f32) for s in shapes],
        in_specs=[whole_block(v.shape) for v in (*sides, k, rate)]
        + [tail_x, tail_x, tail_y, tail_y]
        + [whole_block(v.shape) for v in (*corner, fs, factor_x)],
        out_specs=[whole_block(s) for s in shapes],
        scratch_shapes=[pltpu.VMEM((NS * NX, 128), f32)] * 2,
        compiler_params=pltpu.CompilerParams(vmem_limit_bytes=12 * 2**20),
        name="reduce_species",
    )(*sides, k, rate, xl, xh, yl, yh, *corner, fs, factor_x)


def shift_to(v, dx, dy):
    axis, step = ("tx", dx) if dx else ("ty", dy)
    count = lax.axis_size(axis)
    return lax.ppermute(v, axis, [(i, i + step) for i in range(count) if 0 <= i + step < count])


def body(species, cell_factor, species_rate, factor_x, factor_y, factor_species):
    nspec, cells_x, merged = species.shape
    cells_y = factor_y.shape[0]
    depth = merged // cells_y
    n_tx, n_ty = lax.axis_size("tx"), lax.axis_size("ty")
    ranks_q = factor_species.shape[1]
    c2d = species.reshape(nspec * cells_x, merged)
    faces = pack(c2d, cell_factor)
    xl, xh, yl, yh = (shift_to(v, dx, dy) for v, (dx, dy) in zip(faces, [(-1, 0), (1, 0), (0, -1), (0, 1)]))
    lo, hi = corners(xl, xh)
    corner = shift_to(lo, 0, -1), shift_to(hi, 0, 1)
    faces, rate = (xl, xh, yl, yh), species_rate[:, None]
    sides = advance(c2d, cell_factor, rate, faces)
    advanced, planes = reduce_species(sides, cell_factor, rate, faces, corner, factor_species.T, factor_x)
    planes = planes.reshape(depth, 2 * cells_x, cells_y * ranks_q)
    planes = lax.all_to_all(planes, "tx", 0, 0, tiled=True)
    first = lax.dot_general(
        planes[:, :cells_x], planes[:, cells_x:], (((0, 1), (0, 1)), ((), ())), precision=exact_mode
    )
    first = first.reshape(cells_y, ranks_q, -1).transpose(1, 0, 2)
    sent = jnp.concatenate([first, jnp.broadcast_to(factor_y[None], (n_ty,) + factor_y.shape)], axis=1)
    came = lax.all_to_all(sent, "ty", 0, 0, tiled=True)
    first = came[:, :cells_y].reshape(n_ty * cells_y, -1)
    whole_y = came[:, cells_y:].reshape(n_ty * cells_y, -1)
    plane = lax.dot_general(first, whole_y, (((0,), (0,)), ((), ())), precision=exact_mode)
    rank_a, rank_b = plane.shape
    plane = plane.reshape(n_tx, rank_a // n_tx, n_ty, rank_b // n_ty).transpose(0, 2, 1, 3)
    plane = plane.reshape(n_tx * n_ty, 1, -1)
    core = lax.all_to_all(plane, ("tx", "ty"), 0, 0, tiled=True)
    core = core.reshape(depth, ranks_q, rank_a // n_tx, rank_b // n_ty).transpose(2, 1, 3, 0)
    return advanced.reshape(species.shape), core.reshape(rank_a // n_tx, ranks_q, -1)


def solution(mesh):
    in_specs = (P(None, "tx", "ty"), P("tx", "ty"), P(), P("tx", None), P("ty", None), P())
    out_specs = (P(None, "tx", "ty"), P("tx", None, "ty"))
    return jax.shard_map(body, mesh=mesh, in_specs=in_specs, out_specs=out_specs, check_vma=False)
```

```python
import jax
import jax.numpy as jnp
from jax import lax
from jax.experimental import pallas as pl
from jax.experimental.pallas import tpu as pltpu
from jax.sharding import PartitionSpec as P

exact_mode = lax.Precision.HIGHEST
f32, bf16 = jnp.float32, jnp.bfloat16
NS, NX, NV, NH, NZ, NQ = 32, 32, 256, 128, 32, 16


def lanes(rows):
    return lax.broadcasted_iota(jnp.int32, (rows, 128), 1)


def pack_kernel(c0_ref, c1_ref, k_ref, xl_ref, xh_ref, yl_ref, yh_ref):
    low = lanes(NS // 2) < 64

    def row(x):
        return [r[pl.ds(x, NS, stride=NX), :] for r in (c0_ref, c1_ref)]

    for ref, at, x in ((xl_ref, 0, 0), (xl_ref, NS, 1), (xh_ref, 0, NX - 1), (xh_ref, NS, NX - 2)):
        ref[at : at + NS, :128], ref[at : at + NS, 128:] = row(x)
    xl_ref[2 * NS :, :] = jnp.broadcast_to(k_ref[0:1, :], (8, NV))
    xh_ref[2 * NS :, :] = jnp.broadcast_to(k_ref[NX - 1 : NX, :], (8, NV))
    half = NS // 2
    for x in range(NX):
        t0, t1 = row(x)
        yl_ref[x * half : (x + 1) * half, :] = jnp.where(low, t0[:half], pltpu.roll(t0[half:], 64, 1))
        yh_ref[x * half : (x + 1) * half, :] = jnp.where(low, pltpu.roll(t1[half:], 64, 1), t1[:half])
    yl_ref[NX * half :, :] = k_ref[:, :128]
    yh_ref[NX * half :, :] = k_ref[:, 128:]


def whole_block(shape):
    return pl.BlockSpec(shape, lambda i: (0,) * len(shape))


def halves(v):
    return [pl.BlockSpec((v.shape[0], 128), lambda i, side=side: (0, side)) for side in range(2)]


def pack(c2d, k):
    shapes = [(2 * NS + 8, NV)] * 2 + [(NX * NS // 2 + NX, 128)] * 2
    return pl.pallas_call(
        pack_kernel,
        grid=(1,),
        out_shape=[jax.ShapeDtypeStruct(s, f32) for s in shapes],
        in_specs=halves(c2d) + [whole_block(k.shape)],
        out_specs=[whole_block(s) for s in shapes],
        compiler_params=pltpu.CompilerParams(vmem_limit_bytes=8 * 2**20),
        name="pack_faces",
    )(c2d, c2d, k)


def corner_kernel(xl_ref, xh_ref, lo_ref, hi_ref):
    for at, ref in ((0, xh_ref), (NS, xl_ref)):
        lo_ref[at : at + NS, :] = ref[0:NS, :128]
        hi_ref[at : at + NS, :] = ref[0:NS, 128:]


def corners(xl, xh):
    shapes = [(2 * NS, 128)] * 2
    return pl.pallas_call(
        corner_kernel,
        grid=(1,),
        out_shape=[jax.ShapeDtypeStruct(s, f32) for s in shapes],
        in_specs=[whole_block(v.shape) for v in (xl, xh)],
        out_specs=[whole_block(s) for s in shapes],
        compiler_params=pltpu.CompilerParams(vmem_limit_bytes=4 * 2**20),
        name="corner_columns",
    )(xl, xh)


def split_2(v):
    hi = v.astype(bf16)
    return hi, (v - hi.astype(f32)).astype(bf16)


def advance_kernel(c0_ref, c1_ref, k_ref, rate_ref, xl_ref, xh_ref, yl_ref, yh_ref, left, right, e0, e1, ke):
    half = NS // 2
    lane_s, lane_h = lanes(NS), lanes(half)
    z = lane_s % NZ
    not_first, not_last = z > 0, z < NZ - 1
    below, above = lane_s >= 32, lane_s < 96

    low_h = lane_h < 64
    e0[0, :, :NV] = xh_ref[NS : 2 * NS, :]
    e0[1, :, :NV] = xh_ref[0:NS, :]
    e0[NX + 2, :, :NV] = xl_ref[0:NS, :]
    e0[NX + 3, :, :NV] = xl_ref[NS : 2 * NS, :]
    for row in (0, 1, NX + 2, NX + 3):
        e0[row, :, NV:] = jnp.zeros((NS, NH), f32)
    for x in range(NX):
        after, before = yl_ref[x * half : (x + 1) * half, :], yh_ref[x * half : (x + 1) * half, :]
        e0[x + 2, :, :128] = c0_ref[pl.ds(x, NS, stride=NX), :]
        e0[x + 2, :, 128:NV] = c1_ref[pl.ds(x, NS, stride=NX), :]
        e0[x + 2, :half, NV:] = jnp.where(low_h, after, before)
        e0[x + 2, half:, NV:] = pltpu.roll(jnp.where(low_h, before, after), 64, 1)
    ke[8 : 8 + NX, :NV] = k_ref[...]
    ke[8 : 8 + NX, NV:] = jnp.where(lanes(NX) < 64, yl_ref[NX * half :, :], yh_ref[NX * half :, :])
    ke[0:8, :NV] = xh_ref[2 * NS :, :]
    ke[0:8, NV:] = jnp.zeros((8, NH), f32)
    ke[8 + NX :, :NV] = xl_ref[2 * NS :, :]
    ke[8 + NX :, NV:] = jnp.zeros((8, NH), f32)
    rate = jnp.broadcast_to(rate_ref[...], (NS, 128))

    def step(src, row, k_row, tiles):
        t = [src[row, :, i * 128 : (i + 1) * 128] for i in range(3)]
        up = [pltpu.roll(v, 96, 1) for v in t]
        down = [pltpu.roll(v, 32, 1) for v in t]
        out = []
        for i in range(tiles):
            cut = slice(i * 128, (i + 1) * 128)
            total = src[row - 1, :, cut] + src[row + 1, :, cut]
            total = total + jnp.where(above, up[i], up[(i + 1) % 3]) + jnp.where(below, down[i], down[(i + 2) % 3])
            total = total + jnp.where(not_first, pltpu.roll(t[i], 1, 1), 0.0)
            total = total + jnp.where(not_last, pltpu.roll(t[i], 127, 1), 0.0)
            lap = total - 6.0 * t[i]
            out.append(t[i] + (rate * k_row[:, cut]) * lap)
        return out

    def first_step(x, carry):
        for i, v in enumerate(step(e0, x + 1, ke[pl.ds(x + 7, 1), :], 3)):
            e1[x, :, i * 128 : (i + 1) * 128] = v
        return carry

    lax.fori_loop(0, NX + 2, first_step, 0, unroll=True)

    def second_step(x, carry):
        done = step(e1, x + 1, ke[pl.ds(x + 8, 1), :], 2)
        left[pl.ds(x, NS, stride=NX), :], right[pl.ds(x, NS, stride=NX), :] = done
        return carry

    lax.fori_loop(0, NX, second_step, 0, unroll=True)


def advance(c2d, k, rate, faces):
    small = (k, rate, *faces)
    return pl.pallas_call(
        advance_kernel,
        grid=(1,),
        out_shape=[jax.ShapeDtypeStruct((NS * NX, 128), f32)] * 2,
        in_specs=halves(c2d) + [whole_block(v.shape) for v in small],
        out_specs=[whole_block((NS * NX, 128))] * 2,
        scratch_shapes=[
            pltpu.VMEM((NX + 4, NS, NV + NH), f32),
            pltpu.VMEM((NX + 2, NS, NV + NH), f32),
            pltpu.VMEM((NX + 16, NV + NH), f32),
        ],
        compiler_params=pltpu.CompilerParams(vmem_limit_bytes=16 * 2**20),
        cost_estimate=pl.CostEstimate(flops=10000000000, bytes_accessed=4 * 2**20, transcendentals=0),
        name="advance_twice",
    )(c2d, c2d, *small)


def reduce_kernel(a0_ref, a1_ref, k_ref, rate_ref, kxl_ref, kxh_ref, kyl_ref, kyh_ref, cl_ref, ch_ref, fs_ref, fx_ref,
                  adv_ref, planes_ref, left, right):
    left[...], right[...] = a0_ref[...], a1_ref[...]
    rate = jnp.broadcast_to(rate_ref[...], (NS, 128))
    first_y, last_y = lanes(NS) < NZ, lanes(NS) >= 128 - NZ
    for x, at, kx_ref in ((0, 0, kxh_ref), (NX - 1, NS, kxl_ref)):
        cut = pl.ds(x, NS, stride=NX)
        for ref, own, corner_ref, ky_ref, turn, mask in (
            (left, slice(0, 128), ch_ref, kyh_ref, 32, first_y),
            (right, slice(128, 256), cl_ref, kyl_ref, 96, last_y),
        ):
            paths = kx_ref[0:1, own] + pltpu.roll(jnp.broadcast_to(ky_ref[x : x + 1, :], (8, 128)), turn, 1)[0:1, :]
            term = (rate * k_ref[x : x + 1, own]) * (rate * paths) * pltpu.roll(corner_ref[at : at + NS, :], turn, 1)
            ref[cut, :] = ref[cut, :] + jnp.where(mask, term, 0.0)
    adv_ref[:, :128] = left[...]
    adv_ref[:, 128:] = right[...]
    for z in range(NZ):
        planes_ref[(2 * z + 1) * NX : (2 * z + 2) * NX, :] = fx_ref[...]

    lane_q = lanes(NQ)
    low_q, even_q = lane_q < 64, (lane_q & 32) == 0
    fs_hi, fs_lo = split_2(fs_ref[...])
    weights = jnp.concatenate([fs_hi, fs_hi, fs_lo], axis=1)

    def four_rows(group, carry):
        rows = []
        for g in range(4):
            cut = pl.ds(group * 4 + g, NS, stride=NX)
            hi, lo = split_2(jnp.concatenate([left[cut, :], right[cut, :]], axis=1))
            stacked = jnp.concatenate([hi, lo, hi], axis=0)
            rows.append(jnp.dot(weights, stacked, preferred_element_type=f32))
        swapped = []
        for t in range(2):
            v = [r[:, t * 128 : (t + 1) * 128] for r in rows]
            a = [jnp.where(low_q, v[g], pltpu.roll(v[g + 2], 64, 1)) for g in range(2)]
            b = [jnp.where(low_q, pltpu.roll(v[g], 64, 1), v[g + 2]) for g in range(2)]
            for p, r in (a, b):
                swapped.append(jnp.where(even_q, p, pltpu.roll(r, 32, 1)))
                swapped.append(jnp.where(even_q, pltpu.roll(p, 96, 1), r))
        turned = jnp.concatenate(swapped, axis=0).T
        for g in range(4):
            planes_ref[pl.ds(group * 4 + g, NZ, stride=2 * NX), :] = turned[g * NZ : (g + 1) * NZ, :]
        return carry

    lax.fori_loop(0, NX // 4, four_rows, 0, unroll=True)


def reduce_species(sides, k, rate, faces, corner, fs, factor_x):
    xl, xh, yl, yh = faces
    tail_x, tail_y = pl.BlockSpec((8, NV), lambda i: (2 * NS // 8, 0)), pl.BlockSpec((NX, 128), lambda i: (NS // 2, 0))
    shapes = [(NS * NX, NV), (NZ * 2 * NX, 128)]
    return pl.pallas_call(
        reduce_kernel,
        grid=(1,),
        out_shape=[jax.ShapeDtypeStruct(s, f32) for s in shapes],
        in_specs=[whole_block(v.shape) for v in (*sides, k, rate)]
        + [tail_x, tail_x, tail_y, tail_y]
        + [whole_block(v.shape) for v in (*corner, fs, factor_x)],
        out_specs=[whole_block(s) for s in shapes],
        scratch_shapes=[pltpu.VMEM((NS * NX, 128), f32)] * 2,
        compiler_params=pltpu.CompilerParams(vmem_limit_bytes=12 * 2**20),
        name="reduce_species",
    )(*sides, k, rate, xl, xh, yl, yh, *corner, fs, factor_x)


def shift_to(v, dx, dy):
    axis, step = ("tx", dx) if dx else ("ty", dy)
    count = lax.axis_size(axis)
    return lax.ppermute(v, axis, [(i, i + step) for i in range(count) if 0 <= i + step < count])


def body(species, cell_factor, species_rate, factor_x, factor_y, factor_species):
    nspec, cells_x, merged = species.shape
    cells_y = factor_y.shape[0]
    depth = merged // cells_y
    n_tx, n_ty = lax.axis_size("tx"), lax.axis_size("ty")
    ranks_q = factor_species.shape[1]
    c2d = species.reshape(nspec * cells_x, merged)
    faces = pack(c2d, cell_factor)
    xl, xh, yl, yh = (shift_to(v, dx, dy) for v, (dx, dy) in zip(faces, [(-1, 0), (1, 0), (0, -1), (0, 1)]))
    lo, hi = corners(xl, xh)
    corner = shift_to(lo, 0, -1), shift_to(hi, 0, 1)
    faces, rate = (xl, xh, yl, yh), species_rate[:, None]
    sides = advance(c2d, cell_factor, rate, faces)
    advanced, planes = reduce_species(sides, cell_factor, rate, faces, corner, factor_species.T, factor_x)
    planes = planes.reshape(depth, 2 * cells_x, cells_y * ranks_q)
    planes = lax.all_to_all(planes, "tx", 0, 0, tiled=True)
    first = lax.dot_general(
        planes[:, :cells_x], planes[:, cells_x:], (((0, 1), (0, 1)), ((), ())), precision=exact_mode
    )
    first = first.reshape(cells_y, ranks_q, -1).transpose(1, 0, 2)
    sent = jnp.concatenate([first, jnp.broadcast_to(factor_y[None], (n_ty,) + factor_y.shape)], axis=1)
    came = lax.all_to_all(sent, "ty", 0, 0, tiled=True)
    first = came[:, :cells_y].reshape(n_ty * cells_y, -1)
    whole_y = came[:, cells_y:].reshape(n_ty * cells_y, -1)
    plane = lax.dot_general(first, whole_y, (((0,), (0,)), ((), ())), precision=exact_mode)
    rank_a, rank_b = plane.shape
    plane = plane.reshape(n_tx, rank_a // n_tx, n_ty, rank_b // n_ty).transpose(0, 2, 1, 3)
    plane = plane.reshape(n_tx * n_ty, 1, -1)
    core = lax.all_to_all(plane, ("tx", "ty"), 0, 0, tiled=True)
    core = core.reshape(depth, ranks_q, rank_a // n_tx, rank_b // n_ty).transpose(2, 1, 3, 0)
    return advanced.reshape(species.shape), core.reshape(rank_a // n_tx, ranks_q, -1)


def solution(mesh):
    in_specs = (P(None, "tx", "ty"), P("tx", "ty"), P(), P("tx", None), P("ty", None), P())
    out_specs = (P(None, "tx", "ty"), P("tx", None, "ty"))
    return jax.shard_map(body, mesh=mesh, in_specs=in_specs, out_specs=out_specs, check_vma=False)
```
